32 devices in a mesh: tm: 4 (over y, core), lat: 4 (over z), lon: 2 (over x).
Axes of the slice: x: 2, y: 2, z: 4, core: 2. Of those that a mesh axis runs over, the one named last changes fastest.
Arguments:
- residuals: bfloat16 [256, 180, 256], P('tm', 'lat', 'lon'), may hold values from -10 to 10
- diffusivity: float32 [180, 256], P('lat', 'lon'), may hold values from 0.03 to 0.24
Outputs:
- projected: bfloat16 [256, 180, 256], P('tm', 'lat', 'lon')
The draws below stay inside these ranges and needn't reach their ends.
All inputs are finite; a program needn't handle non-finite values.
Results may differ from the reference program's by a relative error of at most 0.019.
Values may be sent and summed in bfloat16 or wider, within the bound.
No kernel may reach another device: no remote copies, remote signals or barrier semaphores. Data moves between devices by JAX's collectives and lax.ppermute only.
A program may use at most 64 MiB of HBM per device.

```python
import math
import jax
import jax.numpy as jnp
from jax import lax

SNAP_DEV = 64
RANK = 32
PASSES = 4
POWER = 3
SNAPS = 256
NLAT = 180
NLON = 256
LEVELS = 2
N_TM = 4


def draw_residuals(key, part):
    keys = jax.random.split(jax.random.fold_in(key, 11), 4)
    count = 2 * RANK
    amplitude = jnp.exp(jax.random.uniform(keys[0], (count,), jnp.float32, 0.0, math.log(2.0)))
    coefs = jax.random.normal(keys[1], (SNAPS, count), jnp.float32)
    patterns = jax.random.normal(keys[2], (count, NLAT, NLON), jnp.float32)
    noise = jax.random.normal(keys[3], (SNAPS, NLAT * NLON), jnp.float32)
    rise = math.log(4.0)
    rows = (jnp.arange(NLAT).astype(jnp.float32) + 0.5) / NLAT
    centers = (jnp.arange(count).astype(jnp.float32) + 0.5) / count
    envelope = jnp.exp(-((rows[None, :] - centers[:, None]) / 0.15) ** 2)
    gain = jnp.exp(rise * rows)
    shaped = patterns * (envelope * gain[None, :])[:, :, None]
    signal = jnp.dot(coefs * amplitude[None, :] / math.sqrt(0.3 * count), shaped.reshape(count, NLAT * NLON), precision=lax.Precision.HIGHEST)
    values = jnp.clip(signal + 0.18 * noise, -10.0, 10.0)
    return values.reshape(SNAPS, NLAT, NLON).astype(jnp.bfloat16)


def block_scale(own_key, shape, shards, smallest, high):
    level, own = 1.0, jax.random.fold_in(own_key, 6)
    for axis_at, shards_of in shards:
        draws = jnp.exp(jax.random.uniform(jax.random.fold_in(own, axis_at), (shards_of,), jnp.float32, smallest / len(shards), high / len(shards)))
        level = level * jnp.repeat(draws, shape[axis_at] // shards_of).reshape([-1 if axis == axis_at else 1 for axis in range(len(shape))])
    return level


def setup_inputs(seed: int = 0) -> dict:
    key_of = jax.random.split(jax.random.key(seed), 3)
    return {
        "residuals": draw_residuals(jax.random.fold_in(key_of[2], 71), 0),
        "diffusivity": jnp.clip(jnp.exp(math.log(0.24) - 2.0794415 * jax.random.uniform(key_of[1], (NLAT, NLON), jnp.float32) ** block_scale(key_of[1], (NLAT, NLON), ((0, 4), (1, 2)), -0.2, 0.2)), 0.03, 0.24),
    }


exact_precision = lax.Precision.HIGHEST

def extend_grid(values):
    wrapped = jnp.concatenate([values[:, :, -1:], values, values[:, :, :1]], axis=2)
    border = jnp.zeros((wrapped.shape[0], 1, wrapped.shape[2]), jnp.float32)
    return jnp.concatenate([border, wrapped, border], axis=1)

def stencil(current, coeffs):
    center = current[:, 1:-1, 1:-1]
    middle = coeffs[:, 1:-1, 1:-1]
    northward = 0.5 * (middle + coeffs[:, :-2, 1:-1]) * (current[:, :-2, 1:-1] - center)
    southward = 0.5 * (middle + coeffs[:, 2:, 1:-1]) * (current[:, 2:, 1:-1] - center)
    westward = 0.5 * (middle + coeffs[:, 1:-1, :-2]) * (current[:, 1:-1, :-2] - center)
    eastward = 0.5 * (middle + coeffs[:, 1:-1, 2:]) * (current[:, 1:-1, 2:] - center)
    return center + (northward + southward + westward + eastward)

def orthonormal(block):
    inner = jnp.dot(block.T, block, precision=exact_precision)
    lower = jnp.linalg.cholesky(inner)
    return jax.scipy.linalg.solve_triangular(lower, block.T, lower=True).T

def top_space(gram):
    basis = orthonormal(gram[:, :RANK])
    for step_index in range(POWER):
        basis = orthonormal(jnp.dot(gram, basis, precision=exact_precision))
    return basis

def mode_block(stacked, gram):
    basis = top_space(gram).astype(jnp.bfloat16)
    modes = jnp.dot(basis.T.astype(jnp.float32), stacked.astype(jnp.float32), preferred_element_type=jnp.float32).astype(jnp.bfloat16)
    return (basis, modes)

def reference(residuals, diffusivity):
    coeffs = extend_grid(diffusivity[None])
    rows = jnp.arange(NLAT).astype(jnp.float32)
    latitude = (rows + 0.5) * math.pi / NLAT - math.pi / 2
    scale = jnp.sqrt(jnp.cos(latitude))

    def one_group(block):
        current = block.astype(jnp.float32)
        for pass_index in range(PASSES):
            current = stencil(extend_grid(current), coeffs)
        weighted = (current * scale[None, :, None]).astype(jnp.bfloat16).reshape(SNAP_DEV, NLAT * NLON)
        gram = jnp.dot(weighted.astype(jnp.float32), weighted.T.astype(jnp.float32), preferred_element_type=jnp.float32)
        basis, modes = mode_block(weighted, gram)
        return (weighted, modes)
    weighted_all, blocks = lax.map(one_group, residuals.reshape(N_TM, SNAP_DEV, NLAT, NLON))

    def merge_pair(stacked):
        gram = jnp.dot(stacked.astype(jnp.float32), stacked.T.astype(jnp.float32), preferred_element_type=jnp.float32)
        basis, modes = mode_block(stacked, gram)
        return (basis, modes, gram)
    for level_index in range(LEVELS):
        count = blocks.shape[0] // 2
        basis_all, blocks, gram_all = lax.map(merge_pair, blocks.reshape(count, 2 * RANK, NLAT * NLON))
    final = blocks[0]
    basis_f = basis_all[0].astype(jnp.float32)
    curvature = jnp.dot(basis_f.T, jnp.dot(gram_all[0], basis_f, precision=exact_precision), precision=exact_precision)
    factor = jnp.linalg.cholesky(curvature)

    def project(weighted):
        coef = jnp.dot(weighted.astype(jnp.float32), final.T.astype(jnp.float32), preferred_element_type=jnp.float32)
        solved = jax.scipy.linalg.cho_solve((factor, True), coef.T).T.astype(jnp.bfloat16)
        return jnp.dot(solved.astype(jnp.float32), final.astype(jnp.float32), preferred_element_type=jnp.float32).astype(jnp.bfloat16)
    projected = lax.map(project, weighted_all)
    return projected.reshape(SNAPS, NLAT, NLON)
```

```python
import functools
import math

import jax
import jax.numpy as jnp
from jax import lax
from jax.experimental import pallas as pl
from jax.experimental.pallas import tpu as pltpu
from jax.sharding import PartitionSpec as P

RANK = 32
PASSES = 4
LANES = 128
MSG = 80
SEG = 32
exact = lax.Precision.HIGHEST
VMEM = pltpu.VMEM


def whole():
    return pl.BlockSpec(memory_space=VMEM)


def kernel_call(body, outs, scratch=(), flops=1 << 20):
    return pl.pallas_call(
        body,
        out_shape=outs,
        out_specs=jax.tree.map(lambda _: whole(), outs),
        scratch_shapes=list(scratch),
        compiler_params=pltpu.CompilerParams(vmem_limit_bytes=48 << 20),
        cost_estimate=pl.CostEstimate(flops=flops, bytes_accessed=1 << 20, transcendentals=0),
    )


def lane_iota(shape):
    return lax.broadcasted_iota(jnp.int32, shape, len(shape) - 1)


def roll(x, shift):
    return pltpu.roll(x, shift % LANES, x.ndim - 1)


def pack_body(x_ref, d_ref, m_ref, north_ref, south_ref):
    rows = x_ref.shape[0]
    snaps = x_ref.shape[1]
    lane = lane_iota((1, LANES))
    pad = jnp.zeros((MSG - snaps - 2, LANES), jnp.float32)

    def plane(i):
        d = d_ref[i : i + 1, :]
        high = d.astype(jnp.bfloat16).astype(jnp.float32)
        return jnp.concatenate([x_ref[i].astype(jnp.float32), high, d - high, pad], axis=0)

    for p in range(m_ref.shape[0]):
        acc = jnp.zeros((MSG, LANES), jnp.float32)
        for q in range(min(16, rows - 16 * p)):
            v = plane(16 * p + q)
            acc = jnp.where((lane >= 8 * q) & (lane < 8 * q + 4), roll(v, 8 * q), acc)
            acc = jnp.where((lane >= 8 * q + 4) & (lane < 8 * q + 8), roll(v, 8 * q + 8), acc)
        m_ref[p] = acc.astype(jnp.bfloat16)
    for r in range(PASSES):
        north_ref[r] = plane(r).astype(jnp.bfloat16)
        south_ref[r] = plane(rows - PASSES + r).astype(jnp.bfloat16)


def halo_exchange(x, d):
    rows = x.shape[0]
    planes = -(-rows // 16)
    shape = lambda n: jax.ShapeDtypeStruct((n, MSG, LANES), jnp.bfloat16)
    packed, north, south = kernel_call(pack_body, (shape(planes), shape(PASSES), shape(PASSES)))(x, d)
    lons, lats = lax.axis_size("lon"), lax.axis_size("lat")
    forward = [(i, (i + 1) % lons) for i in range(lons)]
    side = lax.ppermute(packed, "lon", forward)
    if lons > 2:
        from_east = lax.ppermute(packed, "lon", [(b, a) for a, b in forward])
        side = jnp.where(lane_iota((1, 1, LANES)) % 8 < 4, from_east, side)
    up = [(i, i + 1) for i in range(lats - 1)]
    down = [(b, a) for a, b in up]
    last = (rows - PASSES) // 16
    from_north = lax.ppermute(jnp.concatenate([south, side[last : last + 1]]), "lat", up)
    from_south = lax.ppermute(jnp.concatenate([north, side[:1]]), "lat", down)
    return side, from_north, from_south


def smooth_body(x_ref, d_ref, side_ref, north_ref, south_ref, y_ref, u, s, dm, ds, ce, cs, se, ss, scale):
    rows, snaps, _ = x_ref.shape
    lats = lax.axis_size("lat")
    lat = lax.axis_index("lat")
    ext = rows + 2 * PASSES
    lane = lane_iota((1, LANES))
    groups = snaps // 8
    last_q = (rows - PASSES) % 16

    def halo(e, lo, hi):
        if e < PASSES:
            ref, p, q = north_ref, PASSES, last_q + e
        elif e < rows + PASSES:
            ref, p, q = side_ref, (e - PASSES) // 16, (e - PASSES) % 16
        else:
            ref, p, q = south_ref, PASSES, e - rows - PASSES
        return ref[p, lo:hi, :], q

    def in_strip(shape_lane, own_high, own_low, edge):
        at = shape_lane % SEG
        return jnp.where(at < 12, own_high, jnp.where(at < 20, edge, own_low))

    u[PASSES : PASSES + rows] = x_ref[...].astype(jnp.float32)
    dm[PASSES : PASSES + rows, :] = d_ref[...]
    dm[ext:, :] = jnp.zeros((dm.shape[0] - ext, LANES), jnp.float32)
    ds[ext:, :] = jnp.zeros((dm.shape[0] - ext, LANES), jnp.float32)
    for r in range(PASSES):
        for e, ref in ((r, north_ref), (rows + PASSES + r, south_ref)):
            u[e] = ref[r, :snaps, :].astype(jnp.float32)
            term = ref[r, snaps : snaps + 16, :].astype(jnp.float32)
            dm[e : e + 1, :] = term[0:1] + term[1:2]
    for e in range(ext):
        piece, q = halo(e, snaps, snaps + 16)
        piece = piece.astype(jnp.float32)
        ds[e : e + 1, :] = roll(piece[0:1] + piece[1:2], 12 - 8 * q)
        piece, q = halo(e, 0, snaps)
        piece = piece.astype(jnp.float32)
        for h in range(groups // 4):
            acc = None
            for g in range(4):
                at = 8 * (4 * h + g)
                own = u[e, at : at + 8, :]
                part = in_strip(
                    lane,
                    roll(own, 12 + SEG * g),
                    roll(own, 20 + SEG * g),
                    roll(piece[at : at + 8], 12 + SEG * g - 8 * q),
                )
                acc = part if g == 0 else jnp.where(lane >= SEG * g, part, acc)
            s[e, 8 * h : 8 * h + 8, :] = acc
    d = dm[...]
    first = in_strip(lane, roll(d, 12), roll(d, 20), ds[...])
    strip = first
    for g in range(1, 4):
        strip = jnp.where(lane >= SEG * g, roll(first, SEG * g), strip)
    ce[...] = 0.5 * (d + roll(d, -1))
    se[...] = 0.5 * (strip + roll(strip, -1))
    ds[...] = strip
    cs[0 : ext - 1, :] = 0.5 * (dm[0 : ext - 1, :] + dm[1:ext, :])
    ss[0 : ext - 1, :] = 0.5 * (ds[0 : ext - 1, :] + ds[1:ext, :])
    row = lax.broadcasted_iota(jnp.int32, scale.shape, 0) + lat * rows
    angle = (row.astype(jnp.float32) + 0.5) * math.pi / (rows * lats) - math.pi / 2
    scale[...] = jnp.sqrt(jnp.maximum(jnp.cos(angle), 0.0))

    def updated(field, e, carry, south_c, east_c):
        current, above = carry
        below = field[e + 1]
        south = south_c[pl.ds(e, 1), :] * (below - current)
        east = east_c[pl.ds(e, 1), :] * (roll(current, -1) - current)
        fresh = current + ((south - above) + (east - roll(east, 1)))
        return fresh, (below, south)

    def entry(field, e, south_c):
        current = field[e]
        return current, south_c[e : e + 1, :] * (current - field[e - 1])

    for step in range(PASSES):
        final = step == PASSES - 1

        def body(e, carry):
            main, edge = carry
            fresh, main = updated(u, e, main, cs, ce)
            fresh_edge, edge = updated(s, e, edge, ss, se)
            if not final:
                u[e] = fresh
                s[e] = fresh_edge
            else:
                parts = []
                for g in range(groups):
                    strip_part = fresh_edge[8 * (g // 4) : 8 * (g // 4) + 8]
                    base = SEG * (g % 4)
                    low = roll(strip_part, -(20 + base))
                    high = roll(strip_part, 116 - base)
                    body_part = fresh[8 * g : 8 * g + 8]
                    merged = jnp.where(lane < PASSES, low, jnp.where(lane >= LANES - PASSES, high, body_part))
                    parts.append(merged)
                i = e - PASSES
                merged = jnp.concatenate(parts, axis=0) * scale[pl.ds(i, 1), :]
                y_ref[i] = merged.astype(jnp.bfloat16)
            return main, edge

        start = step + 1
        lax.fori_loop(start, ext - 1 - step, body, (entry(u, start, cs), entry(s, start, ss)))
        if not final:

            @pl.when(lat == 0)
            def _():
                u[PASSES - 1] = jnp.zeros(u.shape[1:], jnp.float32)
                s[PASSES - 1] = jnp.zeros(s.shape[1:], jnp.float32)

            @pl.when(lat == lats - 1)
            def _():
                u[rows + PASSES] = jnp.zeros(u.shape[1:], jnp.float32)
                s[rows + PASSES] = jnp.zeros(s.shape[1:], jnp.float32)


def smooth(x, d, side, north, south):
    rows, snaps, width = x.shape
    ext = rows + 2 * PASSES
    tall = -(-ext // 8) * 8
    field = lambda n: VMEM((ext, n, width), jnp.float32)
    plane = VMEM((tall, width), jnp.float32)
    return kernel_call(
        smooth_body,
        jax.ShapeDtypeStruct((rows, snaps, width), jnp.bfloat16),
        [field(snaps), field(snaps // 4)] + [plane] * 7,
    )(x, d, side, north, south)


def mm(a, b):
    return jnp.dot(a, b, precision=exact, preferred_element_type=jnp.float32)


def mmt(a, b):
    return lax.dot_general(
        a, b, (((1,), (1,)), ((), ())), precision=exact, preferred_element_type=jnp.float32
    )


def whitened(s, zt, block=16):
    n = s.shape[0]
    a = jnp.concatenate([s, zt], axis=1)
    w = a.shape[1]
    row = lax.broadcasted_iota(jnp.int32, (n, w), 0)
    diagonal = row == lane_iota((n, w))
    floor = jnp.broadcast_to(
        jnp.sum(jnp.where(diagonal, a, 0.0), axis=1, keepdims=True) * 1e-7 + 1e-37, (n, w)
    )
    for k0 in range(0, n, block):
        cols = [jnp.broadcast_to(a[:, k0 + j : k0 + j + 1], (n, w)) for j in range(block)]
        for p in range(block):
            k = k0 + p
            if k == n - 1:
                continue
            inverse = 1.0 / jnp.maximum(cols[p][k : k + 1, :], floor[k : k + 1, :])
            below = jnp.where(row > k, cols[p], 0.0)
            for j in range(p + 1, block):
                cols[j] = cols[j] - below * (cols[j][k : k + 1, :] * inverse)
            a = a - below * (a[k : k + 1, :] * inverse)
    pivots = jnp.sum(jnp.where(diagonal, a, 0.0), axis=1, keepdims=True)
    return a[:, n:] * lax.rsqrt(jnp.maximum(pivots, floor[:, :1]))


def power_basis(h, upper_first):
    n = h.shape[0]
    eye = lax.broadcasted_iota(jnp.int32, (n, n), 0) == lane_iota((n, n))
    top = jnp.max(jnp.max(jnp.where(eye, h, 0.0), axis=1, keepdims=True), axis=0, keepdims=True)
    unit = 1.0 / jnp.maximum(top, 1e-30)
    h2 = mm(h, h) * (unit * unit)
    start = h2[:RANK]
    if upper_first is not None:
        start = jnp.where(upper_first, h2[RANK:], start)
    return mm(whitened(mmt(start, start), start), h2)


def top_rows(h, upper_first=None):
    zt = power_basis(h, upper_first)
    return whitened(mmt(zt, zt), zt)


def dot_t(a, b):
    return lax.dot_general(a, b, (((1,), (1,)), ((), ())), preferred_element_type=jnp.float32)


def pair_gram_body(own_ref, other_ref, o_ref):
    acc = None
    for i in range(own_ref.shape[0]):
        own = own_ref[i]
        part = dot_t(own, jnp.concatenate([own, other_ref[i]], axis=0))
        acc = part if acc is None else acc + part
    for j in range(o_ref.shape[0]):
        o_ref[j] = acc


def odd(level):
    return (lax.axis_index("tm") >> level & 1) == 1


def leaf_body(g_ref, gp_ref, own_ref, other_ref, modes_ref, h_ref, c_ref):
    n = own_ref.shape[1]
    own_rows, other_rows = g_ref[...], gp_ref[...]
    gram = jnp.concatenate([own_rows, pltpu.roll(other_rows, n, 1)], axis=0)
    q_own = top_rows(own_rows[:, :n])
    q_other = top_rows(other_rows[:, :n])
    zero = jnp.zeros_like(q_own)
    basis = jnp.concatenate(
        [jnp.concatenate([q_own, zero], axis=1), jnp.concatenate([zero, q_other], axis=1)], axis=0
    )
    merged = mmt(mm(basis, gram), basis)
    w = mm(top_rows(merged, odd(0)), basis).astype(jnp.bfloat16)
    wf = w.astype(jnp.float32)
    gw = mmt(gram, wf)
    c_ref[...] = gw[:n]
    h_ref[...] = mm(wf, gw)
    for i in range(own_ref.shape[0]):
        stacked = jnp.concatenate([own_ref[i], other_ref[i]], axis=0)
        modes_ref[i] = jnp.dot(w, stacked, preferred_element_type=jnp.float32).astype(jnp.bfloat16)


def cross_body(other_ref, y_ref, own_ref, o_ref):
    acc = None
    for i in range(y_ref.shape[0]):
        other = other_ref[i]
        part = dot_t(other, jnp.concatenate([y_ref[i], own_ref[i], other], axis=0))
        acc = part if acc is None else acc + part
    for j in range(o_ref.shape[0]):
        o_ref[j] = acc


def merged_gram(p_ref, h_ref, c_ref, n):
    total = p_ref[0]
    for j in range(1, p_ref.shape[0]):
        total = total + p_ref[j]
    mixed = total[:, n : n + RANK]
    gram = jnp.concatenate(
        [
            jnp.concatenate([h_ref[...], mixed.T], axis=1),
            jnp.concatenate([mixed, total[:, n + RANK :]], axis=1),
        ],
        axis=0,
    )
    coef = jnp.concatenate([c_ref[...], total[:, :n].T], axis=1)
    return gram, coef


def merge_body(level, p_ref, h_ref, c_ref, own_ref, other_ref, modes_ref, hn_ref, cn_ref):
    gram, coef = merged_gram(p_ref, h_ref, c_ref, c_ref.shape[0])
    w = top_rows(gram, odd(level)).astype(jnp.bfloat16)
    wf = w.astype(jnp.float32)
    cn_ref[...] = mmt(coef, wf)
    hn_ref[...] = mmt(mm(wf, gram), wf)
    for i in range(own_ref.shape[0]):
        stacked = jnp.concatenate([own_ref[i], other_ref[i]], axis=0)
        modes_ref[i] = jnp.dot(w, stacked, preferred_element_type=jnp.float32).astype(jnp.bfloat16)


def project_body(level, p_ref, h_ref, c_ref, own_ref, other_ref, o_ref):
    gram, coef = merged_gram(p_ref, h_ref, c_ref, c_ref.shape[0])
    zt = power_basis(gram, odd(level))
    r = whitened(mmt(mm(zt, gram), zt), zt)
    weights = mm(mmt(coef, r), r).astype(jnp.bfloat16)
    for i in range(own_ref.shape[0]):
        stacked = jnp.concatenate([own_ref[i], other_ref[i]], axis=0)
        o_ref[i] = jnp.dot(weights, stacked, preferred_element_type=jnp.float32).astype(jnp.bfloat16)


def exchanged(block, level):
    count = lax.axis_size("tm")
    return lax.ppermute(block, "tm", [(i, i ^ 1 << level) for i in range(count)])


def gathered(parts):
    return lax.all_to_all(parts, ("lat", "lon"), 0, 0, tiled=True)


def shards(residuals, diffusivity):
    snaps, rows, width = residuals.shape
    tiles = lax.axis_size("lat") * lax.axis_size("lon")
    levels = lax.axis_size("tm").bit_length() - 1
    f32 = lambda *shape: jax.ShapeDtypeStruct(shape, jnp.float32)
    b16 = lambda *shape: jax.ShapeDtypeStruct(shape, jnp.bfloat16)
    x = jnp.transpose(residuals, (1, 0, 2))
    y = smooth(x, diffusivity, *halo_exchange(x, diffusivity))
    other = exchanged(y, 0)
    parts = gathered(kernel_call(pair_gram_body, f32(tiles, snaps, 2 * snaps))(y, other))
    gram = jnp.sum(parts, axis=0)
    small = (f32(RANK, RANK), f32(snaps, RANK))
    modes, h, c = kernel_call(leaf_body, (b16(rows, RANK, width),) + small)(
        gram, exchanged(gram, 0), y, other
    )
    for level in range(1, levels):
        other = exchanged(modes, level)
        parts = gathered(kernel_call(cross_body, f32(tiles, RANK, snaps + 2 * RANK))(other, y, modes))
        if level < levels - 1:
            modes, h, c = kernel_call(
                functools.partial(merge_body, level), (b16(rows, RANK, width),) + small
            )(parts, h, c, modes, other)
    out = kernel_call(functools.partial(project_body, levels - 1), b16(rows, snaps, width))(
        parts, h, c, modes, other
    )
    return jnp.transpose(out, (1, 0, 2))


def solution(mesh):
    return jax.shard_map(
        shards,
        mesh=mesh,
        in_specs=(P("tm", "lat", "lon"), P("lat", "lon")),
        out_specs=P("tm", "lat", "lon"),
        check_vma=False,
    )
```

```python
import functools
import math

import jax
import jax.numpy as jnp
from jax import lax
from jax.experimental import pallas as pl
from jax.experimental.pallas import tpu as pltpu
from jax.sharding import PartitionSpec as P

RANK = 32
PASSES = 4
LANES = 128
MSG = 80
BATCH = 60
SEG = 32
exact = lax.Precision.HIGHEST
VMEM = pltpu.VMEM


def whole():
    return pl.BlockSpec(memory_space=VMEM)


def kernel_call(body, outs, scratch=(), flops=1 << 20):
    return pl.pallas_call(
        body,
        out_shape=outs,
        out_specs=jax.tree.map(lambda _: whole(), outs),
        scratch_shapes=list(scratch),
        compiler_params=pltpu.CompilerParams(vmem_limit_bytes=48 << 20),
        cost_estimate=pl.CostEstimate(flops=flops, bytes_accessed=1 << 20, transcendentals=0),
    )


def lane_iota(shape):
    return lax.broadcasted_iota(jnp.int32, shape, len(shape) - 1)


def roll(x, shift):
    return pltpu.roll(x, shift % LANES, x.ndim - 1)


def pack_body(x_ref, d_ref, m_ref, north_ref, south_ref):
    rows = x_ref.shape[0]
    snaps = x_ref.shape[1]
    lane = lane_iota((1, LANES))
    pad = jnp.zeros((MSG - snaps - 2, LANES), jnp.float32)

    def plane(i):
        d = d_ref[i : i + 1, :]
        high = d.astype(jnp.bfloat16).astype(jnp.float32)
        return jnp.concatenate([x_ref[i].astype(jnp.float32), high, d - high, pad], axis=0)

    for p in range(m_ref.shape[0]):
        acc = jnp.zeros((MSG, LANES), jnp.float32)
        for q in range(min(16, rows - 16 * p)):
            v = plane(16 * p + q)
            acc = jnp.where((lane >= 8 * q) & (lane < 8 * q + 4), roll(v, 8 * q), acc)
            acc = jnp.where((lane >= 8 * q + 4) & (lane < 8 * q + 8), roll(v, 8 * q + 8), acc)
        m_ref[p] = acc.astype(jnp.bfloat16)
    for r in range(PASSES):
        north_ref[r] = plane(r).astype(jnp.bfloat16)
        south_ref[r] = plane(rows - PASSES + r).astype(jnp.bfloat16)


def halo_exchange(x, d):
    rows = x.shape[0]
    planes = -(-rows // 16)
    shape = lambda n: jax.ShapeDtypeStruct((n, MSG, LANES), jnp.bfloat16)
    packed, north, south = kernel_call(pack_body, (shape(planes), shape(PASSES), shape(PASSES)))(x, d)
    lons, lats = lax.axis_size("lon"), lax.axis_size("lat")
    forward = [(i, (i + 1) % lons) for i in range(lons)]
    side = lax.ppermute(packed, "lon", forward)
    if lons > 2:
        from_east = lax.ppermute(packed, "lon", [(b, a) for a, b in forward])
        side = jnp.where(lane_iota((1, 1, LANES)) % 8 < 4, from_east, side)
    up = [(i, i + 1) for i in range(lats - 1)]
    down = [(b, a) for a, b in up]
    last = (rows - PASSES) // 16
    from_north = lax.ppermute(jnp.concatenate([south, side[last : last + 1]]), "lat", up)
    from_south = lax.ppermute(jnp.concatenate([north, side[:1]]), "lat", down)
    return side, from_north, from_south


def smooth_body(x_ref, d_ref, side_ref, north_ref, south_ref, y_ref, u, s, dm, ds, ce, cs, se, ss, scale):
    rows, snaps, _ = x_ref.shape
    lats = lax.axis_size("lat")
    lat = lax.axis_index("lat")
    ext = rows + 2 * PASSES
    lane = lane_iota((1, LANES))
    groups = snaps // 8
    last_q = (rows - PASSES) % 16

    def halo(e, lo, hi):
        if e < PASSES:
            ref, p, q = north_ref, PASSES, last_q + e
        elif e < rows + PASSES:
            ref, p, q = side_ref, (e - PASSES) // 16, (e - PASSES) % 16
        else:
            ref, p, q = south_ref, PASSES, e - rows - PASSES
        return ref[p, lo:hi, :], q

    def in_strip(shape_lane, own_high, own_low, edge):
        at = shape_lane % SEG
        return jnp.where(at < 12, own_high, jnp.where(at < 20, edge, own_low))

    u[PASSES : PASSES + rows] = x_ref[...].astype(jnp.float32)
    dm[PASSES : PASSES + rows, :] = d_ref[...]
    dm[ext:, :] = jnp.zeros((dm.shape[0] - ext, LANES), jnp.float32)
    ds[ext:, :] = jnp.zeros((dm.shape[0] - ext, LANES), jnp.float32)
    for r in range(PASSES):
        for e, ref in ((r, north_ref), (rows + PASSES + r, south_ref)):
            u[e] = ref[r, :snaps, :].astype(jnp.float32)
            term = ref[r, snaps : snaps + 16, :].astype(jnp.float32)
            dm[e : e + 1, :] = term[0:1] + term[1:2]
    for e in range(ext):
        piece, q = halo(e, snaps, snaps + 16)
        piece = piece.astype(jnp.float32)
        ds[e : e + 1, :] = roll(piece[0:1] + piece[1:2], 12 - 8 * q)
        piece, q = halo(e, 0, snaps)
        piece = piece.astype(jnp.float32)
        for h in range(groups // 4):
            acc = None
            for g in range(4):
                at = 8 * (4 * h + g)
                own = u[e, at : at + 8, :]
                part = in_strip(
                    lane,
                    roll(own, 12 + SEG * g),
                    roll(own, 20 + SEG * g),
                    roll(piece[at : at + 8], 12 + SEG * g - 8 * q),
                )
                acc = part if g == 0 else jnp.where(lane >= SEG * g, part, acc)
            s[e, 8 * h : 8 * h + 8, :] = acc
    d = dm[...]
    first = in_strip(lane, roll(d, 12), roll(d, 20), ds[...])
    strip = first
    for g in range(1, 4):
        strip = jnp.where(lane >= SEG * g, roll(first, SEG * g), strip)
    ce[...] = 0.5 * (d + roll(d, -1))
    se[...] = 0.5 * (strip + roll(strip, -1))
    ds[...] = strip
    cs[0 : ext - 1, :] = 0.5 * (dm[0 : ext - 1, :] + dm[1:ext, :])
    ss[0 : ext - 1, :] = 0.5 * (ds[0 : ext - 1, :] + ds[1:ext, :])
    row = lax.broadcasted_iota(jnp.int32, scale.shape, 0) + lat * rows
    angle = (row.astype(jnp.float32) + 0.5) * math.pi / (rows * lats) - math.pi / 2
    scale[...] = jnp.sqrt(jnp.maximum(jnp.cos(angle), 0.0))

    def updated(field, e, carry, south_c, east_c):
        current, above = carry
        below = field[e + 1]
        south = south_c[pl.ds(e, 1), :] * (below - current)
        east_face = east_c[pl.ds(e, 1), :]
        east = east_face * (roll(current, -1) - current)
        west = roll(east_face, 1) * (current - roll(current, 1))
        fresh = current + ((south - above) + (east - west))
        return fresh, (below, south)

    def entry(field, e, south_c):
        current = field[e]
        return current, south_c[e : e + 1, :] * (current - field[e - 1])

    for step in range(PASSES):
        final = step == PASSES - 1

        def one(e, carry):
            main, edge = carry
            fresh, main = updated(u, e, main, cs, ce)
            fresh_edge, edge = updated(s, e, edge, ss, se)
            if not final:
                u[e] = fresh
                s[e] = fresh_edge
            else:
                parts = []
                for g in range(groups):
                    strip_part = fresh_edge[8 * (g // 4) : 8 * (g // 4) + 8]
                    base = SEG * (g % 4)
                    low = roll(strip_part, -(20 + base))
                    high = roll(strip_part, 116 - base)
                    body_part = fresh[8 * g : 8 * g + 8]
                    merged = jnp.where(lane < PASSES, low, jnp.where(lane >= LANES - PASSES, high, body_part))
                    parts.append(merged)
                i = e - PASSES
                merged = jnp.concatenate(parts, axis=0) * scale[pl.ds(i, 1), :]
                y_ref[i] = merged.astype(jnp.bfloat16)
            return main, edge

        start, stop = (PASSES, ext - PASSES) if final else (1, ext - 1)
        batch = max(b for b in range(1, BATCH + 1) if (stop - start) % b == 0)

        def body(t, carry):
            for r in range(batch):
                carry = one(start + t * batch + r, carry)
            return carry

        lax.fori_loop(0, (stop - start) // batch, body, (entry(u, start, cs), entry(s, start, ss)))
        if not final:

            @pl.when(lat == 0)
            def _():
                u[PASSES - 1] = jnp.zeros(u.shape[1:], jnp.float32)
                s[PASSES - 1] = jnp.zeros(s.shape[1:], jnp.float32)

            @pl.when(lat == lats - 1)
            def _():
                u[rows + PASSES] = jnp.zeros(u.shape[1:], jnp.float32)
                s[rows + PASSES] = jnp.zeros(s.shape[1:], jnp.float32)


def smooth(x, d, side, north, south):
    rows, snaps, width = x.shape
    ext = rows + 2 * PASSES
    tall = -(-ext // 8) * 8
    field = lambda n: VMEM((ext, n, width), jnp.float32)
    plane = VMEM((tall, width), jnp.float32)
    return kernel_call(
        smooth_body,
        jax.ShapeDtypeStruct((rows, snaps, width), jnp.bfloat16),
        [field(snaps), field(snaps // 4)] + [plane] * 7,
    )(x, d, side, north, south)


def mm(a, b):
    return jnp.dot(a, b, precision=exact, preferred_element_type=jnp.float32)


def mmt(a, b):
    return lax.dot_general(
        a, b, (((1,), (1,)), ((), ())), precision=exact, preferred_element_type=jnp.float32
    )


def whitened(s, zt, block=16):
    n = s.shape[0]
    a = jnp.concatenate([s, zt], axis=1)
    w = a.shape[1]
    row = lax.broadcasted_iota(jnp.int32, (n, w), 0)
    diagonal = row == lane_iota((n, w))
    floor = jnp.broadcast_to(
        jnp.sum(jnp.where(diagonal, a, 0.0), axis=1, keepdims=True) * 1e-7 + 1e-37, (n, w)
    )
    for k0 in range(0, n, block):
        cols = [jnp.broadcast_to(a[:, k0 + j : k0 + j + 1], (n, w)) for j in range(block)]
        for p in range(block):
            k = k0 + p
            if k == n - 1:
                continue
            inverse = 1.0 / jnp.maximum(cols[p][k : k + 1, :], floor[k : k + 1, :])
            below = jnp.where(row > k, cols[p], 0.0)
            for j in range(p + 1, block):
                cols[j] = cols[j] - below * (cols[j][k : k + 1, :] * inverse)
            a = a - below * (a[k : k + 1, :] * inverse)
    pivots = jnp.sum(jnp.where(diagonal, a, 0.0), axis=1, keepdims=True)
    return a[:, n:] * lax.rsqrt(jnp.maximum(pivots, floor[:, :1]))


def power_basis(h, upper_first):
    n = h.shape[0]
    eye = lax.broadcasted_iota(jnp.int32, (n, n), 0) == lane_iota((n, n))
    top = jnp.max(jnp.max(jnp.where(eye, h, 0.0), axis=1, keepdims=True), axis=0, keepdims=True)
    unit = 1.0 / jnp.maximum(top, 1e-30)
    h2 = mm(h, h) * (unit * unit)
    start = h2[:RANK]
    if upper_first is not None:
        start = jnp.where(upper_first, h2[RANK:], start)
    return mm(whitened(mmt(start, start), start), h2)


def top_rows(h, upper_first=None):
    zt = power_basis(h, upper_first)
    return whitened(mmt(zt, zt), zt)


def dot_t(a, b):
    return lax.dot_general(a, b, (((1,), (1,)), ((), ())), preferred_element_type=jnp.float32)


def pair_gram_body(own_ref, other_ref, o_ref):
    acc = None
    for i in range(own_ref.shape[0]):
        own = own_ref[i]
        part = dot_t(own, jnp.concatenate([own, other_ref[i]], axis=0))
        acc = part if acc is None else acc + part
    for j in range(o_ref.shape[0]):
        o_ref[j] = acc


def odd(level):
    return (lax.axis_index("tm") >> level & 1) == 1


def leaf_body(g_ref, gp_ref, own_ref, other_ref, modes_ref, h_ref, c_ref):
    n = own_ref.shape[1]
    own_rows, other_rows = g_ref[...], gp_ref[...]
    gram = jnp.concatenate([own_rows, pltpu.roll(other_rows, n, 1)], axis=0)
    q_own = top_rows(own_rows[:, :n])
    q_other = top_rows(other_rows[:, :n])
    zero = jnp.zeros_like(q_own)
    basis = jnp.concatenate(
        [jnp.concatenate([q_own, zero], axis=1), jnp.concatenate([zero, q_other], axis=1)], axis=0
    )
    merged = mmt(mm(basis, gram), basis)
    w = mm(top_rows(merged, odd(0)), basis).astype(jnp.bfloat16)
    wf = w.astype(jnp.float32)
    gw = mmt(gram, wf)
    c_ref[...] = gw[:n]
    h_ref[...] = mm(wf, gw)
    for i in range(own_ref.shape[0]):
        stacked = jnp.concatenate([own_ref[i], other_ref[i]], axis=0)
        modes_ref[i] = jnp.dot(w, stacked, preferred_element_type=jnp.float32).astype(jnp.bfloat16)


def cross_body(other_ref, y_ref, own_ref, o_ref):
    acc = None
    for i in range(y_ref.shape[0]):
        other = other_ref[i]
        part = dot_t(other, jnp.concatenate([y_ref[i], own_ref[i], other], axis=0))
        acc = part if acc is None else acc + part
    for j in range(o_ref.shape[0]):
        o_ref[j] = acc


def merged_gram(p_ref, h_ref, c_ref, n):
    total = p_ref[0]
    for j in range(1, p_ref.shape[0]):
        total = total + p_ref[j]
    mixed = total[:, n : n + RANK]
    gram = jnp.concatenate(
        [
            jnp.concatenate([h_ref[...], mixed.T], axis=1),
            jnp.concatenate([mixed, total[:, n + RANK :]], axis=1),
        ],
        axis=0,
    )
    coef = jnp.concatenate([c_ref[...], total[:, :n].T], axis=1)
    return gram, coef


def merge_body(level, p_ref, h_ref, c_ref, own_ref, other_ref, modes_ref, hn_ref, cn_ref):
    gram, coef = merged_gram(p_ref, h_ref, c_ref, c_ref.shape[0])
    w = top_rows(gram, odd(level)).astype(jnp.bfloat16)
    wf = w.astype(jnp.float32)
    cn_ref[...] = mmt(coef, wf)
    hn_ref[...] = mmt(mm(wf, gram), wf)
    for i in range(own_ref.shape[0]):
        stacked = jnp.concatenate([own_ref[i], other_ref[i]], axis=0)
        modes_ref[i] = jnp.dot(w, stacked, preferred_element_type=jnp.float32).astype(jnp.bfloat16)


def project_body(level, p_ref, h_ref, c_ref, own_ref, other_ref, o_ref):
    gram, coef = merged_gram(p_ref, h_ref, c_ref, c_ref.shape[0])
    zt = power_basis(gram, odd(level))
    r = whitened(mmt(mm(zt, gram), zt), zt)
    weights = mm(mmt(coef, r), r).astype(jnp.bfloat16)
    for i in range(own_ref.shape[0]):
        stacked = jnp.concatenate([own_ref[i], other_ref[i]], axis=0)
        o_ref[i] = jnp.dot(weights, stacked, preferred_element_type=jnp.float32).astype(jnp.bfloat16)


def exchanged(block, level):
    count = lax.axis_size("tm")
    return lax.ppermute(block, "tm", [(i, i ^ 1 << level) for i in range(count)])


def gathered(parts):
    return lax.all_to_all(parts, ("lat", "lon"), 0, 0, tiled=True)


def shards(residuals, diffusivity):
    snaps, rows, width = residuals.shape
    tiles = lax.axis_size("lat") * lax.axis_size("lon")
    levels = lax.axis_size("tm").bit_length() - 1
    f32 = lambda *shape: jax.ShapeDtypeStruct(shape, jnp.float32)
    b16 = lambda *shape: jax.ShapeDtypeStruct(shape, jnp.bfloat16)
    x = jnp.transpose(residuals, (1, 0, 2))
    y = smooth(x, diffusivity, *halo_exchange(x, diffusivity))
    other = exchanged(y, 0)
    parts = gathered(kernel_call(pair_gram_body, f32(tiles, snaps, 2 * snaps))(y, other))
    gram = jnp.sum(parts, axis=0)
    small = (f32(RANK, RANK), f32(snaps, RANK))
    modes, h, c = kernel_call(leaf_body, (b16(rows, RANK, width),) + small)(
        gram, exchanged(gram, 0), y, other
    )
    for level in range(1, levels):
        other = exchanged(modes, level)
        parts = gathered(kernel_call(cross_body, f32(tiles, RANK, snaps + 2 * RANK))(other, y, modes))
        if level < levels - 1:
            modes, h, c = kernel_call(
                functools.partial(merge_body, level), (b16(rows, RANK, width),) + small
            )(parts, h, c, modes, other)
    out = kernel_call(functools.partial(project_body, levels - 1), b16(rows, snaps, width))(
        parts, h, c, modes, other
    )
    return jnp.transpose(out, (1, 0, 2))


def solution(mesh):
    return jax.shard_map(
        shards,
        mesh=mesh,
        in_specs=(P("tm", "lat", "lon"), P("lat", "lon")),
        out_specs=P("tm", "lat", "lon"),
        check_vma=False,
    )
```

```python
import functools
import math

import jax
import jax.numpy as jnp
from jax import lax
from jax.experimental import pallas as pl
from jax.experimental.pallas import tpu as pltpu
from jax.sharding import PartitionSpec as P

RANK = 32
PASSES = 4
LANES = 128
exact = lax.Precision.HIGHEST
VMEM = pltpu.VMEM


def whole():
    return pl.BlockSpec(memory_space=VMEM)


def kernel_call(body, outs, scratch=(), flops=1 << 20):
    return pl.pallas_call(
        body,
        out_shape=outs,
        out_specs=jax.tree.map(lambda _: whole(), outs),
        scratch_shapes=list(scratch),
        compiler_params=pltpu.CompilerParams(vmem_limit_bytes=48 << 20),
        cost_estimate=pl.CostEstimate(flops=flops, bytes_accessed=1 << 20, transcendentals=0),
    )


def lane_iota(shape):
    return lax.broadcasted_iota(jnp.int32, shape, len(shape) - 1)


def roll(x, shift):
    return pltpu.roll(x, shift % LANES, x.ndim - 1)


def eye(n, dtype=jnp.bfloat16):
    row = lax.broadcasted_iota(jnp.int32, (n, n), 0)
    return (row == lax.broadcasted_iota(jnp.int32, (n, n), 1)).astype(dtype)


def dot_t(a, b):
    return lax.dot_general(a, b, (((1,), (1,)), ((), ())), preferred_element_type=jnp.float32)


def split2(v):
    high = v.astype(jnp.bfloat16)
    return high, (v - high.astype(jnp.float32)).astype(jnp.bfloat16)


def even_lat():
    return lax.axis_index("lat") % 2 == 0


def pack_body(x_ref, d_ref, m_ref, a_ref, b_ref):
    rows, snaps, width = x_ref.shape
    half = -(-rows // 2)
    row = lax.broadcasted_iota(jnp.int32, (16, width), 0)
    lane = lane_iota((16, width))
    column = jnp.where(row % 8 < PASSES, row % 8, width - 8 + row % 8)
    pick = [((lane == column) & (row // 8 == k)).astype(jnp.bfloat16) for k in range(2)]

    def tile(t):
        return jnp.concatenate([x_ref[t], x_ref[t + rows - half]], axis=0)

    for t in range(0, half, 2):
        out = dot_t(pick[0], tile(t))
        if t + 1 < half:
            out = out + dot_t(pick[1], tile(t + 1))
        m_ref[8 * t : 8 * t + 16, :] = out.astype(jnp.bfloat16)
    d = d_ref[...]
    high, low = split2(jnp.concatenate([d, jnp.zeros((width - rows, width), jnp.float32)], axis=0))
    end = m_ref.shape[0]
    m_ref[end - 16 :, :] = (dot_t(pick[0], high) + dot_t(pick[1], low)).astype(jnp.bfloat16)

    even = even_lat()
    pad = jnp.zeros((8, width), jnp.float32)
    edge = lambda lo: [v.astype(jnp.float32) for v in split2(d[lo : lo + PASSES])]
    first, final = edge(0), edge(rows - PASSES)
    for ref, south in ((a_ref, even), (b_ref, jnp.logical_not(even))):
        start = jnp.where(south, rows - PASSES, 0)
        for r in range(PASSES):
            ref[r * snaps : (r + 1) * snaps, :] = x_ref[start + r]
        term = [jnp.where(south, f, g) for f, g in zip(final, first)]
        ref[PASSES * snaps :, :] = jnp.concatenate(term + [pad], axis=0).astype(jnp.bfloat16)


def halo_exchange(x, d):
    rows, snaps, width = x.shape
    half = -(-rows // 2)
    tiles = 16 * (-(-half // 2))
    shape = lambda n: jax.ShapeDtypeStruct((n, width), jnp.bfloat16)
    edge = PASSES * snaps + 16
    packed, a, b = kernel_call(pack_body, (shape(tiles + 16), shape(edge), shape(edge)))(x, d)
    lons, lats = lax.axis_size("lon"), lax.axis_size("lat")
    forward = [(i, (i + 1) % lons) for i in range(lons)]
    side = lax.ppermute(packed, "lon", forward)
    if lons > 2:
        from_east = lax.ppermute(packed, "lon", [(j, i) for i, j in forward])
        side = jnp.where(lax.broadcasted_iota(jnp.int32, side.shape, 0) % 8 < PASSES, from_east, side)
    even = even_lat()
    corner = 8 * PASSES
    north_corner, south_corner = side[:corner], side[8 * (half - PASSES) : 8 * half]

    def swapped(base, south, start):
        message = jnp.concatenate([base, jnp.where(south, south_corner, north_corner), side[tiles:]])
        pairs = [(i, i + 1) for i in range(start, lats - 1, 2)]
        return lax.ppermute(message, "lat", pairs + [(j, i) for i, j in pairs])

    return side, swapped(a, even, 0), swapped(b, jnp.logical_not(even), 1)


PADDED = 160


def smooth_body(x_ref, d_ref, side_ref, a_ref, b_ref, y_ref, u0, u1, ce, cs, dn, dt):
    rows, snaps, width = x_ref.shape
    half = -(-rows // 2)
    shift = rows - half
    count = half + 2 * PASSES
    lats, lat = lax.axis_size("lat"), lax.axis_index("lat")
    even = even_lat()
    lane = lane_iota((1, LANES))
    left = lane < snaps
    own = 16
    east = own + width
    unit = eye(width)
    edge = PASSES * snaps
    corner = edge + 16
    tail = corner + 8 * PASSES
    tiles = side_ref.shape[0] - 16

    def picked(lo, hi):
        a, b = a_ref[lo:hi, :], b_ref[lo:hi, :]
        return jnp.where(even, b, a), jnp.where(even, a, b)

    north, south = picked(0, edge)
    north_corner, south_corner = (v.astype(jnp.float32) for v in picked(corner, tail))
    north_d, south_d = (v.astype(jnp.float32) for v in picked(edge, corner))
    north_t, south_t = (v.astype(jnp.float32) for v in picked(tail, tail + 16))
    side = lambda t: side_ref[16 * (t // 2) : 16 * (t // 2) + 16, :].astype(jnp.float32)[
        8 * (t % 2) : 8 * (t % 2) + 8
    ]

    for k in range(count):
        t = k - PASSES
        first = north[k * snaps : (k + 1) * snaps] if t < 0 else x_ref[t]
        r = t + shift
        second = x_ref[r] if r < rows else south[(r - rows) * snaps : (r - rows + 1) * snaps]
        u0[k, own:east, :] = dot_t(unit, jnp.concatenate([first, second], axis=0))
        if t < 0:
            halo = roll(jnp.where(left, side(r), north_corner[8 * k : 8 * k + 8]), snaps)
        elif t >= half:
            j = t - half
            halo = roll(jnp.where(left, south_corner[8 * j : 8 * j + 8], side(t - shift)), snaps)
        else:
            halo = side(t)
        u0[k, own - 8 : own, :] = halo
        u0[k, east : east + 8, :] = halo

    dn[...] = jnp.zeros(dn.shape, jnp.float32)
    dn[PASSES : PASSES + rows, :] = d_ref[...]
    dn[0:PASSES, :] = north_d[0:PASSES] + north_d[PASSES : 2 * PASSES]
    dn[PASSES + rows : 2 * PASSES + rows, :] = south_d[0:PASSES] + south_d[PASSES : 2 * PASSES]
    dt[own:east, :] = dn[...].T
    side_d = side_ref[tiles:, :].astype(jnp.float32)
    fold = lambda v: v[0:8] + v[8:16]
    halo = jnp.where(
        lane < PASSES,
        roll(fold(north_t), PASSES - rows),
        jnp.where(lane < PASSES + rows, roll(fold(side_d), PASSES), roll(fold(south_t), PASSES + rows)),
    )
    dt[0 : own - 8, :] = jnp.zeros((own - 8, LANES), jnp.float32)
    dt[own - 8 : own, :] = halo
    dt[east : east + 8, :] = halo
    dt[east + 8 :, :] = jnp.zeros((PADDED - east - 8, LANES), jnp.float32)
    low, high = own - 8, east + 8
    here = dt[low:high, :]
    faces = jnp.concatenate([here + dt[low + 1 : high + 1, :], here + roll(here, -1)], axis=0) * 0.5
    f_high, f_low = split2(faces)
    terms = jnp.where(lane < LANES // 2, f_high.astype(jnp.float32), roll(f_low.astype(jnp.float32), LANES // 2))
    terms = terms.astype(jnp.bfloat16)
    source = lax.broadcasted_iota(jnp.int32, (LANES, LANES), 0) % (LANES // 2)
    offset = jnp.where(lane_iota((LANES, LANES)) < snaps, 0, shift)
    relative = source - offset
    for k in range(count):
        spread = jnp.dot(
            terms, (relative == k).astype(jnp.bfloat16), preferred_element_type=jnp.float32
        )
        ce[k, low:high, :] = spread[: high - low]
        cs[k, low:high, :] = spread[high - low :]

    buffers = (u0, u1)
    for step in range(PASSES):
        src, dst = buffers[step % 2], buffers[(step + 1) % 2]
        final = step == PASSES - 1
        start, stop = step + 1, count - 1 - step
        for r in range(own if final else low, east if final else high, 8):
            here = slice(r, r + 8)
            current = src[start, here, :]
            above = cs[start - 1, here, :] * (current - src[start - 1, here, :])
            for k in range(start, stop):
                below = src[k + 1, here, :]
                southward = cs[k, here, :] * (below - current)
                eastward = ce[k, here, :] * (src[k, r + 1 : r + 9, :] - current)
                westward = ce[k, r - 1 : r + 7, :] * (current - src[k, r - 1 : r + 7, :])
                dst[k, here, :] = current + ((southward - above) + (eastward - westward))
                current, above = below, southward
        if not final:

            @pl.when(lat == 0)
            def _():
                dst[PASSES - 1, low:high, :] = jnp.where(left, 0.0, dst[PASSES - 1, low:high, :])

            @pl.when(lat == lats - 1)
            def _():
                dst[PASSES + half, low:high, :] = jnp.where(left, dst[PASSES + half, low:high, :], 0.0)

    tall = -(-half // 8) * 8
    row = lax.broadcasted_iota(jnp.int32, (tall, LANES), 0) + jnp.where(lane_iota((tall, LANES)) < snaps, 0, shift)
    angle = ((row + lat * rows).astype(jnp.float32) + 0.5) * math.pi / (rows * lats) - math.pi / 2
    scale = jnp.sqrt(jnp.maximum(jnp.cos(angle), 0.0))
    for t in range(half):
        weighted = (dst[t + PASSES, own:east, :] * scale[t : t + 1]).astype(jnp.bfloat16)
        both = dot_t(unit, weighted).astype(jnp.bfloat16)
        y_ref[t] = both[:snaps]
        y_ref[t + shift] = both[snaps:]


def smooth(x, d, side, a, b):
    rows, snaps, width = x.shape
    count = -(-rows // 2) + 2 * PASSES
    field = VMEM((count, PADDED, LANES), jnp.float32)
    return kernel_call(
        smooth_body,
        jax.ShapeDtypeStruct((rows, snaps, width), jnp.bfloat16),
        [field] * 4 + [VMEM((width, LANES), jnp.float32), VMEM((PADDED, LANES), jnp.float32)],
    )(x, d, side, a, b)


def mm(a, b):
    return jnp.dot(a, b, precision=exact, preferred_element_type=jnp.float32)


def mmt(a, b):
    return lax.dot_general(
        a, b, (((1,), (1,)), ((), ())), precision=exact, preferred_element_type=jnp.float32
    )


def whitened(s, zt, block=16):
    n = s.shape[0]
    a = jnp.concatenate([s, zt], axis=1)
    w = a.shape[1]
    row = lax.broadcasted_iota(jnp.int32, (n, w), 0)
    diagonal = row == lane_iota((n, w))
    floor = jnp.broadcast_to(
        jnp.sum(jnp.where(diagonal, a, 0.0), axis=1, keepdims=True) * 1e-7 + 1e-37, (n, w)
    )
    for k0 in range(0, n, block):
        cols = [jnp.broadcast_to(a[:, k0 + j : k0 + j + 1], (n, w)) for j in range(block)]
        for p in range(block):
            k = k0 + p
            if k == n - 1:
                continue
            inverse = 1.0 / jnp.maximum(cols[p][k : k + 1, :], floor[k : k + 1, :])
            below = jnp.where(row > k, cols[p], 0.0)
            for j in range(p + 1, block):
                cols[j] = cols[j] - below * (cols[j][k : k + 1, :] * inverse)
            a = a - below * (a[k : k + 1, :] * inverse)
    pivots = jnp.sum(jnp.where(diagonal, a, 0.0), axis=1, keepdims=True)
    return a[:, n:] * lax.rsqrt(jnp.maximum(pivots, floor[:, :1]))


def power_basis(h, upper_first):
    n = h.shape[0]
    eye = lax.broadcasted_iota(jnp.int32, (n, n), 0) == lane_iota((n, n))
    top = jnp.max(jnp.max(jnp.where(eye, h, 0.0), axis=1, keepdims=True), axis=0, keepdims=True)
    unit = 1.0 / jnp.maximum(top, 1e-30)
    h2 = mm(h, h) * (unit * unit)
    start = h2[:RANK]
    if upper_first is not None:
        start = jnp.where(upper_first, h2[RANK:], start)
    return mm(whitened(mmt(start, start), start), h2)


def top_rows(h, upper_first=None):
    zt = power_basis(h, upper_first)
    return whitened(mmt(zt, zt), zt)


def pair_gram_body(own_ref, other_ref, o_ref):
    acc = None
    for i in range(own_ref.shape[0]):
        own = own_ref[i]
        part = dot_t(own, jnp.concatenate([own, other_ref[i]], axis=0))
        acc = part if acc is None else acc + part
    for j in range(o_ref.shape[0]):
        o_ref[j] = acc


def odd(level):
    return (lax.axis_index("tm") >> level & 1) == 1


def leaf_body(g_ref, gp_ref, own_ref, other_ref, modes_ref, h_ref, c_ref):
    n = own_ref.shape[1]
    own_rows, other_rows = g_ref[...], gp_ref[...]
    gram = jnp.concatenate([own_rows, pltpu.roll(other_rows, n, 1)], axis=0)
    q_own = top_rows(own_rows[:, :n])
    q_other = top_rows(other_rows[:, :n])
    zero = jnp.zeros_like(q_own)
    basis = jnp.concatenate(
        [jnp.concatenate([q_own, zero], axis=1), jnp.concatenate([zero, q_other], axis=1)], axis=0
    )
    merged = mmt(mm(basis, gram), basis)
    w = mm(top_rows(merged, odd(0)), basis).astype(jnp.bfloat16)
    wf = w.astype(jnp.float32)
    gw = mmt(gram, wf)
    c_ref[...] = gw[:n]
    h_ref[...] = mm(wf, gw)
    for i in range(own_ref.shape[0]):
        stacked = jnp.concatenate([own_ref[i], other_ref[i]], axis=0)
        modes_ref[i] = jnp.dot(w, stacked, preferred_element_type=jnp.float32).astype(jnp.bfloat16)


def cross_body(other_ref, y_ref, own_ref, o_ref):
    acc = None
    for i in range(y_ref.shape[0]):
        other = other_ref[i]
        part = dot_t(other, jnp.concatenate([y_ref[i], own_ref[i], other], axis=0))
        acc = part if acc is None else acc + part
    for j in range(o_ref.shape[0]):
        o_ref[j] = acc


def merged_gram(p_ref, h_ref, c_ref, n):
    total = p_ref[0]
    for j in range(1, p_ref.shape[0]):
        total = total + p_ref[j]
    mixed = total[:, n : n + RANK]
    gram = jnp.concatenate(
        [
            jnp.concatenate([h_ref[...], mixed.T], axis=1),
            jnp.concatenate([mixed, total[:, n + RANK :]], axis=1),
        ],
        axis=0,
    )
    coef = jnp.concatenate([c_ref[...], total[:, :n].T], axis=1)
    return gram, coef


def merge_body(level, p_ref, h_ref, c_ref, own_ref, other_ref, modes_ref, hn_ref, cn_ref):
    gram, coef = merged_gram(p_ref, h_ref, c_ref, c_ref.shape[0])
    w = top_rows(gram, odd(level)).astype(jnp.bfloat16)
    wf = w.astype(jnp.float32)
    cn_ref[...] = mmt(coef, wf)
    hn_ref[...] = mmt(mm(wf, gram), wf)
    for i in range(own_ref.shape[0]):
        stacked = jnp.concatenate([own_ref[i], other_ref[i]], axis=0)
        modes_ref[i] = jnp.dot(w, stacked, preferred_element_type=jnp.float32).astype(jnp.bfloat16)


def project_body(level, p_ref, h_ref, c_ref, own_ref, other_ref, o_ref):
    gram, coef = merged_gram(p_ref, h_ref, c_ref, c_ref.shape[0])
    zt = power_basis(gram, odd(level))
    r = whitened(mmt(mm(zt, gram), zt), zt)
    weights = mm(mmt(coef, r), r).astype(jnp.bfloat16)
    for i in range(own_ref.shape[0]):
        stacked = jnp.concatenate([own_ref[i], other_ref[i]], axis=0)
        o_ref[i] = jnp.dot(weights, stacked, preferred_element_type=jnp.float32).astype(jnp.bfloat16)


def exchanged(block, level):
    count = lax.axis_size("tm")
    return lax.ppermute(block, "tm", [(i, i ^ 1 << level) for i in range(count)])


def gathered(parts):
    return lax.all_to_all(parts, ("lat", "lon"), 0, 0, tiled=True)


def shards(residuals, diffusivity):
    snaps, rows, width = residuals.shape
    tiles = lax.axis_size("lat") * lax.axis_size("lon")
    levels = lax.axis_size("tm").bit_length() - 1
    f32 = lambda *shape: jax.ShapeDtypeStruct(shape, jnp.float32)
    b16 = lambda *shape: jax.ShapeDtypeStruct(shape, jnp.bfloat16)
    x = jnp.transpose(residuals, (1, 0, 2))
    y = smooth(x, diffusivity, *halo_exchange(x, diffusivity))
    other = exchanged(y, 0)
    parts = gathered(kernel_call(pair_gram_body, f32(tiles, snaps, 2 * snaps))(y, other))
    gram = jnp.sum(parts, axis=0)
    small = (f32(RANK, RANK), f32(snaps, RANK))
    modes, h, c = kernel_call(leaf_body, (b16(rows, RANK, width),) + small)(
        gram, exchanged(gram, 0), y, other
    )
    for level in range(1, levels):
        other = exchanged(modes, level)
        parts = gathered(kernel_call(cross_body, f32(tiles, RANK, snaps + 2 * RANK))(other, y, modes))
        if level < levels - 1:
            modes, h, c = kernel_call(
                functools.partial(merge_body, level), (b16(rows, RANK, width),) + small
            )(parts, h, c, modes, other)
    out = kernel_call(functools.partial(project_body, levels - 1), b16(rows, snaps, width))(
        parts, h, c, modes, other
    )
    return jnp.transpose(out, (1, 0, 2))


def solution(mesh):
    return jax.shard_map(
        shards,
        mesh=mesh,
        in_specs=(P("tm", "lat", "lon"), P("lat", "lon")),
        out_specs=P("tm", "lat", "lon"),
        check_vma=False,
    )
```

```python
import functools
import math

import jax
import jax.numpy as jnp
from jax import lax
from jax.experimental import pallas as pl
from jax.experimental.pallas import tpu as pltpu
from jax.sharding import PartitionSpec as P

RANK = 32
PASSES = 4
LANES = 128
exact = lax.Precision.HIGHEST
VMEM = pltpu.VMEM


def whole():
    return pl.BlockSpec(memory_space=VMEM)


def kernel_call(body, outs, scratch=(), flops=1 << 20):
    return pl.pallas_call(
        body,
        out_shape=outs,
        out_specs=jax.tree.map(lambda _: whole(), outs),
        scratch_shapes=list(scratch),
        compiler_params=pltpu.CompilerParams(vmem_limit_bytes=48 << 20),
        cost_estimate=pl.CostEstimate(flops=flops, bytes_accessed=1 << 20, transcendentals=0),
    )


def lane_iota(shape):
    return lax.broadcasted_iota(jnp.int32, shape, len(shape) - 1)


def roll(x, shift):
    return pltpu.roll(x, shift % LANES, x.ndim - 1)


def eye(n, dtype=jnp.bfloat16):
    row = lax.broadcasted_iota(jnp.int32, (n, n), 0)
    return (row == lax.broadcasted_iota(jnp.int32, (n, n), 1)).astype(dtype)


def dot_t(a, b):
    return lax.dot_general(a, b, (((1,), (1,)), ((), ())), preferred_element_type=jnp.float32)


def split2(v):
    high = v.astype(jnp.bfloat16)
    return high, (v - high.astype(jnp.float32)).astype(jnp.bfloat16)


def even_lat():
    return lax.axis_index("lat") % 2 == 0


def pack_body(x_ref, d_ref, m_ref, a_ref, b_ref):
    rows, snaps, width = x_ref.shape
    half = -(-rows // 2)
    row = lax.broadcasted_iota(jnp.int32, (16, width), 0)
    lane = lane_iota((16, width))
    column = jnp.where(row % 8 < PASSES, row % 8, width - 8 + row % 8)
    pick = [((lane == column) & (row // 8 == k)).astype(jnp.bfloat16) for k in range(2)]

    def tile(t):
        return jnp.concatenate([x_ref[t], x_ref[t + rows - half]], axis=0)

    for t in range(0, half, 2):
        out = dot_t(pick[0], tile(t))
        if t + 1 < half:
            out = out + dot_t(pick[1], tile(t + 1))
        m_ref[8 * t : 8 * t + 16, :] = out.astype(jnp.bfloat16)
    d = d_ref[...]
    high, low = split2(jnp.concatenate([d, jnp.zeros((width - rows, width), jnp.float32)], axis=0))
    end = m_ref.shape[0]
    m_ref[end - 16 :, :] = (dot_t(pick[0], high) + dot_t(pick[1], low)).astype(jnp.bfloat16)

    even = even_lat()
    pad = jnp.zeros((8, width), jnp.float32)
    edge = lambda lo: [v.astype(jnp.float32) for v in split2(d[lo : lo + PASSES])]
    first, final = edge(0), edge(rows - PASSES)
    for ref, south in ((a_ref, even), (b_ref, jnp.logical_not(even))):
        start = jnp.where(south, rows - PASSES, 0)
        for r in range(PASSES):
            ref[r * snaps : (r + 1) * snaps, :] = x_ref[start + r]
        term = [jnp.where(south, f, g) for f, g in zip(final, first)]
        ref[PASSES * snaps :, :] = jnp.concatenate(term + [pad], axis=0).astype(jnp.bfloat16)


def halo_exchange(x, d):
    rows, snaps, width = x.shape
    half = -(-rows // 2)
    tiles = 16 * (-(-half // 2))
    shape = lambda n: jax.ShapeDtypeStruct((n, width), jnp.bfloat16)
    edge = PASSES * snaps + 16
    packed, a, b = kernel_call(pack_body, (shape(tiles + 16), shape(edge), shape(edge)))(x, d)
    lons, lats = lax.axis_size("lon"), lax.axis_size("lat")
    forward = [(i, (i + 1) % lons) for i in range(lons)]
    side = lax.ppermute(packed, "lon", forward)
    if lons > 2:
        from_east = lax.ppermute(packed, "lon", [(j, i) for i, j in forward])
        side = jnp.where(lax.broadcasted_iota(jnp.int32, side.shape, 0) % 8 < PASSES, from_east, side)
    even = even_lat()
    corner = 8 * PASSES
    north_corner, south_corner = side[:corner], side[8 * (half - PASSES) : 8 * half]

    def swapped(base, south, start):
        message = jnp.concatenate([base, jnp.where(south, south_corner, north_corner), side[tiles:]])
        pairs = [(i, i + 1) for i in range(start, lats - 1, 2)]
        return lax.ppermute(message, "lat", pairs + [(j, i) for i, j in pairs])

    return side, swapped(a, even, 0), swapped(b, jnp.logical_not(even), 1)


PADDED = 160


def smooth_body(x_ref, d_ref, side_ref, a_ref, b_ref, y_ref, u0, u1, ce, cs, dn, dt):
    rows, snaps, width = x_ref.shape
    half = -(-rows // 2)
    shift = rows - half
    count = half + 2 * PASSES
    lats, lat = lax.axis_size("lat"), lax.axis_index("lat")
    even = even_lat()
    lane = lane_iota((1, LANES))
    left = lane < snaps
    own = 16
    east = own + width
    unit = eye(width)
    edge = PASSES * snaps
    corner = edge + 16
    tail = corner + 8 * PASSES
    tiles = side_ref.shape[0] - 16

    def picked(lo, hi):
        a, b = a_ref[lo:hi, :], b_ref[lo:hi, :]
        return jnp.where(even, b, a), jnp.where(even, a, b)

    north, south = picked(0, edge)
    north_corner, south_corner = (v.astype(jnp.float32) for v in picked(corner, tail))
    north_d, south_d = (v.astype(jnp.float32) for v in picked(edge, corner))
    north_t, south_t = (v.astype(jnp.float32) for v in picked(tail, tail + 16))
    side = lambda t: side_ref[16 * (t // 2) : 16 * (t // 2) + 16, :].astype(jnp.float32)[
        8 * (t % 2) : 8 * (t % 2) + 8
    ]

    for k in range(count):
        t = k - PASSES
        first = north[k * snaps : (k + 1) * snaps] if t < 0 else x_ref[t]
        r = t + shift
        second = x_ref[r] if r < rows else south[(r - rows) * snaps : (r - rows + 1) * snaps]
        u0[k, own:east, :] = dot_t(unit, jnp.concatenate([first, second], axis=0))
        if t < 0:
            halo = roll(jnp.where(left, side(r), north_corner[8 * k : 8 * k + 8]), snaps)
        elif t >= half:
            j = t - half
            halo = roll(jnp.where(left, south_corner[8 * j : 8 * j + 8], side(t - shift)), snaps)
        else:
            halo = side(t)
        u0[k, own - 8 : own, :] = halo
        u0[k, east : east + 8, :] = halo

    dn[...] = jnp.zeros(dn.shape, jnp.float32)
    dn[PASSES : PASSES + rows, :] = d_ref[...]
    dn[0:PASSES, :] = north_d[0:PASSES] + north_d[PASSES : 2 * PASSES]
    dn[PASSES + rows : 2 * PASSES + rows, :] = south_d[0:PASSES] + south_d[PASSES : 2 * PASSES]
    dt[own:east, :] = dn[...].T
    side_d = side_ref[tiles:, :].astype(jnp.float32)
    fold = lambda v: v[0:8] + v[8:16]
    halo = jnp.where(
        lane < PASSES,
        roll(fold(north_t), PASSES - rows),
        jnp.where(lane < PASSES + rows, roll(fold(side_d), PASSES), roll(fold(south_t), PASSES + rows)),
    )
    dt[0 : own - 8, :] = jnp.zeros((own - 8, LANES), jnp.float32)
    dt[own - 8 : own, :] = halo
    dt[east : east + 8, :] = halo
    dt[east + 8 :, :] = jnp.zeros((PADDED - east - 8, LANES), jnp.float32)
    low, high = own - 8, east + 8
    here = dt[low:high, :]
    faces = jnp.concatenate([here + dt[low + 1 : high + 1, :], here + roll(here, -1)], axis=0) * 0.5
    f_high, f_low = split2(faces)
    terms = jnp.where(lane < LANES // 2, f_high.astype(jnp.float32), roll(f_low.astype(jnp.float32), LANES // 2))
    terms = terms.astype(jnp.bfloat16)
    source = lax.broadcasted_iota(jnp.int32, (LANES, LANES), 0) % (LANES // 2)
    offset = jnp.where(lane_iota((LANES, LANES)) < snaps, 0, shift)
    relative = source - offset
    for k in range(count):
        spread = jnp.dot(
            terms, (relative == k).astype(jnp.bfloat16), preferred_element_type=jnp.float32
        )
        ce[k, low:high, :] = spread[: high - low]
        cs[k, low:high, :] = spread[high - low :]

    buffers = (u0, u1)
    for step in range(PASSES):
        src, dst = buffers[step % 2], buffers[(step + 1) % 2]
        final = step == PASSES - 1
        start, stop = step + 1, count - 1 - step
        for r in range(own if final else low, east if final else high, 8):
            here = slice(r, r + 8)
            current = src[start, here, :]
            above = cs[start - 1, here, :] * (current - src[start - 1, here, :])
            for k in range(start, stop):
                below = src[k + 1, here, :]
                southward = cs[k, here, :] * (below - current)
                eastward = ce[k, here, :] * (src[k, r + 1 : r + 9, :] - current)
                westward = ce[k, r - 1 : r + 7, :] * (current - src[k, r - 1 : r + 7, :])
                dst[k, here, :] = current + ((southward - above) + (eastward - westward))
                current, above = below, southward
        if not final:

            @pl.when(lat == 0)
            def _():
                dst[PASSES - 1, low:high, :] = jnp.where(left, 0.0, dst[PASSES - 1, low:high, :])

            @pl.when(lat == lats - 1)
            def _():
                dst[PASSES + half, low:high, :] = jnp.where(left, dst[PASSES + half, low:high, :], 0.0)

    tall = -(-half // 8) * 8
    row = lax.broadcasted_iota(jnp.int32, (tall, LANES), 0) + jnp.where(lane_iota((tall, LANES)) < snaps, 0, shift)
    angle = ((row + lat * rows).astype(jnp.float32) + 0.5) * math.pi / (rows * lats) - math.pi / 2
    scale = jnp.sqrt(jnp.maximum(jnp.cos(angle), 0.0))
    for t in range(half):
        weighted = (dst[t + PASSES, own:east, :] * scale[t : t + 1]).astype(jnp.bfloat16)
        both = dot_t(unit, weighted).astype(jnp.bfloat16)
        y_ref[t] = both[:snaps]
        y_ref[t + shift] = both[snaps:]


def smooth(x, d, side, a, b):
    rows, snaps, width = x.shape
    count = -(-rows // 2) + 2 * PASSES
    field = VMEM((count, PADDED, LANES), jnp.float32)
    return kernel_call(
        smooth_body,
        jax.ShapeDtypeStruct((rows, snaps, width), jnp.bfloat16),
        [field] * 4 + [VMEM((width, LANES), jnp.float32), VMEM((PADDED, LANES), jnp.float32)],
    )(x, d, side, a, b)


def mm(a, b):
    return jnp.dot(a, b, precision=exact, preferred_element_type=jnp.float32)


def mmt(a, b):
    return lax.dot_general(
        a, b, (((1,), (1,)), ((), ())), precision=exact, preferred_element_type=jnp.float32
    )


def whitened(s, zt, block=16):
    n = s.shape[0]
    a = jnp.concatenate([s, zt], axis=1)
    w = a.shape[1]
    diagonal = lax.broadcasted_iota(jnp.int32, (n, w), 0) == lane_iota((n, w))
    least = jnp.sum(jnp.where(diagonal, a, 0.0), axis=1, keepdims=True) * 1e-7 + 1e-37
    floor = jnp.broadcast_to(least, (n, w))
    done = []
    for k0 in range(0, n, block):
        tall = n - k0
        row = lax.broadcasted_iota(jnp.int32, (tall, w), 0)
        cols = [jnp.broadcast_to(a[:, k0 + j : k0 + j + 1], (tall, w)) for j in range(block)]
        for p in range(min(block, tall - 1)):
            inverse = 1.0 / jnp.maximum(cols[p][p : p + 1, :], floor[k0 + p : k0 + p + 1, :])
            below = jnp.where(row > p, cols[p], 0.0)
            for j in range(p + 1, block):
                cols[j] = cols[j] - below * (cols[j][p : p + 1, :] * inverse)
            a = a - below * (a[p : p + 1, :] * inverse)
        done.append(a[:block])
        a = a[block:]
    a = jnp.concatenate(done, axis=0)
    pivots = jnp.sum(jnp.where(diagonal, a, 0.0), axis=1, keepdims=True)
    return a[:, n:] * lax.rsqrt(jnp.maximum(pivots, least))


def power_basis(h, upper_first):
    n = h.shape[0]
    eye = lax.broadcasted_iota(jnp.int32, (n, n), 0) == lane_iota((n, n))
    top = jnp.max(jnp.max(jnp.where(eye, h, 0.0), axis=1, keepdims=True), axis=0, keepdims=True)
    unit = 1.0 / jnp.maximum(top, 1e-30)
    h2 = mm(h, h) * (unit * unit)
    start = h2[:RANK]
    if upper_first is not None:
        start = jnp.where(upper_first, h2[RANK:], start)
    return mm(whitened(mmt(start, start), start), h2)


def top_rows(h, upper_first=None):
    zt = power_basis(h, upper_first)
    return whitened(mmt(zt, zt), zt)


def odd(level):
    return (lax.axis_index("tm") >> level & 1) == 1


def pair_gram_body(own_ref, other_ref, o_ref):
    n = own_ref.shape[1]
    acc = None
    for i in range(own_ref.shape[0]):
        both = jnp.concatenate([own_ref[i], other_ref[i]], axis=0)
        part = dot_t(both, both)
        acc = part if acc is None else acc + part
    cross = jnp.where(odd(0), pltpu.roll(acc[n + n // 2 :], n, 1), acc[: n // 2])[:, n:]
    tall = o_ref.shape[1]
    packed = jnp.concatenate(
        [acc[:tall, :n], jnp.concatenate([acc[tall:n, :n], cross], axis=0)], axis=1
    )
    for j in range(o_ref.shape[0]):
        o_ref[j] = packed


def pair_gram(g, gp, n):
    tall = g.shape[0]
    rest = n - tall
    block = lambda v: jnp.concatenate([v[:, :n], v[:rest, n:]], axis=0)
    mine, theirs = g[rest:, n:], gp[rest:, n:]
    upper = odd(0)
    cross = jnp.concatenate([jnp.where(upper, theirs, mine), jnp.where(upper, mine, theirs)], axis=0)
    flipped = cross.T
    return block(g), block(gp), jnp.where(upper, flipped, cross), jnp.where(upper, cross, flipped)


def put_modes(w, own_ref, other, modes_ref, part_ref):
    rows, half = modes_ref.shape[0], part_ref.shape[0]
    for i in range(rows):
        stacked = jnp.concatenate([own_ref[i], other(i)], axis=0)
        modes_ref[i] = jnp.dot(w, stacked, preferred_element_type=jnp.float32).astype(jnp.bfloat16)
    start = jnp.where(odd(0), rows - half, 0)
    for i in range(half):
        part_ref[i] = modes_ref[start + i]


def halves(rows, here_ref, there_ref):
    half = here_ref.shape[0]
    upper = odd(0)

    def row(i):
        if i < half:
            return jnp.where(upper, there_ref[i], here_ref[i])
        j = i - (rows - half)
        return jnp.where(upper, here_ref[j], there_ref[j])

    return row


def leaf_body(g_ref, gp_ref, own_ref, other_ref, modes_ref, part_ref, h_ref, c_ref):
    n = own_ref.shape[1]
    own, other, cross, flipped = pair_gram(g_ref[...], gp_ref[...], n)
    q_own = top_rows(own)
    q_other = top_rows(other)
    gram = jnp.concatenate(
        [jnp.concatenate([own, cross], axis=1), jnp.concatenate([flipped, other], axis=1)], axis=0
    )
    zero = jnp.zeros_like(q_own)
    basis = jnp.concatenate(
        [jnp.concatenate([q_own, zero], axis=1), jnp.concatenate([zero, q_other], axis=1)], axis=0
    )
    merged = mmt(mm(basis, gram), basis)
    w = mm(top_rows(merged, odd(0)), basis).astype(jnp.bfloat16)
    wf = w.astype(jnp.float32)
    gw = mmt(gram, wf)
    c_ref[...] = gw[:n]
    h_ref[...] = mm(wf, gw)
    put_modes(w, own_ref, lambda i: other_ref[i], modes_ref, part_ref)


def cross_body(here_ref, there_ref, y_ref, own_ref, o_ref):
    acc = None
    rows = y_ref.shape[0]
    other = halves(rows, here_ref, there_ref)
    for i in range(rows):
        theirs = other(i)
        part = dot_t(theirs, jnp.concatenate([y_ref[i], own_ref[i], theirs], axis=0))
        acc = part if acc is None else acc + part
    for j in range(o_ref.shape[0]):
        o_ref[j] = acc


def merged_gram(p_ref, h_ref, c_ref, n):
    total = p_ref[0]
    for j in range(1, p_ref.shape[0]):
        total = total + p_ref[j]
    mixed = total[:, n : n + RANK]
    gram = jnp.concatenate(
        [
            jnp.concatenate([h_ref[...], mixed.T], axis=1),
            jnp.concatenate([mixed, total[:, n + RANK :]], axis=1),
        ],
        axis=0,
    )
    coef = jnp.concatenate([c_ref[...], total[:, :n].T], axis=1)
    return gram, coef


def merge_body(level, p_ref, h_ref, c_ref, own_ref, here_ref, there_ref, modes_ref, part_ref, hn_ref, cn_ref):
    gram, coef = merged_gram(p_ref, h_ref, c_ref, c_ref.shape[0])
    w = top_rows(gram, odd(level)).astype(jnp.bfloat16)
    wf = w.astype(jnp.float32)
    cn_ref[...] = mmt(coef, wf)
    hn_ref[...] = mmt(mm(wf, gram), wf)
    put_modes(w, own_ref, halves(own_ref.shape[0], here_ref, there_ref), modes_ref, part_ref)


def project_body(level, p_ref, h_ref, c_ref, own_ref, here_ref, there_ref, o_ref):
    gram, coef = merged_gram(p_ref, h_ref, c_ref, c_ref.shape[0])
    zt = power_basis(gram, odd(level))
    r = whitened(mmt(mm(zt, gram), zt), zt)
    weights = mm(mmt(coef, r), r).astype(jnp.bfloat16)
    rows = own_ref.shape[0]
    other = halves(rows, here_ref, there_ref)
    for i in range(rows):
        stacked = jnp.concatenate([own_ref[i], other(i)], axis=0)
        o_ref[i] = jnp.dot(weights, stacked, preferred_element_type=jnp.float32).astype(jnp.bfloat16)


def exchanged(block, level):
    count = lax.axis_size("tm")
    return lax.ppermute(block, "tm", [(i, i ^ 1 << level) for i in range(count)])


def gathered(parts):
    return lax.all_to_all(parts, ("lat", "lon"), 0, 0, tiled=True)


def shards(residuals, diffusivity):
    snaps, rows, width = residuals.shape
    tiles = lax.axis_size("lat") * lax.axis_size("lon")
    levels = lax.axis_size("tm").bit_length() - 1
    f32 = lambda *shape: jax.ShapeDtypeStruct(shape, jnp.float32)
    b16 = lambda *shape: jax.ShapeDtypeStruct(shape, jnp.bfloat16)
    x = jnp.transpose(residuals, (1, 0, 2))
    y = smooth(x, diffusivity, *halo_exchange(x, diffusivity))
    other = exchanged(y, 0)
    parts = gathered(kernel_call(pair_gram_body, f32(tiles, snaps * 3 // 4, 2 * snaps))(y, other))
    gram = jnp.sum(parts, axis=0)
    block = (
        b16(rows, RANK, width),
        b16(-(-rows // 2), RANK, width),
        f32(RANK, RANK),
        f32(snaps, RANK),
    )
    modes, part, h, c = kernel_call(leaf_body, block)(gram, exchanged(gram, 0), y, other)
    for level in range(1, levels):
        here = exchanged(part, level)
        there = exchanged(here, 0)
        parts = gathered(kernel_call(cross_body, f32(tiles, RANK, snaps + 2 * RANK))(here, there, y, modes))
        if level < levels - 1:
            modes, part, h, c = kernel_call(functools.partial(merge_body, level), block)(
                parts, h, c, modes, here, there
            )
    out = kernel_call(functools.partial(project_body, levels - 1), b16(rows, snaps, width))(
        parts, h, c, modes, here, there
    )
    return jnp.transpose(out, (1, 0, 2))


def solution(mesh):
    return jax.shard_map(
        shards,
        mesh=mesh,
        in_specs=(P("tm", "lat", "lon"), P("lat", "lon")),
        out_specs=P("tm", "lat", "lon"),
        check_vma=False,
    )
```

```python
import functools
import math

import jax
import jax.numpy as jnp
from jax import lax
from jax.experimental import pallas as pl
from jax.experimental.pallas import tpu as pltpu
from jax.sharding import PartitionSpec as P

RANK = 32
PASSES = 4
LANES = 128
exact = lax.Precision.HIGHEST
VMEM = pltpu.VMEM


def whole():
    return pl.BlockSpec(memory_space=VMEM)


def kernel_call(body, outs, scratch=(), flops=1 << 20):
    return pl.pallas_call(
        body,
        out_shape=outs,
        out_specs=jax.tree.map(lambda _: whole(), outs),
        scratch_shapes=list(scratch),
        compiler_params=pltpu.CompilerParams(vmem_limit_bytes=48 << 20),
        cost_estimate=pl.CostEstimate(flops=flops, bytes_accessed=1 << 20, transcendentals=0),
    )


def lane_iota(shape):
    return lax.broadcasted_iota(jnp.int32, shape, len(shape) - 1)


def roll(x, shift):
    return pltpu.roll(x, shift % LANES, x.ndim - 1)


def eye(n, dtype=jnp.bfloat16):
    row = lax.broadcasted_iota(jnp.int32, (n, n), 0)
    return (row == lax.broadcasted_iota(jnp.int32, (n, n), 1)).astype(dtype)


def dot_t(a, b):
    return lax.dot_general(a, b, (((1,), (1,)), ((), ())), preferred_element_type=jnp.float32)


def split2(v):
    high = v.astype(jnp.bfloat16)
    return high, (v - high.astype(jnp.float32)).astype(jnp.bfloat16)


def odd(level):
    return (lax.axis_index("tm") >> level & 1) == 1


def even_lat():
    return lax.axis_index("lat") % 2 == 0


def pack_body(x_ref, d_ref, m_ref, a_ref, b_ref):
    rows, snaps, width = x_ref.shape
    half = -(-rows // 2)
    row = lax.broadcasted_iota(jnp.int32, (16, width), 0)
    lane = lane_iota((16, width))
    column = jnp.where(row % 8 < PASSES, row % 8, width - 8 + row % 8)
    pick = [((lane == column) & (row // 8 == k)).astype(jnp.bfloat16) for k in range(2)]

    def tile(t):
        return jnp.concatenate([x_ref[t], x_ref[t + rows - half]], axis=0)

    for t in range(0, half, 2):
        out = dot_t(pick[0], tile(t))
        if t + 1 < half:
            out = out + dot_t(pick[1], tile(t + 1))
        m_ref[8 * t : 8 * t + 16, :] = out.astype(jnp.bfloat16)
    d = d_ref[...]
    high, low = split2(jnp.concatenate([d, jnp.zeros((width - rows, width), jnp.float32)], axis=0))
    end = m_ref.shape[0]
    m_ref[end - 16 :, :] = (dot_t(pick[0], high) + dot_t(pick[1], low)).astype(jnp.bfloat16)

    even = even_lat()
    pad = jnp.zeros((8, width), jnp.float32)
    edge = lambda lo: [v.astype(jnp.float32) for v in split2(d[lo : lo + PASSES])]
    first, final = edge(0), edge(rows - PASSES)
    for ref, south in ((a_ref, even), (b_ref, jnp.logical_not(even))):
        start = jnp.where(south, rows - PASSES, 0)
        for r in range(PASSES):
            ref[r * snaps : (r + 1) * snaps, :] = x_ref[start + r]
        term = [jnp.where(south, f, g) for f, g in zip(final, first)]
        ref[PASSES * snaps :, :] = jnp.concatenate(term + [pad], axis=0).astype(jnp.bfloat16)


def halo_exchange(x, d):
    rows, snaps, width = x.shape
    half = -(-rows // 2)
    tiles = 16 * (-(-half // 2))
    shape = lambda n: jax.ShapeDtypeStruct((n, width), jnp.bfloat16)
    edge = PASSES * snaps + 16
    packed, a, b = kernel_call(pack_body, (shape(tiles + 16), shape(edge), shape(edge)))(x, d)
    lons, lats = lax.axis_size("lon"), lax.axis_size("lat")
    forward = [(i, (i + 1) % lons) for i in range(lons)]
    side = lax.ppermute(packed, "lon", forward)
    if lons > 2:
        from_east = lax.ppermute(packed, "lon", [(j, i) for i, j in forward])
        side = jnp.where(lax.broadcasted_iota(jnp.int32, side.shape, 0) % 8 < PASSES, from_east, side)
    even = even_lat()
    corner = 8 * PASSES
    north_corner, south_corner = side[:corner], side[8 * (half - PASSES) : 8 * half]

    def swapped(base, south, start):
        message = jnp.concatenate([base, jnp.where(south, south_corner, north_corner), side[tiles:]])
        pairs = [(i, i + 1) for i in range(start, lats - 1, 2)]
        return lax.ppermute(message, "lat", pairs + [(j, i) for i, j in pairs])

    return side, swapped(a, even, 0), swapped(b, jnp.logical_not(even), 1)


PADDED = 160


def smooth_body(x_ref, d_ref, side_ref, a_ref, b_ref, y_ref, u0, u1, ce, cs, dn, dt):
    rows, snaps, width = x_ref.shape
    half = -(-rows // 2)
    shift = rows - half
    count = half + 2 * PASSES
    lats, lat = lax.axis_size("lat"), lax.axis_index("lat")
    even = even_lat()
    lane = lane_iota((1, LANES))
    left = lane < snaps
    own = 16
    east = own + width
    unit = eye(width)
    edge = PASSES * snaps
    corner = edge + 16
    tail = corner + 8 * PASSES
    tiles = side_ref.shape[0] - 16

    def picked(lo, hi):
        a, b = a_ref[lo:hi, :], b_ref[lo:hi, :]
        return jnp.where(even, b, a), jnp.where(even, a, b)

    north, south = picked(0, edge)
    north_corner, south_corner = (v.astype(jnp.float32) for v in picked(corner, tail))
    north_d, south_d = (v.astype(jnp.float32) for v in picked(edge, corner))
    north_t, south_t = (v.astype(jnp.float32) for v in picked(tail, tail + 16))
    side = lambda t: side_ref[16 * (t // 2) : 16 * (t // 2) + 16, :].astype(jnp.float32)[
        8 * (t % 2) : 8 * (t % 2) + 8
    ]

    for k in range(count):
        t = k - PASSES
        first = north[k * snaps : (k + 1) * snaps] if t < 0 else x_ref[t]
        r = t + shift
        second = x_ref[r] if r < rows else south[(r - rows) * snaps : (r - rows + 1) * snaps]
        u0[k, own:east, :] = dot_t(unit, jnp.concatenate([first, second], axis=0))
        if t < 0:
            halo = roll(jnp.where(left, side(r), north_corner[8 * k : 8 * k + 8]), snaps)
        elif t >= half:
            j = t - half
            halo = roll(jnp.where(left, south_corner[8 * j : 8 * j + 8], side(t - shift)), snaps)
        else:
            halo = side(t)
        u0[k, own - 8 : own, :] = halo
        u0[k, east : east + 8, :] = halo

    dn[...] = jnp.zeros(dn.shape, jnp.float32)
    dn[PASSES : PASSES + rows, :] = d_ref[...]
    dn[0:PASSES, :] = north_d[0:PASSES] + north_d[PASSES : 2 * PASSES]
    dn[PASSES + rows : 2 * PASSES + rows, :] = south_d[0:PASSES] + south_d[PASSES : 2 * PASSES]
    dt[own:east, :] = dn[...].T
    side_d = side_ref[tiles:, :].astype(jnp.float32)
    fold = lambda v: v[0:8] + v[8:16]
    halo = jnp.where(
        lane < PASSES,
        roll(fold(north_t), PASSES - rows),
        jnp.where(lane < PASSES + rows, roll(fold(side_d), PASSES), roll(fold(south_t), PASSES + rows)),
    )
    dt[0 : own - 8, :] = jnp.zeros((own - 8, LANES), jnp.float32)
    dt[own - 8 : own, :] = halo
    dt[east : east + 8, :] = halo
    dt[east + 8 :, :] = jnp.zeros((PADDED - east - 8, LANES), jnp.float32)
    low, high = own - 8, east + 8
    here = dt[low:high, :]
    faces = jnp.concatenate([here + dt[low + 1 : high + 1, :], here + roll(here, -1)], axis=0) * 0.5
    f_high, f_low = split2(faces)
    terms = jnp.where(lane < LANES // 2, f_high.astype(jnp.float32), roll(f_low.astype(jnp.float32), LANES // 2))
    terms = terms.astype(jnp.bfloat16)
    source = lax.broadcasted_iota(jnp.int32, (LANES, LANES), 0) % (LANES // 2)
    offset = jnp.where(lane_iota((LANES, LANES)) < snaps, 0, shift)
    relative = source - offset
    for k in range(count):
        spread = jnp.dot(
            terms, (relative == k).astype(jnp.bfloat16), preferred_element_type=jnp.float32
        )
        ce[k, low:high, :] = spread[: high - low]
        cs[k, low:high, :] = spread[high - low :]

    buffers = (u0, u1)
    for step in range(PASSES):
        src, dst = buffers[step % 2], buffers[(step + 1) % 2]
        final = step == PASSES - 1
        start, stop = step + 1, count - 1 - step
        for r in range(own if final else low, east if final else high, 8):
            here = slice(r, r + 8)
            current = src[start, here, :]
            above = cs[start - 1, here, :] * (current - src[start - 1, here, :])
            for k in range(start, stop):
                below = src[k + 1, here, :]
                southward = cs[k, here, :] * (below - current)
                eastward = ce[k, here, :] * (src[k, r + 1 : r + 9, :] - current)
                westward = ce[k, r - 1 : r + 7, :] * (current - src[k, r - 1 : r + 7, :])
                dst[k, here, :] = current + ((southward - above) + (eastward - westward))
                current, above = below, southward
        if not final:

            @pl.when(lat == 0)
            def _():
                dst[PASSES - 1, low:high, :] = jnp.where(left, 0.0, dst[PASSES - 1, low:high, :])

            @pl.when(lat == lats - 1)
            def _():
                dst[PASSES + half, low:high, :] = jnp.where(left, dst[PASSES + half, low:high, :], 0.0)

    tall = -(-half // 8) * 8
    row = lax.broadcasted_iota(jnp.int32, (tall, LANES), 0) + jnp.where(lane_iota((tall, LANES)) < snaps, 0, shift)
    angle = ((row + lat * rows).astype(jnp.float32) + 0.5) * math.pi / (rows * lats) - math.pi / 2
    scale = jnp.sqrt(jnp.maximum(jnp.cos(angle), 0.0))
    for t in range(half):
        weighted = (dst[t + PASSES, own:east, :] * scale[t : t + 1]).astype(jnp.bfloat16)
        both = dot_t(unit, weighted).astype(jnp.bfloat16)
        y_ref[t] = both[:snaps]
        y_ref[t + shift] = both[snaps:]


def smooth(x, d, side, a, b):
    rows, snaps, width = x.shape
    count = -(-rows // 2) + 2 * PASSES
    field = VMEM((count, PADDED, LANES), jnp.float32)
    return kernel_call(
        smooth_body,
        jax.ShapeDtypeStruct((rows, snaps, width), jnp.bfloat16),
        [field] * 4 + [VMEM((width, LANES), jnp.float32), VMEM((PADDED, LANES), jnp.float32)],
    )(x, d, side, a, b)


def mm(a, b):
    return jnp.dot(a, b, precision=exact, preferred_element_type=jnp.float32)


def mmt(a, b):
    return lax.dot_general(
        a, b, (((1,), (1,)), ((), ())), precision=exact, preferred_element_type=jnp.float32
    )


def inverse_factors(grams, block=16):
    n = RANK
    row = lax.broadcasted_iota(jnp.int32, (n, LANES), 0)
    lane = lane_iota((n, LANES))
    diagonal = row == lane % n
    unit = diagonal.astype(jnp.float32)
    first = lane // n * n
    s = jnp.concatenate(list(grams) + [unit[:, :n]] * (LANES // n - len(grams)), axis=1)

    def pivots(m):
        return jnp.sum(jnp.where(diagonal, m, 0.0), axis=0, keepdims=True)

    least = pivots(s) * 1e-7 + 1e-37
    inv = unit
    done = []
    for k0 in range(0, n, block):
        tall = n - k0
        cols = [jnp.take_along_axis(s, (first + (k0 + j))[:tall], axis=1) for j in range(block)]
        floor = [jnp.take_along_axis(jnp.broadcast_to(least, (8, LANES)), (first + (k0 + j))[:8], axis=1) for j in range(block)]
        for p in range(min(block, tall - 1)):
            inverse = 1.0 / jnp.maximum(cols[p][p : p + 1], floor[p][0:1])
            below = jnp.where(row[:tall] > p, cols[p], 0.0)
            for j in range(p + 1, block):
                cols[j] = cols[j] - below * (cols[j][p : p + 1] * inverse)
            s = s - below * (s[p : p + 1] * inverse)
            inv = inv - below * (inv[p : p + 1] * inverse)
        done.append((s[:block], inv[:block]))
        s, inv = s[block:], inv[block:]
    s, inv = (jnp.concatenate(v, axis=0) for v in zip(*done))
    scale = lax.rsqrt(jnp.maximum(pivots(s), least))
    out = []
    for g in range(len(grams)):
        seg = slice(n * g, n * g + n)
        rows_scale = jnp.sum(jnp.where(diagonal[:, seg], scale[:, seg], 0.0), axis=1, keepdims=True)
        out.append(inv[:, seg] * rows_scale)
    return out


def power_bases(hs, upper_first):
    squares, starts = [], []
    for h in hs:
        n = h.shape[0]
        on = lax.broadcasted_iota(jnp.int32, (n, n), 0) == lane_iota((n, n))
        top = jnp.max(jnp.max(jnp.where(on, h, 0.0), axis=1, keepdims=True), axis=0, keepdims=True)
        unit = 1.0 / jnp.maximum(top, 1e-30)
        h2 = mm(h, h) * (unit * unit)
        squares.append(h2)
        starts.append(h2[:RANK] if upper_first is None else jnp.where(upper_first, h2[RANK:], h2[:RANK]))
    factors = inverse_factors([mmt(z, z) for z in starts])
    return [mm(mm(f, z), h2) for f, z, h2 in zip(factors, starts, squares)]


def top_rows(hs, upper_first=None):
    zs = power_bases(hs, upper_first)
    return [mm(f, z) for f, z in zip(inverse_factors([mmt(z, z) for z in zs]), zs)]


def diagonal_blocks(a, b):
    top = jnp.concatenate([a, jnp.zeros((a.shape[0], b.shape[1]), a.dtype)], axis=1)
    low = jnp.concatenate([jnp.zeros((b.shape[0], a.shape[1]), b.dtype), b], axis=1)
    return jnp.concatenate([top, low], axis=0)


def projection(gram, coef, upper_first):
    zt = power_bases([gram], upper_first)[0]
    r = mm(inverse_factors([mmt(mm(zt, gram), zt)])[0], zt)
    return mm(mmt(coef, r), r)


def pair_gram_body(own_ref, other_ref, o_ref):
    n = own_ref.shape[1]
    acc = None
    for i in range(own_ref.shape[0]):
        both = jnp.concatenate([own_ref[i], other_ref[i]], axis=0)
        part = dot_t(both, both)
        acc = part if acc is None else acc + part
    cross = jnp.where(odd(0), pltpu.roll(acc[n + n // 2 :], n, 1), acc[: n // 2])[:, n:]
    tall = o_ref.shape[1]
    packed = jnp.concatenate(
        [acc[:tall, :n], jnp.concatenate([acc[tall:n, :n], cross], axis=0)], axis=1
    )
    for j in range(o_ref.shape[0]):
        o_ref[j] = packed


def pair_gram(g, gp, n):
    tall = g.shape[0]
    rest = n - tall
    block = lambda v: jnp.concatenate([v[:, :n], v[:rest, n:]], axis=0)
    mine, theirs = g[rest:, n:], gp[rest:, n:]
    upper = odd(0)
    cross = jnp.concatenate([jnp.where(upper, theirs, mine), jnp.where(upper, mine, theirs)], axis=0)
    flipped = cross.T
    return block(g), block(gp), jnp.where(upper, flipped, cross), jnp.where(upper, cross, flipped)


def put_rows(w, stacked, o_ref):
    for i in range(o_ref.shape[0]):
        o_ref[i] = jnp.dot(w, stacked(i), preferred_element_type=jnp.float32).astype(jnp.bfloat16)


def put_modes(w, stacked, modes_ref, part_ref):
    rows, half = modes_ref.shape[0], part_ref.shape[0]
    put_rows(w, stacked, modes_ref)
    start = jnp.where(odd(0), rows - half, 0)
    for i in range(half):
        part_ref[i] = modes_ref[start + i]


def halves(rows, here_ref, there_ref):
    half = here_ref.shape[0]
    upper = odd(0)

    def row(i):
        if i < half:
            return jnp.where(upper, there_ref[i], here_ref[i])
        j = i - (rows - half)
        return jnp.where(upper, here_ref[j], there_ref[j])

    return row


def far_gram_body(own_ref, other_ref, far_ref, o_ref):
    n = own_ref.shape[1]
    acc = None
    for i in range(own_ref.shape[0]):
        part = dot_t(jnp.concatenate([own_ref[i], other_ref[i]], axis=0), far_ref[i])
        acc = part if acc is None else acc + part
    packed = jnp.concatenate([acc[:n], acc[n:]], axis=1)
    for j in range(o_ref.shape[0]):
        o_ref[j] = packed


def square(a, b, c, d):
    return jnp.concatenate(
        [jnp.concatenate([a, b], axis=1), jnp.concatenate([c, d], axis=1)], axis=0
    )


def pair_levels_body(g_ref, gp_ref, wh_ref, c_ref):
    n = c_ref.shape[0]
    own, other, cross, flipped = pair_gram(g_ref[...], gp_ref[...], n)
    gram = square(own, cross, flipped, other)
    basis = diagonal_blocks(*top_rows([own, other]))
    w = mm(top_rows([mmt(mm(basis, gram), basis)], odd(0))[0], basis)
    on = mmt(gram, w)
    c_ref[...] = on[:n]
    h = mm(w, on)
    wh_ref[...] = jnp.concatenate(
        [w, jnp.concatenate([h, jnp.zeros((RANK, LANES - RANK), jnp.float32)], axis=1)], axis=0
    )


def quad_level(wh_ref, c_ref, far_wh_ref, cs_ref, twin_ref):
    n = c_ref.shape[0]
    cs, twin = cs_ref[...], twin_ref[...]
    between = square(cs[:, :n], twin[:, n:], cs[:, n:], twin[:, :n])
    wa, wb = wh_ref[:RANK, :], far_wh_ref[:RANK, :]
    on_b = mmt(between, wb)
    mixed = mm(wa, on_b)
    gram = square(wh_ref[RANK:, :RANK], mixed, mixed.T, far_wh_ref[RANK:, :RANK])
    return diagonal_blocks(wa, wb), gram, jnp.concatenate([c_ref[...], on_b[:n]], axis=1)


def stack_of(*refs):
    return lambda i: jnp.concatenate([ref[i] for ref in refs], axis=0)


def quad_project_body(wh, c, far_wh, cs, twin, yo, yp, yy, yz, o_ref):
    w, gram, coef = quad_level(wh, c, far_wh, cs, twin)
    weights = mm(projection(gram, coef, odd(1)), w).astype(jnp.bfloat16)
    put_rows(weights, stack_of(yo, yp, yy, yz), o_ref)


def quad_modes_body(wh, c, far_wh, cs, twin, yo, yp, yy, yz, modes_ref, part_ref, h_ref, c_ref):
    w, gram, coef = quad_level(wh, c, far_wh, cs, twin)
    q = top_rows([gram], odd(1))[0]
    h_ref[...] = mmt(mm(q, gram), q)
    c_ref[...] = mmt(coef, q)
    put_modes(mm(q, w).astype(jnp.bfloat16), stack_of(yo, yp, yy, yz), modes_ref, part_ref)


def cross_body(here_ref, there_ref, y_ref, own_ref, o_ref):
    acc = None
    rows = y_ref.shape[0]
    other = halves(rows, here_ref, there_ref)
    for i in range(rows):
        theirs = other(i)
        part = dot_t(theirs, jnp.concatenate([y_ref[i], own_ref[i], theirs], axis=0))
        acc = part if acc is None else acc + part
    for j in range(o_ref.shape[0]):
        o_ref[j] = acc


def merged_gram(p_ref, h_ref, c_ref, n):
    total = p_ref[0]
    for j in range(1, p_ref.shape[0]):
        total = total + p_ref[j]
    mixed = total[:, n : n + RANK]
    gram = jnp.concatenate(
        [
            jnp.concatenate([h_ref[...], mixed.T], axis=1),
            jnp.concatenate([mixed, total[:, n + RANK :]], axis=1),
        ],
        axis=0,
    )
    coef = jnp.concatenate([c_ref[...], total[:, :n].T], axis=1)
    return gram, coef


def merge_body(level, p_ref, h_ref, c_ref, own_ref, here_ref, there_ref, modes_ref, part_ref, hn_ref, cn_ref):
    gram, coef = merged_gram(p_ref, h_ref, c_ref, c_ref.shape[0])
    w = top_rows([gram], odd(level))[0].astype(jnp.bfloat16)
    wf = w.astype(jnp.float32)
    cn_ref[...] = mmt(coef, wf)
    hn_ref[...] = mmt(mm(wf, gram), wf)
    other = halves(own_ref.shape[0], here_ref, there_ref)
    put_modes(w, lambda i: jnp.concatenate([own_ref[i], other(i)], axis=0), modes_ref, part_ref)


def project_body(level, p_ref, h_ref, c_ref, own_ref, here_ref, there_ref, o_ref):
    gram, coef = merged_gram(p_ref, h_ref, c_ref, c_ref.shape[0])
    weights = projection(gram, coef, odd(level)).astype(jnp.bfloat16)
    other = halves(own_ref.shape[0], here_ref, there_ref)
    put_rows(weights, lambda i: jnp.concatenate([own_ref[i], other(i)], axis=0), o_ref)


def exchanged(block, level):
    count = lax.axis_size("tm")
    return lax.ppermute(block, "tm", [(i, i ^ 1 << level) for i in range(count)])


def gathered(parts):
    return lax.all_to_all(parts, ("lat", "lon"), 0, 0, tiled=True)


def shards(residuals, diffusivity):
    snaps, rows, width = residuals.shape
    tiles = lax.axis_size("lat") * lax.axis_size("lon")
    levels = lax.axis_size("tm").bit_length() - 1
    f32 = lambda *shape: jax.ShapeDtypeStruct(shape, jnp.float32)
    b16 = lambda *shape: jax.ShapeDtypeStruct(shape, jnp.bfloat16)
    x = jnp.transpose(residuals, (1, 0, 2))
    y = smooth(x, diffusivity, *halo_exchange(x, diffusivity))
    other, far = exchanged(y, 0), exchanged(y, 1)
    pair = kernel_call(pair_gram_body, f32(tiles, snaps * 3 // 4, 2 * snaps))(y, other)
    pair = jnp.sum(gathered(pair), axis=0)
    cross = kernel_call(far_gram_body, f32(tiles, snaps, 2 * snaps))(y, other, far)
    cross = jnp.sum(gathered(cross), axis=0)
    wh, c = kernel_call(
        pair_levels_body, (f32(2 * RANK, 2 * snaps), f32(snaps, RANK)), flops=1 << 32
    )(pair, exchanged(pair, 0))
    operands = (wh, c, exchanged(wh, 1), cross, exchanged(cross, 0))
    operands += (y, other, far, exchanged(far, 0))
    if levels == 2:
        out = kernel_call(quad_project_body, b16(rows, snaps, width))(*operands)
        return jnp.transpose(out, (1, 0, 2))
    block = (
        b16(rows, RANK, width),
        b16(-(-rows // 2), RANK, width),
        f32(RANK, RANK),
        f32(snaps, RANK),
    )
    modes, part, h, c = kernel_call(quad_modes_body, block)(*operands)
    for level in range(2, levels):
        here = exchanged(part, level)
        there = exchanged(here, 0)
        parts = gathered(kernel_call(cross_body, f32(tiles, RANK, snaps + 2 * RANK))(here, there, y, modes))
        if level < levels - 1:
            modes, part, h, c = kernel_call(functools.partial(merge_body, level), block)(
                parts, h, c, modes, here, there
            )
    out = kernel_call(functools.partial(project_body, levels - 1), b16(rows, snaps, width))(
        parts, h, c, modes, here, there
    )
    return jnp.transpose(out, (1, 0, 2))


def solution(mesh):
    return jax.shard_map(
        shards,
        mesh=mesh,
        in_specs=(P("tm", "lat", "lon"), P("lat", "lon")),
        out_specs=P("tm", "lat", "lon"),
        check_vma=False,
    )
```

```python
import functools
import math

import jax
import jax.numpy as jnp
from jax import lax
from jax.experimental import pallas as pl
from jax.experimental.pallas import tpu as pltpu
from jax.sharding import PartitionSpec as P

RANK = 32
PASSES = 4
LANES = 128
exact = lax.Precision.HIGHEST
VMEM = pltpu.VMEM


def whole():
    return pl.BlockSpec(memory_space=VMEM)


def kernel_call(body, outs, scratch=(), flops=1 << 20, specs=None, vmem=48 << 20):
    return pl.pallas_call(
        body,
        out_shape=outs,
        **({} if specs is None else {"in_specs": specs}),
        out_specs=jax.tree.map(lambda _: whole(), outs),
        scratch_shapes=list(scratch),
        compiler_params=pltpu.CompilerParams(vmem_limit_bytes=vmem),
        cost_estimate=pl.CostEstimate(flops=flops, bytes_accessed=1 << 20, transcendentals=0),
    )


def lane_iota(shape):
    return lax.broadcasted_iota(jnp.int32, shape, len(shape) - 1)


def roll(x, shift):
    return pltpu.roll(x, shift % LANES, x.ndim - 1)


def eye(n, dtype=jnp.bfloat16):
    row = lax.broadcasted_iota(jnp.int32, (n, n), 0)
    return (row == lax.broadcasted_iota(jnp.int32, (n, n), 1)).astype(dtype)


def dot_t(a, b):
    return lax.dot_general(a, b, (((1,), (1,)), ((), ())), preferred_element_type=jnp.float32)


def split2(v):
    high = v.astype(jnp.bfloat16)
    return high, (v - high.astype(jnp.float32)).astype(jnp.bfloat16)


def odd(level):
    return (lax.axis_index("tm") >> level & 1) == 1


def even_lat():
    return lax.axis_index("lat") % 2 == 0


def edge_body(x_hbm, d_hbm, a_ref, b_ref, d_ref, sems):
    rows, snaps, width = x_hbm.shape
    even = even_lat()
    flags = ((a_ref, even), (b_ref, jnp.logical_not(even)))
    copies = [pltpu.make_async_copy(d_hbm, d_ref, sems.at[0])]
    for ref, south in flags:
        start = jnp.where(south, rows - PASSES, 0)
        for r in range(PASSES):
            copies.append(
                pltpu.make_async_copy(
                    x_hbm.at[start + r], ref.at[pl.ds(r * snaps, snaps)], sems.at[len(copies)]
                )
            )
    for copy in copies:
        copy.start()
    copies[0].wait()
    pad = jnp.zeros((8, width), jnp.float32)
    edge = lambda lo: [v.astype(jnp.float32) for v in split2(d_ref[lo : lo + PASSES, :])]
    first, final = edge(0), edge(rows - PASSES)
    for ref, south in flags:
        term = [jnp.where(south, f, g) for f, g in zip(final, first)]
        ref[PASSES * snaps :, :] = jnp.concatenate(term + [pad], axis=0).astype(jnp.bfloat16)
    for copy in copies[1:]:
        copy.wait()


def by_side(a_ref, b_ref):
    even = even_lat()

    def picked(lo, hi):
        a, b = a_ref[lo:hi, :], b_ref[lo:hi, :]
        return jnp.where(even, b, a), jnp.where(even, a, b)

    return picked


def tile_rows(x_ref, north, south, t):
    rows, snaps, _ = x_ref.shape
    first = north[(t + PASSES) * snaps : (t + PASSES + 1) * snaps] if t < 0 else x_ref[t]
    r = t + rows // 2
    second = x_ref[r] if r < rows else south[(r - rows) * snaps : (r - rows + 1) * snaps]
    return jnp.concatenate([first, second], axis=0)


def extend_rows(dn, d_ref, north_d, south_d):
    rows = d_ref.shape[0]
    dn[...] = jnp.zeros(dn.shape, jnp.float32)
    dn[PASSES : PASSES + rows, :] = d_ref[...]
    dn[0:PASSES, :] = north_d[0:PASSES] + north_d[PASSES : 2 * PASSES]
    dn[PASSES + rows : 2 * PASSES + rows, :] = south_d[0:PASSES] + south_d[PASSES : 2 * PASSES]


def pack_body(x_ref, d_ref, b_ref, a_ref, m_ref, dn):
    rows, snaps, width = x_ref.shape
    half = -(-rows // 2)
    count = half + 2 * PASSES
    edge = PASSES * snaps
    row = lax.broadcasted_iota(jnp.int32, (16, width), 0)
    lane = lane_iota((16, width))
    column = jnp.where(row % 8 < PASSES, row % 8, width - 8 + row % 8)
    pick = [((lane == column) & (row // 8 == k)).astype(jnp.bfloat16) for k in range(2)]
    picked = by_side(a_ref, b_ref)
    north, south = picked(0, edge)
    north_d, south_d = (v.astype(jnp.float32) for v in picked(edge, edge + 16))
    for k in range(0, count, 2):
        out = dot_t(pick[0], tile_rows(x_ref, north, south, k - PASSES))
        if k + 1 < count:
            out = out + dot_t(pick[1], tile_rows(x_ref, north, south, k + 1 - PASSES))
        m_ref[8 * k : 8 * k + 16, :] = out.astype(jnp.bfloat16)
    extend_rows(dn, d_ref, north_d, south_d)
    high, low = split2(dn[...])
    end = m_ref.shape[0]
    m_ref[end - 16 :, :] = (dot_t(pick[0], high) + dot_t(pick[1], low)).astype(jnp.bfloat16)


def halo_exchange(x, d):
    rows, snaps, width = x.shape
    count = -(-rows // 2) + 2 * PASSES
    shape = lambda n: jax.ShapeDtypeStruct((n, width), jnp.bfloat16)
    edge = PASSES * snaps + 16
    hbm = pl.BlockSpec(memory_space=pltpu.HBM)
    a, b = kernel_call(
        edge_body,
        (shape(edge), shape(edge)),
        [VMEM(d.shape, d.dtype), pltpu.SemaphoreType.DMA((2 * PASSES + 1,))],
        specs=[hbm, hbm],
        vmem=60 << 20,
    )(x, d)
    lons, lats = lax.axis_size("lon"), lax.axis_size("lat")

    def swapped(message, start):
        pairs = [(i, i + 1) for i in range(start, lats - 1, 2)]
        return lax.ppermute(message, "lat", pairs + [(j, i) for i, j in pairs])

    a, b = swapped(a, 0), swapped(b, 1)
    packed = kernel_call(
        pack_body, shape(16 * (-(-count // 2)) + 16), [VMEM((width, LANES), jnp.float32)]
    )(x, d, b, a)
    forward = [(i, (i + 1) % lons) for i in range(lons)]
    side = lax.ppermute(packed, "lon", forward)
    if lons > 2:
        from_east = lax.ppermute(packed, "lon", [(j, i) for i, j in forward])
        side = jnp.where(lax.broadcasted_iota(jnp.int32, side.shape, 0) % 8 < PASSES, from_east, side)
    return side, a, b


PADDED = 160


def smooth_body(x_ref, d_ref, side_ref, a_ref, b_ref, y_ref, u0, u1, ce, cs, dn, dt):
    rows, snaps, width = x_ref.shape
    half = -(-rows // 2)
    shift = rows - half
    count = half + 2 * PASSES
    lats, lat = lax.axis_size("lat"), lax.axis_index("lat")
    lane = lane_iota((1, LANES))
    left = lane < snaps
    own = 16
    east = own + width
    unit = eye(width)
    edge = PASSES * snaps
    picked = by_side(a_ref, b_ref)
    north, south = picked(0, edge)
    north_d, south_d = (v.astype(jnp.float32) for v in picked(edge, edge + 16))

    for k in range(count):
        u0[k, own:east, :] = dot_t(unit, tile_rows(x_ref, north, south, k - PASSES))
        pair = side_ref[16 * (k // 2) : 16 * (k // 2) + 16, :].astype(jnp.float32)
        halo = pair[8 * (k % 2) : 8 * (k % 2) + 8]
        u0[k, own - 8 : own, :] = halo
        u0[k, east : east + 8, :] = halo

    extend_rows(dn, d_ref, north_d, south_d)
    dt[own:east, :] = dn[...].T
    side_d = side_ref[side_ref.shape[0] - 16 :, :].astype(jnp.float32)
    halo = side_d[0:8] + side_d[8:16]
    dt[0 : own - 8, :] = jnp.zeros((own - 8, LANES), jnp.float32)
    dt[own - 8 : own, :] = halo
    dt[east : east + 8, :] = halo
    dt[east + 8 :, :] = jnp.zeros((PADDED - east - 8, LANES), jnp.float32)
    low, high = own - 8, east + 8
    here = dt[low:high, :]
    faces = jnp.concatenate([here + dt[low + 1 : high + 1, :], here + roll(here, -1)], axis=0) * 0.5
    f_high, f_low = split2(faces)
    terms = jnp.where(lane < LANES // 2, f_high.astype(jnp.float32), roll(f_low.astype(jnp.float32), LANES // 2))
    terms = terms.astype(jnp.bfloat16)
    source = lax.broadcasted_iota(jnp.int32, (LANES, LANES), 0) % (LANES // 2)
    offset = jnp.where(lane_iota((LANES, LANES)) < snaps, 0, shift)
    relative = source - offset
    for k in range(count):
        spread = jnp.dot(
            terms, (relative == k).astype(jnp.bfloat16), preferred_element_type=jnp.float32
        )
        ce[k, low:high, :] = spread[: high - low]
        cs[k, low:high, :] = spread[high - low :]

    buffers = (u0, u1)
    first_row = lax.broadcasted_iota(jnp.int32, (8, LANES), 0) == 0
    for step in range(PASSES):
        src, dst = buffers[step % 2], buffers[(step + 1) % 2]
        final = step == PASSES - 1
        start, stop = step + 1, count - 1 - step
        blocks = range(own, east, 8) if final else range(low, high, 8)
        current = [src[start, r : r + 8, :] for r in blocks]
        above = [
            cs[start - 1, r : r + 8, :] * (c - src[start - 1, r : r + 8, :])
            for r, c in zip(blocks, current)
        ]

        def eastward(k, r, here):
            return ce[k, r : r + 8, :] * (src[k, r + 1 : r + 9, :] - here)

        for k in range(start, stop):
            before = None
            if final:
                before = pltpu.roll(eastward(k, low, src[k, low:own, :]), 1, 0)
            for i, r in enumerate(blocks):
                here = current[i]
                east_flux = eastward(k, r, here)
                turned = pltpu.roll(east_flux, 1, 0)
                west_flux = turned if before is None else jnp.where(first_row, before, turned)
                below = src[k + 1, r : r + 8, :]
                south_flux = cs[k, r : r + 8, :] * (below - here)
                dst[k, r : r + 8, :] = here + ((south_flux - above[i]) + (east_flux - west_flux))
                current[i], above[i], before = below, south_flux, turned
        if not final:

            @pl.when(lat == 0)
            def _():
                dst[PASSES - 1, low:high, :] = jnp.where(left, 0.0, dst[PASSES - 1, low:high, :])

            @pl.when(lat == lats - 1)
            def _():
                dst[PASSES + half, low:high, :] = jnp.where(left, dst[PASSES + half, low:high, :], 0.0)

    tall = -(-half // 8) * 8
    row = lax.broadcasted_iota(jnp.int32, (tall, LANES), 0) + jnp.where(lane_iota((tall, LANES)) < snaps, 0, shift)
    angle = ((row + lat * rows).astype(jnp.float32) + 0.5) * math.pi / (rows * lats) - math.pi / 2
    scale = jnp.sqrt(jnp.maximum(jnp.cos(angle), 0.0))
    for t in range(half):
        weighted = (dst[t + PASSES, own:east, :] * scale[t : t + 1]).astype(jnp.bfloat16)
        both = dot_t(unit, weighted).astype(jnp.bfloat16)
        y_ref[t] = both[:snaps]
        y_ref[t + shift] = both[snaps:]


def smooth(x, d, side, a, b):
    rows, snaps, width = x.shape
    count = -(-rows // 2) + 2 * PASSES
    field = VMEM((count, PADDED, LANES), jnp.float32)
    return kernel_call(
        smooth_body,
        jax.ShapeDtypeStruct((rows, snaps, width), jnp.bfloat16),
        [field] * 4 + [VMEM((width, LANES), jnp.float32), VMEM((PADDED, LANES), jnp.float32)],
    )(x, d, side, a, b)


def mm(a, b):
    return jnp.dot(a, b, precision=exact, preferred_element_type=jnp.float32)


def mmt(a, b):
    return lax.dot_general(
        a, b, (((1,), (1,)), ((), ())), precision=exact, preferred_element_type=jnp.float32
    )


def inverse_factors(grams, block=16):
    n = RANK
    row = lax.broadcasted_iota(jnp.int32, (n, LANES), 0)
    lane = lane_iota((n, LANES))
    diagonal = row == lane % n
    unit = diagonal.astype(jnp.float32)
    first = lane // n * n
    s = jnp.concatenate(list(grams) + [unit[:, :n]] * (LANES // n - len(grams)), axis=1)

    def pivots(m):
        return jnp.sum(jnp.where(diagonal, m, 0.0), axis=0, keepdims=True)

    least = jnp.max(pivots(s), axis=1, keepdims=True) * 1e-12 + 1e-37
    inv = unit
    done = []
    for k0 in range(0, n, block):
        tall = n - k0
        cols = [jnp.take_along_axis(s, (first + (k0 + j))[:tall], axis=1) for j in range(block)]
        for p in range(min(block, tall - 1)):
            inverse = 1.0 / jnp.maximum(cols[p][p : p + 1], least)
            below = jnp.where(row[:tall] > p, cols[p], 0.0)
            for j in range(p + 1, block):
                cols[j] = cols[j] - below * (cols[j][p : p + 1] * inverse)
            s = s - below * (s[p : p + 1] * inverse)
            inv = inv - below * (inv[p : p + 1] * inverse)
        done.append((s[:block], inv[:block]))
        s, inv = s[block:], inv[block:]
    s, inv = (jnp.concatenate(v, axis=0) for v in zip(*done))
    scale = lax.rsqrt(jnp.maximum(pivots(s), least))
    out = []
    for g in range(len(grams)):
        seg = slice(n * g, n * g + n)
        rows_scale = jnp.sum(jnp.where(diagonal[:, seg], scale[:, seg], 0.0), axis=1, keepdims=True)
        out.append(inv[:, seg] * rows_scale)
    return out


def power_bases(hs, upper_first):
    squares, starts = [], []
    for h in hs:
        n = h.shape[0]
        on = lax.broadcasted_iota(jnp.int32, (n, n), 0) == lane_iota((n, n))
        top = jnp.max(jnp.max(jnp.where(on, h, 0.0), axis=1, keepdims=True), axis=0, keepdims=True)
        unit = 1.0 / jnp.maximum(top, 1e-30)
        h2 = mm(h, h) * (unit * unit)
        squares.append(h2)
        starts.append(h2[:RANK] if upper_first is None else jnp.where(upper_first, h2[RANK:], h2[:RANK]))
    factors = inverse_factors([mmt(z, z) for z in starts])
    return [mm(mm(f, z), h2) for f, z, h2 in zip(factors, starts, squares)]


def top_rows(hs, upper_first=None):
    zs = power_bases(hs, upper_first)
    return [mm(f, z) for f, z in zip(inverse_factors([mmt(z, z) for z in zs]), zs)]


def diagonal_blocks(a, b):
    top = jnp.concatenate([a, jnp.zeros((a.shape[0], b.shape[1]), a.dtype)], axis=1)
    low = jnp.concatenate([jnp.zeros((b.shape[0], a.shape[1]), b.dtype), b], axis=1)
    return jnp.concatenate([top, low], axis=0)


def projection(gram, coef, upper_first, w=None):
    zt = power_bases([gram], upper_first)[0]
    on, out = mmt(coef, zt), zt if w is None else mm(zt, w)
    f = inverse_factors([mmt(mm(zt, gram), zt)])[0]
    return mm(mmt(on, f), mm(f, out))


def pair_gram_body(own_ref, other_ref, o_ref):
    n = own_ref.shape[1]
    acc = None
    for i in range(own_ref.shape[0]):
        both = jnp.concatenate([own_ref[i], other_ref[i]], axis=0)
        part = dot_t(both, both)
        acc = part if acc is None else acc + part
    cross = jnp.where(odd(0), pltpu.roll(acc[n + n // 2 :], n, 1), acc[: n // 2])[:, n:]
    tall = o_ref.shape[1]
    packed = jnp.concatenate(
        [acc[:tall, :n], jnp.concatenate([acc[tall:n, :n], cross], axis=0)], axis=1
    )
    for j in range(o_ref.shape[0]):
        o_ref[j] = packed


def pair_gram(g, gp, n):
    tall = g.shape[0]
    rest = n - tall
    block = lambda v: jnp.concatenate([v[:, :n], v[:rest, n:]], axis=0)
    mine, theirs = g[rest:, n:], gp[rest:, n:]
    upper = odd(0)
    cross = jnp.concatenate([jnp.where(upper, theirs, mine), jnp.where(upper, mine, theirs)], axis=0)
    flipped = cross.T
    return block(g), block(gp), jnp.where(upper, flipped, cross), jnp.where(upper, cross, flipped)


def put_rows(w, stacked, o_ref):
    for i in range(o_ref.shape[0]):
        o_ref[i] = jnp.dot(w, stacked(i), preferred_element_type=jnp.float32).astype(jnp.bfloat16)


def put_modes(w, stacked, modes_ref, part_ref):
    rows, half = modes_ref.shape[0], part_ref.shape[0]
    put_rows(w, stacked, modes_ref)
    start = jnp.where(odd(0), rows - half, 0)
    for i in range(half):
        part_ref[i] = modes_ref[start + i]


def halves(rows, here_ref, there_ref):
    half = here_ref.shape[0]
    upper = odd(0)

    def row(i):
        if i < half:
            return jnp.where(upper, there_ref[i], here_ref[i])
        j = i - (rows - half)
        return jnp.where(upper, here_ref[j], there_ref[j])

    return row


def far_gram_body(own_ref, other_ref, far_ref, o_ref):
    n = own_ref.shape[1]
    acc = None
    for i in range(own_ref.shape[0]):
        part = dot_t(jnp.concatenate([own_ref[i], other_ref[i]], axis=0), far_ref[i])
        acc = part if acc is None else acc + part
    packed = jnp.concatenate([acc[:n], acc[n:]], axis=1)
    for j in range(o_ref.shape[0]):
        o_ref[j] = packed


def square(a, b, c, d):
    return jnp.concatenate(
        [jnp.concatenate([a, b], axis=1), jnp.concatenate([c, d], axis=1)], axis=0
    )


def pair_levels_body(g_ref, gp_ref, wh_ref, c_ref):
    n = c_ref.shape[0]
    own, other, cross, flipped = pair_gram(g_ref[...], gp_ref[...], n)
    gram = square(own, cross, flipped, other)
    basis = diagonal_blocks(*top_rows([own, other]))
    merged = mmt(mm(basis, gram), basis)
    q = top_rows([merged], odd(0))[0]
    h = mmt(mm(q, merged), q)
    w = mm(q, basis)
    c_ref[...] = mmt(gram[:n], w)
    wh_ref[...] = jnp.concatenate(
        [w, jnp.concatenate([h, jnp.zeros((RANK, LANES - RANK), jnp.float32)], axis=1)], axis=0
    )


def quad_level(wh_ref, c_ref, far_wh_ref, cs_ref, twin_ref):
    n = c_ref.shape[0]
    cs, twin = cs_ref[...], twin_ref[...]
    between = square(cs[:, :n], twin[:, n:], cs[:, n:], twin[:, :n])
    wa, wb = wh_ref[:RANK, :], far_wh_ref[:RANK, :]
    on_b = mmt(between, wb)
    mixed = mm(wa, on_b)
    gram = square(wh_ref[RANK:, :RANK], mixed, mixed.T, far_wh_ref[RANK:, :RANK])
    return diagonal_blocks(wa, wb), gram, jnp.concatenate([c_ref[...], on_b[:n]], axis=1)


def stack_of(*refs):
    return lambda i: jnp.concatenate([ref[i] for ref in refs], axis=0)


def quad_project_body(wh, c, far_wh, cs, twin, yo, yp, yy, yz, o_ref):
    w, gram, coef = quad_level(wh, c, far_wh, cs, twin)
    weights = projection(gram, coef, odd(1), w).astype(jnp.bfloat16)
    put_rows(weights, stack_of(yo, yp, yy, yz), o_ref)


def quad_modes_body(wh, c, far_wh, cs, twin, yo, yp, yy, yz, modes_ref, part_ref, h_ref, c_ref):
    w, gram, coef = quad_level(wh, c, far_wh, cs, twin)
    q = top_rows([gram], odd(1))[0]
    h_ref[...] = mmt(mm(q, gram), q)
    c_ref[...] = mmt(coef, q)
    put_modes(mm(q, w).astype(jnp.bfloat16), stack_of(yo, yp, yy, yz), modes_ref, part_ref)


def cross_body(here_ref, there_ref, y_ref, own_ref, o_ref):
    acc = None
    rows = y_ref.shape[0]
    other = halves(rows, here_ref, there_ref)
    for i in range(rows):
        theirs = other(i)
        part = dot_t(theirs, jnp.concatenate([y_ref[i], own_ref[i], theirs], axis=0))
        acc = part if acc is None else acc + part
    for j in range(o_ref.shape[0]):
        o_ref[j] = acc


def merged_gram(p_ref, h_ref, c_ref, n):
    total = p_ref[0]
    for j in range(1, p_ref.shape[0]):
        total = total + p_ref[j]
    mixed = total[:, n : n + RANK]
    gram = jnp.concatenate(
        [
            jnp.concatenate([h_ref[...], mixed.T], axis=1),
            jnp.concatenate([mixed, total[:, n + RANK :]], axis=1),
        ],
        axis=0,
    )
    coef = jnp.concatenate([c_ref[...], total[:, :n].T], axis=1)
    return gram, coef


def merge_body(level, p_ref, h_ref, c_ref, own_ref, here_ref, there_ref, modes_ref, part_ref, hn_ref, cn_ref):
    gram, coef = merged_gram(p_ref, h_ref, c_ref, c_ref.shape[0])
    w = top_rows([gram], odd(level))[0].astype(jnp.bfloat16)
    wf = w.astype(jnp.float32)
    cn_ref[...] = mmt(coef, wf)
    hn_ref[...] = mmt(mm(wf, gram), wf)
    other = halves(own_ref.shape[0], here_ref, there_ref)
    put_modes(w, lambda i: jnp.concatenate([own_ref[i], other(i)], axis=0), modes_ref, part_ref)


def project_body(level, p_ref, h_ref, c_ref, own_ref, here_ref, there_ref, o_ref):
    gram, coef = merged_gram(p_ref, h_ref, c_ref, c_ref.shape[0])
    weights = projection(gram, coef, odd(level)).astype(jnp.bfloat16)
    other = halves(own_ref.shape[0], here_ref, there_ref)
    put_rows(weights, lambda i: jnp.concatenate([own_ref[i], other(i)], axis=0), o_ref)


def exchanged(block, level):
    count = lax.axis_size("tm")
    return lax.ppermute(block, "tm", [(i, i ^ 1 << level) for i in range(count)])


def gathered(parts):
    return lax.all_to_all(parts, ("lat", "lon"), 0, 0, tiled=True)


def shards(residuals, diffusivity):
    snaps, rows, width = residuals.shape
    tiles = lax.axis_size("lat") * lax.axis_size("lon")
    levels = lax.axis_size("tm").bit_length() - 1
    f32 = lambda *shape: jax.ShapeDtypeStruct(shape, jnp.float32)
    b16 = lambda *shape: jax.ShapeDtypeStruct(shape, jnp.bfloat16)
    x = jnp.transpose(residuals, (1, 0, 2))
    y = smooth(x, diffusivity, *halo_exchange(x, diffusivity))
    other, far = exchanged(y, 0), exchanged(y, 1)
    pair = kernel_call(pair_gram_body, f32(tiles, snaps * 3 // 4, 2 * snaps))(y, other)
    pair = jnp.sum(gathered(pair), axis=0)
    cross = kernel_call(far_gram_body, f32(tiles, snaps, 2 * snaps))(y, other, far)
    cross = jnp.sum(gathered(cross), axis=0)
    wh, c = kernel_call(
        pair_levels_body, (f32(2 * RANK, 2 * snaps), f32(snaps, RANK)), flops=1 << 32
    )(pair, exchanged(pair, 0))
    operands = (wh, c, exchanged(wh, 1), cross, exchanged(cross, 0))
    operands += (y, other, far, exchanged(far, 0))
    if levels == 2:
        out = kernel_call(quad_project_body, b16(rows, snaps, width))(*operands)
        return jnp.transpose(out, (1, 0, 2))
    block = (
        b16(rows, RANK, width),
        b16(-(-rows // 2), RANK, width),
        f32(RANK, RANK),
        f32(snaps, RANK),
    )
    modes, part, h, c = kernel_call(quad_modes_body, block)(*operands)
    for level in range(2, levels):
        here = exchanged(part, level)
        there = exchanged(here, 0)
        parts = gathered(kernel_call(cross_body, f32(tiles, RANK, snaps + 2 * RANK))(here, there, y, modes))
        if level < levels - 1:
            modes, part, h, c = kernel_call(functools.partial(merge_body, level), block)(
                parts, h, c, modes, here, there
            )
    out = kernel_call(functools.partial(project_body, levels - 1), b16(rows, snaps, width))(
        parts, h, c, modes, here, there
    )
    return jnp.transpose(out, (1, 0, 2))


def solution(mesh):
    return jax.shard_map(
        shards,
        mesh=mesh,
        in_specs=(P("tm", "lat", "lon"), P("lat", "lon")),
        out_specs=P("tm", "lat", "lon"),
        check_vma=False,
    )
```

```python
import functools
import math

import jax
import jax.numpy as jnp
from jax import lax
from jax.experimental import pallas as pl
from jax.experimental.pallas import tpu as pltpu
from jax.sharding import PartitionSpec as P

RANK = 32
PASSES = 4
LANES = 128
exact = lax.Precision.HIGHEST
VMEM = pltpu.VMEM


def whole():
    return pl.BlockSpec(memory_space=VMEM)


def kernel_call(body, outs, scratch=(), flops=1 << 20, specs=None, vmem=48 << 20, out_spec=None):
    return pl.pallas_call(
        body,
        out_shape=outs,
        **({} if specs is None else {"in_specs": specs}),
        out_specs=jax.tree.map(lambda _: out_spec or whole(), outs),
        scratch_shapes=list(scratch),
        compiler_params=pltpu.CompilerParams(vmem_limit_bytes=vmem),
        cost_estimate=pl.CostEstimate(flops=flops, bytes_accessed=1 << 20, transcendentals=0),
    )


def lane_iota(shape):
    return lax.broadcasted_iota(jnp.int32, shape, len(shape) - 1)


def roll(x, shift):
    return pltpu.roll(x, shift % LANES, x.ndim - 1)


def eye(n, dtype=jnp.bfloat16):
    row = lax.broadcasted_iota(jnp.int32, (n, n), 0)
    return (row == lax.broadcasted_iota(jnp.int32, (n, n), 1)).astype(dtype)


def dot_t(a, b):
    return lax.dot_general(a, b, (((1,), (1,)), ((), ())), preferred_element_type=jnp.float32)


def split2(v):
    high = v.astype(jnp.bfloat16)
    return high, (v - high.astype(jnp.float32)).astype(jnp.bfloat16)


def odd(level):
    return (lax.axis_index("tm") >> level & 1) == 1


def even_lat():
    return lax.axis_index("lat") % 2 == 0


def edge_body(x_hbm, d_hbm, a_ref, b_ref, d_ref, sems):
    rows, snaps, width = x_hbm.shape
    even = even_lat()
    flags = ((a_ref, even), (b_ref, jnp.logical_not(even)))
    copies = [pltpu.make_async_copy(d_hbm, d_ref, sems.at[0])]
    for ref, south in flags:
        start = jnp.where(south, rows - PASSES, 0)
        for r in range(PASSES):
            copies.append(
                pltpu.make_async_copy(
                    x_hbm.at[start + r], ref.at[pl.ds(r * snaps, snaps)], sems.at[len(copies)]
                )
            )
    for copy in copies:
        copy.start()
    copies[0].wait()
    pad = jnp.zeros((8, width), jnp.float32)
    edge = lambda lo: [v.astype(jnp.float32) for v in split2(d_ref[lo : lo + PASSES, :])]
    first, final = edge(0), edge(rows - PASSES)
    for ref, south in flags:
        term = [jnp.where(south, f, g) for f, g in zip(final, first)]
        ref[PASSES * snaps :, :] = jnp.concatenate(term + [pad], axis=0).astype(jnp.bfloat16)
    for copy in copies[1:]:
        copy.wait()


def by_side(a_ref, b_ref):
    even = even_lat()

    def picked(lo, hi):
        a, b = a_ref[lo:hi, :], b_ref[lo:hi, :]
        return jnp.where(even, b, a), jnp.where(even, a, b)

    return picked


def tile_rows(x_ref, north, south, t):
    rows, snaps, _ = x_ref.shape
    first = north[(t + PASSES) * snaps : (t + PASSES + 1) * snaps] if t < 0 else x_ref[t]
    r = t + rows // 2
    second = x_ref[r] if r < rows else south[(r - rows) * snaps : (r - rows + 1) * snaps]
    return jnp.concatenate([first, second], axis=0)


def extend_rows(dn, d_ref, north_d, south_d):
    rows = d_ref.shape[0]
    dn[...] = jnp.zeros(dn.shape, jnp.float32)
    dn[PASSES : PASSES + rows, :] = d_ref[...]
    dn[0:PASSES, :] = north_d[0:PASSES] + north_d[PASSES : 2 * PASSES]
    dn[PASSES + rows : 2 * PASSES + rows, :] = south_d[0:PASSES] + south_d[PASSES : 2 * PASSES]


def pack_body(x_ref, d_ref, b_ref, a_ref, m_ref, dn):
    rows, snaps, width = x_ref.shape
    half = -(-rows // 2)
    count = half + 2 * PASSES
    edge = PASSES * snaps
    row = lax.broadcasted_iota(jnp.int32, (16, width), 0)
    lane = lane_iota((16, width))
    column = jnp.where(row % 8 < PASSES, row % 8, width - 8 + row % 8)
    pick = [((lane == column) & (row // 8 == k)).astype(jnp.bfloat16) for k in range(2)]
    picked = by_side(a_ref, b_ref)
    north, south = picked(0, edge)
    north_d, south_d = (v.astype(jnp.float32) for v in picked(edge, edge + 16))
    for k in range(0, count, 2):
        out = dot_t(pick[0], tile_rows(x_ref, north, south, k - PASSES))
        if k + 1 < count:
            out = out + dot_t(pick[1], tile_rows(x_ref, north, south, k + 1 - PASSES))
        m_ref[8 * k : 8 * k + 16, :] = out.astype(jnp.bfloat16)
    extend_rows(dn, d_ref, north_d, south_d)
    high, low = split2(dn[...])
    end = m_ref.shape[0]
    m_ref[end - 16 :, :] = (dot_t(pick[0], high) + dot_t(pick[1], low)).astype(jnp.bfloat16)


def halo_exchange(x, d):
    rows, snaps, width = x.shape
    count = -(-rows // 2) + 2 * PASSES
    shape = lambda n: jax.ShapeDtypeStruct((n, width), jnp.bfloat16)
    edge = PASSES * snaps + 16
    hbm = pl.BlockSpec(memory_space=pltpu.HBM)
    a, b = kernel_call(
        edge_body,
        (shape(edge), shape(edge)),
        [VMEM(d.shape, d.dtype), pltpu.SemaphoreType.DMA((2 * PASSES + 1,))],
        specs=[hbm, hbm],
        vmem=60 << 20,
    )(x, d)
    lons, lats = lax.axis_size("lon"), lax.axis_size("lat")

    def swapped(message, start):
        pairs = [(i, i + 1) for i in range(start, lats - 1, 2)]
        return lax.ppermute(message, "lat", pairs + [(j, i) for i, j in pairs])

    a, b = swapped(a, 0), swapped(b, 1)
    packed = kernel_call(
        pack_body, shape(16 * (-(-count // 2)) + 16), [VMEM((width, LANES), jnp.float32)]
    )(x, d, b, a)
    forward = [(i, (i + 1) % lons) for i in range(lons)]
    side = lax.ppermute(packed, "lon", forward)
    if lons > 2:
        from_east = lax.ppermute(packed, "lon", [(j, i) for i, j in forward])
        side = jnp.where(lax.broadcasted_iota(jnp.int32, side.shape, 0) % 8 < PASSES, from_east, side)
    return side, a, b


PADDED = 160


def smooth_body(x_ref, d_ref, side_ref, a_ref, b_ref, y_ref, u0, u1, ce, cs, dn, dt):
    rows, snaps, width = x_ref.shape
    half = -(-rows // 2)
    shift = rows - half
    count = half + 2 * PASSES
    lats, lat = lax.axis_size("lat"), lax.axis_index("lat")
    lane = lane_iota((1, LANES))
    left = lane < snaps
    own = 16
    east = own + width
    unit = eye(width)
    edge = PASSES * snaps
    picked = by_side(a_ref, b_ref)
    north, south = picked(0, edge)
    north_d, south_d = (v.astype(jnp.float32) for v in picked(edge, edge + 16))

    for k in range(count):
        u0[k, own:east, :] = dot_t(unit, tile_rows(x_ref, north, south, k - PASSES))
        pair = side_ref[16 * (k // 2) : 16 * (k // 2) + 16, :].astype(jnp.float32)
        halo = pair[8 * (k % 2) : 8 * (k % 2) + 8]
        u0[k, own - 8 : own, :] = halo
        u0[k, east : east + 8, :] = halo

    extend_rows(dn, d_ref, north_d, south_d)
    dt[own:east, :] = dn[...].T
    side_d = side_ref[side_ref.shape[0] - 16 :, :].astype(jnp.float32)
    halo = side_d[0:8] + side_d[8:16]
    dt[0 : own - 8, :] = jnp.zeros((own - 8, LANES), jnp.float32)
    dt[own - 8 : own, :] = halo
    dt[east : east + 8, :] = halo
    dt[east + 8 :, :] = jnp.zeros((PADDED - east - 8, LANES), jnp.float32)
    low, high = own - 8, east + 8
    here = dt[low:high, :]
    faces = jnp.concatenate([here + dt[low + 1 : high + 1, :], here + roll(here, -1)], axis=0) * 0.5
    f_high, f_low = split2(faces)
    terms = jnp.where(lane < LANES // 2, f_high.astype(jnp.float32), roll(f_low.astype(jnp.float32), LANES // 2))
    terms = terms.astype(jnp.bfloat16)
    source = lax.broadcasted_iota(jnp.int32, (LANES, LANES), 0) % (LANES // 2)
    offset = jnp.where(lane_iota((LANES, LANES)) < snaps, 0, shift)
    relative = source - offset
    for k in range(count):
        spread = jnp.dot(
            terms, (relative == k).astype(jnp.bfloat16), preferred_element_type=jnp.float32
        )
        ce[k, low:high, :] = spread[: high - low]
        cs[k, low:high, :] = spread[high - low :]

    buffers = (u0, u1)
    first_row = lax.broadcasted_iota(jnp.int32, (8, LANES), 0) == 0
    for step in range(PASSES):
        src, dst = buffers[step % 2], buffers[(step + 1) % 2]
        final = step == PASSES - 1
        start, stop = step + 1, count - 1 - step
        blocks = range(own, east, 8) if final else range(low, high, 8)
        current = [src[start, r : r + 8, :] for r in blocks]
        above = [
            cs[start - 1, r : r + 8, :] * (c - src[start - 1, r : r + 8, :])
            for r, c in zip(blocks, current)
        ]

        def eastward(k, r, here):
            return ce[k, r : r + 8, :] * (src[k, r + 1 : r + 9, :] - here)

        for k in range(start, stop):
            before = None
            if final:
                before = pltpu.roll(eastward(k, low, src[k, low:own, :]), 1, 0)
            for i, r in enumerate(blocks):
                here = current[i]
                east_flux = eastward(k, r, here)
                turned = pltpu.roll(east_flux, 1, 0)
                west_flux = turned if before is None else jnp.where(first_row, before, turned)
                below = src[k + 1, r : r + 8, :]
                south_flux = cs[k, r : r + 8, :] * (below - here)
                dst[k, r : r + 8, :] = here + ((south_flux - above[i]) + (east_flux - west_flux))
                current[i], above[i], before = below, south_flux, turned
        if not final:

            @pl.when(lat == 0)
            def _():
                dst[PASSES - 1, low:high, :] = jnp.where(left, 0.0, dst[PASSES - 1, low:high, :])

            @pl.when(lat == lats - 1)
            def _():
                dst[PASSES + half, low:high, :] = jnp.where(left, dst[PASSES + half, low:high, :], 0.0)

    tall = -(-half // 8) * 8
    row = lax.broadcasted_iota(jnp.int32, (tall, LANES), 0) + jnp.where(lane_iota((tall, LANES)) < snaps, 0, shift)
    angle = ((row + lat * rows).astype(jnp.float32) + 0.5) * math.pi / (rows * lats) - math.pi / 2
    scale = jnp.sqrt(jnp.maximum(jnp.cos(angle), 0.0))
    for t in range(half):
        weighted = (dst[t + PASSES, own:east, :] * scale[t : t + 1]).astype(jnp.bfloat16)
        both = dot_t(unit, weighted).astype(jnp.bfloat16)
        y_ref[t] = both[:snaps]
        y_ref[t + shift] = both[snaps:]


def smooth(x, d, side, a, b):
    rows, snaps, width = x.shape
    count = -(-rows // 2) + 2 * PASSES
    field = VMEM((count, PADDED, LANES), jnp.float32)
    return kernel_call(
        smooth_body,
        jax.ShapeDtypeStruct((rows, snaps, width), jnp.bfloat16),
        [field] * 4 + [VMEM((width, LANES), jnp.float32), VMEM((PADDED, LANES), jnp.float32)],
    )(x, d, side, a, b)


def mm(a, b):
    return jnp.dot(a, b, precision=exact, preferred_element_type=jnp.float32)


def mmt(a, b):
    return lax.dot_general(
        a, b, (((1,), (1,)), ((), ())), precision=exact, preferred_element_type=jnp.float32
    )


def inverse_factors(grams, block=16):
    n = RANK
    row = lax.broadcasted_iota(jnp.int32, (n, LANES), 0)
    lane = lane_iota((n, LANES))
    diagonal = row == lane % n
    unit = diagonal.astype(jnp.float32)
    first = lane // n * n
    s = jnp.concatenate(list(grams) + [unit[:, :n]] * (LANES // n - len(grams)), axis=1)

    def pivots(m):
        return jnp.sum(jnp.where(diagonal, m, 0.0), axis=0, keepdims=True)

    least = jnp.max(pivots(s), axis=1, keepdims=True) * 1e-12 + 1e-37
    inv = unit
    done = []
    for k0 in range(0, n, block):
        tall = n - k0
        cols = [jnp.take_along_axis(s, (first + (k0 + j))[:tall], axis=1) for j in range(block)]
        for p in range(min(block, tall - 1)):
            inverse = 1.0 / jnp.maximum(cols[p][p : p + 1], least)
            below = jnp.where(row[:tall] > p, cols[p], 0.0)
            for j in range(p + 1, block):
                cols[j] = cols[j] - below * (cols[j][p : p + 1] * inverse)
            s = s - below * (s[p : p + 1] * inverse)
            inv = inv - below * (inv[p : p + 1] * inverse)
        done.append((s[:block], inv[:block]))
        s, inv = s[block:], inv[block:]
    s, inv = (jnp.concatenate(v, axis=0) for v in zip(*done))
    scale = lax.rsqrt(jnp.maximum(pivots(s), least))
    out = []
    for g in range(len(grams)):
        seg = slice(n * g, n * g + n)
        rows_scale = jnp.sum(jnp.where(diagonal[:, seg], scale[:, seg], 0.0), axis=1, keepdims=True)
        out.append(inv[:, seg] * rows_scale)
    return out


def power_bases(hs, upper_first):
    squares, starts = [], []
    for h in hs:
        n = h.shape[0]
        on = lax.broadcasted_iota(jnp.int32, (n, n), 0) == lane_iota((n, n))
        top = jnp.max(jnp.max(jnp.where(on, h, 0.0), axis=1, keepdims=True), axis=0, keepdims=True)
        unit = 1.0 / jnp.maximum(top, 1e-30)
        h2 = mm(h, h) * (unit * unit)
        squares.append(h2)
        starts.append(h2[:RANK] if upper_first is None else jnp.where(upper_first, h2[RANK:], h2[:RANK]))
    factors = inverse_factors([mmt(z, z) for z in starts])
    return [mm(mm(f, z), h2) for f, z, h2 in zip(factors, starts, squares)]


def top_rows(hs, upper_first=None):
    zs = power_bases(hs, upper_first)
    return [mm(f, z) for f, z in zip(inverse_factors([mmt(z, z) for z in zs]), zs)]


def diagonal_blocks(a, b):
    top = jnp.concatenate([a, jnp.zeros((a.shape[0], b.shape[1]), a.dtype)], axis=1)
    low = jnp.concatenate([jnp.zeros((b.shape[0], a.shape[1]), b.dtype), b], axis=1)
    return jnp.concatenate([top, low], axis=0)


def projection(gram, coef, upper_first, w=None):
    zt = power_bases([gram], upper_first)[0]
    on, out = mmt(coef, zt), zt if w is None else mm(zt, w)
    f = inverse_factors([mmt(mm(zt, gram), zt)])[0]
    return mm(mmt(on, f), mm(f, out))


def stack_of(*refs):
    return lambda i: jnp.concatenate([ref[i] for ref in refs], axis=0)


def gram_sum(left, right, rows):
    acc = None
    for i in range(0, rows, 2):
        at = range(i, min(i + 2, rows))
        part = dot_t(
            jnp.concatenate([left(r) for r in at], axis=1),
            jnp.concatenate([right(r) for r in at], axis=1),
        )
        acc = part if acc is None else acc + part
    return acc


def pair_gram_body(own_ref, other_ref, o_ref):
    n = own_ref.shape[1]
    both = stack_of(own_ref, other_ref)
    acc = gram_sum(both, both, own_ref.shape[0])
    cross = jnp.where(odd(0), pltpu.roll(acc[n + n // 2 :], n, 1), acc[: n // 2])[:, n:]
    tall = o_ref.shape[1]
    packed = jnp.concatenate(
        [acc[:tall, :n], jnp.concatenate([acc[tall:n, :n], cross], axis=0)], axis=1
    )
    for j in range(o_ref.shape[0]):
        o_ref[j] = packed


def pair_gram(g, gp, n):
    tall = g.shape[0]
    rest = n - tall
    block = lambda v: jnp.concatenate([v[:, :n], v[:rest, n:]], axis=0)
    mine, theirs = g[rest:, n:], gp[rest:, n:]
    upper = odd(0)
    cross = jnp.concatenate([jnp.where(upper, theirs, mine), jnp.where(upper, mine, theirs)], axis=0)
    flipped = cross.T
    return block(g), block(gp), jnp.where(upper, flipped, cross), jnp.where(upper, cross, flipped)


def put_rows(w, stacked, o_ref):
    for i in range(o_ref.shape[0]):
        o_ref[i] = jnp.dot(w, stacked(i), preferred_element_type=jnp.float32).astype(jnp.bfloat16)


def put_result(w, stacked, o_hbm, buffer, sems):
    rows = buffer.shape[0]
    parts = sems.shape[0]
    size = -(-rows // parts)
    copies = []
    for p in range(parts):
        lo, hi = p * size, min(rows, p * size + size)
        for i in range(lo, hi):
            buffer[i] = jnp.dot(w, stacked(i), preferred_element_type=jnp.float32).astype(jnp.bfloat16)
        at = pl.ds(lo, hi - lo)
        copies.append(pltpu.make_async_copy(buffer.at[at], o_hbm.at[at], sems.at[p]))
        copies[-1].start()
    for copy in copies:
        copy.wait()


def result_call(body, rows, snaps, width):
    parts = 5
    return kernel_call(
        body,
        jax.ShapeDtypeStruct((rows, snaps, width), jnp.bfloat16),
        [VMEM((rows, snaps, width), jnp.bfloat16), pltpu.SemaphoreType.DMA((parts,))],
        out_spec=pl.BlockSpec(memory_space=pl.ANY),
    )


def put_modes(w, stacked, modes_ref, part_ref):
    rows, half = modes_ref.shape[0], part_ref.shape[0]
    put_rows(w, stacked, modes_ref)
    start = jnp.where(odd(0), rows - half, 0)
    for i in range(half):
        part_ref[i] = modes_ref[start + i]


def halves(rows, here_ref, there_ref):
    half = here_ref.shape[0]
    upper = odd(0)

    def row(i):
        if i < half:
            return jnp.where(upper, there_ref[i], here_ref[i])
        j = i - (rows - half)
        return jnp.where(upper, here_ref[j], there_ref[j])

    return row


def far_gram_body(own_ref, other_ref, far_ref, o_ref):
    n = own_ref.shape[1]
    acc = gram_sum(stack_of(own_ref, other_ref), lambda i: far_ref[i], own_ref.shape[0])
    packed = jnp.concatenate([acc[:n], acc[n:]], axis=1)
    for j in range(o_ref.shape[0]):
        o_ref[j] = packed


def square(a, b, c, d):
    return jnp.concatenate(
        [jnp.concatenate([a, b], axis=1), jnp.concatenate([c, d], axis=1)], axis=0
    )


def pair_levels_body(g_ref, gp_ref, wh_ref, c_ref):
    n = c_ref.shape[0]
    own, other, cross, flipped = pair_gram(g_ref[...], gp_ref[...], n)
    gram = square(own, cross, flipped, other)
    basis = diagonal_blocks(*top_rows([own, other]))
    merged = mmt(mm(basis, gram), basis)
    q = top_rows([merged], odd(0))[0]
    h = mmt(mm(q, merged), q)
    w = mm(q, basis)
    c_ref[...] = mmt(gram[:n], w)
    wh_ref[...] = jnp.concatenate(
        [w, jnp.concatenate([h, jnp.zeros((RANK, LANES - RANK), jnp.float32)], axis=1)], axis=0
    )


def quad_level(wh_ref, c_ref, far_wh_ref, cs_ref, twin_ref):
    n = c_ref.shape[0]
    cs, twin = cs_ref[...], twin_ref[...]
    between = square(cs[:, :n], twin[:, n:], cs[:, n:], twin[:, :n])
    wa, wb = wh_ref[:RANK, :], far_wh_ref[:RANK, :]
    on_b = mmt(between, wb)
    mixed = mm(wa, on_b)
    gram = square(wh_ref[RANK:, :RANK], mixed, mixed.T, far_wh_ref[RANK:, :RANK])
    return diagonal_blocks(wa, wb), gram, jnp.concatenate([c_ref[...], on_b[:n]], axis=1)


def quad_project_body(wh, c, far_wh, cs, twin, yo, yp, yy, yz, o_hbm, buffer, sems):
    w, gram, coef = quad_level(wh, c, far_wh, cs, twin)
    weights = projection(gram, coef, odd(1), w).astype(jnp.bfloat16)
    put_result(weights, stack_of(yo, yp, yy, yz), o_hbm, buffer, sems)


def quad_modes_body(wh, c, far_wh, cs, twin, yo, yp, yy, yz, modes_ref, part_ref, h_ref, c_ref):
    w, gram, coef = quad_level(wh, c, far_wh, cs, twin)
    q = top_rows([gram], odd(1))[0]
    h_ref[...] = mmt(mm(q, gram), q)
    c_ref[...] = mmt(coef, q)
    put_modes(mm(q, w).astype(jnp.bfloat16), stack_of(yo, yp, yy, yz), modes_ref, part_ref)


def cross_body(here_ref, there_ref, y_ref, own_ref, o_ref):
    rows = y_ref.shape[0]
    other = halves(rows, here_ref, there_ref)
    acc = gram_sum(other, lambda i: jnp.concatenate([y_ref[i], own_ref[i], other(i)], axis=0), rows)
    for j in range(o_ref.shape[0]):
        o_ref[j] = acc


def merged_gram(p_ref, h_ref, c_ref, n):
    total = p_ref[0]
    for j in range(1, p_ref.shape[0]):
        total = total + p_ref[j]
    mixed = total[:, n : n + RANK]
    gram = jnp.concatenate(
        [
            jnp.concatenate([h_ref[...], mixed.T], axis=1),
            jnp.concatenate([mixed, total[:, n + RANK :]], axis=1),
        ],
        axis=0,
    )
    coef = jnp.concatenate([c_ref[...], total[:, :n].T], axis=1)
    return gram, coef


def merge_body(level, p_ref, h_ref, c_ref, own_ref, here_ref, there_ref, modes_ref, part_ref, hn_ref, cn_ref):
    gram, coef = merged_gram(p_ref, h_ref, c_ref, c_ref.shape[0])
    w = top_rows([gram], odd(level))[0].astype(jnp.bfloat16)
    wf = w.astype(jnp.float32)
    cn_ref[...] = mmt(coef, wf)
    hn_ref[...] = mmt(mm(wf, gram), wf)
    other = halves(own_ref.shape[0], here_ref, there_ref)
    put_modes(w, lambda i: jnp.concatenate([own_ref[i], other(i)], axis=0), modes_ref, part_ref)


def project_body(level, p_ref, h_ref, c_ref, own_ref, here_ref, there_ref, o_hbm, buffer, sems):
    gram, coef = merged_gram(p_ref, h_ref, c_ref, c_ref.shape[0])
    weights = projection(gram, coef, odd(level)).astype(jnp.bfloat16)
    other = halves(own_ref.shape[0], here_ref, there_ref)
    stacked = lambda i: jnp.concatenate([own_ref[i], other(i)], axis=0)
    put_result(weights, stacked, o_hbm, buffer, sems)


def exchanged(block, level):
    count = lax.axis_size("tm")
    return lax.ppermute(block, "tm", [(i, i ^ 1 << level) for i in range(count)])


def gathered(parts):
    return lax.all_to_all(parts, ("lat", "lon"), 0, 0, tiled=True)


def shards(residuals, diffusivity):
    snaps, rows, width = residuals.shape
    tiles = lax.axis_size("lat") * lax.axis_size("lon")
    levels = lax.axis_size("tm").bit_length() - 1
    f32 = lambda *shape: jax.ShapeDtypeStruct(shape, jnp.float32)
    b16 = lambda *shape: jax.ShapeDtypeStruct(shape, jnp.bfloat16)
    x = jnp.transpose(residuals, (1, 0, 2))
    y = smooth(x, diffusivity, *halo_exchange(x, diffusivity))
    other, far = exchanged(y, 0), exchanged(y, 1)
    pair = kernel_call(pair_gram_body, f32(tiles, snaps * 3 // 4, 2 * snaps))(y, other)
    pair = jnp.sum(gathered(pair), axis=0)
    pair_twin = exchanged(pair, 0)
    far, pair_twin = lax.optimization_barrier((far, pair_twin))
    cross = kernel_call(far_gram_body, f32(tiles, snaps, 2 * snaps))(y, other, far)
    cross = jnp.sum(gathered(cross), axis=0)
    wh, c = kernel_call(
        pair_levels_body, (f32(2 * RANK, 2 * snaps), f32(snaps, RANK)), flops=1 << 32
    )(pair, pair_twin)
    operands = (wh, c, exchanged(wh, 1), cross, exchanged(cross, 0))
    operands += (y, other, far, exchanged(far, 0))
    if levels == 2:
        out = result_call(quad_project_body, rows, snaps, width)(*operands)
        return jnp.transpose(out, (1, 0, 2))
    block = (
        b16(rows, RANK, width),
        b16(-(-rows // 2), RANK, width),
        f32(RANK, RANK),
        f32(snaps, RANK),
    )
    modes, part, h, c = kernel_call(quad_modes_body, block)(*operands)
    for level in range(2, levels):
        here = exchanged(part, level)
        there = exchanged(here, 0)
        parts = gathered(kernel_call(cross_body, f32(tiles, RANK, snaps + 2 * RANK))(here, there, y, modes))
        if level < levels - 1:
            modes, part, h, c = kernel_call(functools.partial(merge_body, level), block)(
                parts, h, c, modes, here, there
            )
    out = result_call(functools.partial(project_body, levels - 1), rows, snaps, width)(
        parts, h, c, modes, here, there
    )
    return jnp.transpose(out, (1, 0, 2))


def solution(mesh):
    return jax.shard_map(
        shards,
        mesh=mesh,
        in_specs=(P("tm", "lat", "lon"), P("lat", "lon")),
        out_specs=P("tm", "lat", "lon"),
        check_vma=False,
    )
```

```python
import functools
import math

import jax
import jax.numpy as jnp
from jax import lax
from jax.experimental import pallas as pl
from jax.experimental.pallas import tpu as pltpu
from jax.sharding import PartitionSpec as P

RANK = 32
PASSES = 4
LANES = 128
exact = lax.Precision.HIGHEST
VMEM = pltpu.VMEM


def whole():
    return pl.BlockSpec(memory_space=VMEM)


def kernel_call(body, outs, scratch=(), flops=1 << 20, specs=None, vmem=48 << 20, out_spec=None):
    return pl.pallas_call(
        body,
        out_shape=outs,
        **({} if specs is None else {"in_specs": specs}),
        out_specs=jax.tree.map(lambda _: out_spec or whole(), outs),
        scratch_shapes=list(scratch),
        compiler_params=pltpu.CompilerParams(vmem_limit_bytes=vmem),
        cost_estimate=pl.CostEstimate(flops=flops, bytes_accessed=1 << 20, transcendentals=0),
    )


def lane_iota(shape):
    return lax.broadcasted_iota(jnp.int32, shape, len(shape) - 1)


def roll(x, shift):
    return pltpu.roll(x, shift % LANES, x.ndim - 1)


def eye(n, dtype=jnp.bfloat16):
    row = lax.broadcasted_iota(jnp.int32, (n, n), 0)
    return (row == lax.broadcasted_iota(jnp.int32, (n, n), 1)).astype(dtype)


def dot_t(a, b):
    return lax.dot_general(a, b, (((1,), (1,)), ((), ())), preferred_element_type=jnp.float32)


def split2(v):
    high = v.astype(jnp.bfloat16)
    return high, (v - high.astype(jnp.float32)).astype(jnp.bfloat16)


def odd(level):
    return (lax.axis_index("tm") >> level & 1) == 1


def even_lat():
    return lax.axis_index("lat") % 2 == 0


def edge_body(x_hbm, d_hbm, a_ref, b_ref, d_ref, sems):
    rows, snaps, width = x_hbm.shape
    even = even_lat()
    flags = ((a_ref, even), (b_ref, jnp.logical_not(even)))
    copies = [pltpu.make_async_copy(d_hbm, d_ref, sems.at[0])]
    for ref, south in flags:
        start = jnp.where(south, rows - PASSES, 0)
        for r in range(PASSES):
            copies.append(
                pltpu.make_async_copy(
                    x_hbm.at[start + r], ref.at[pl.ds(r * snaps, snaps)], sems.at[len(copies)]
                )
            )
    for copy in copies:
        copy.start()
    copies[0].wait()
    pad = jnp.zeros((8, width), jnp.float32)
    edge = lambda lo: [v.astype(jnp.float32) for v in split2(d_ref[lo : lo + PASSES, :])]
    first, final = edge(0), edge(rows - PASSES)
    for ref, south in flags:
        term = [jnp.where(south, f, g) for f, g in zip(final, first)]
        ref[PASSES * snaps :, :] = jnp.concatenate(term + [pad], axis=0).astype(jnp.bfloat16)
    for copy in copies[1:]:
        copy.wait()


def by_side(a_ref, b_ref):
    even = even_lat()

    def picked(lo, hi):
        a, b = a_ref[lo:hi, :], b_ref[lo:hi, :]
        return jnp.where(even, b, a), jnp.where(even, a, b)

    return picked


def tile_rows(x_ref, north, south, t):
    rows, snaps, _ = x_ref.shape
    first = north[(t + PASSES) * snaps : (t + PASSES + 1) * snaps] if t < 0 else x_ref[t]
    r = t + rows // 2
    second = x_ref[r] if r < rows else south[(r - rows) * snaps : (r - rows + 1) * snaps]
    return jnp.concatenate([first, second], axis=0)


def extend_rows(dn, d_ref, north_d, south_d):
    rows = d_ref.shape[0]
    dn[...] = jnp.zeros(dn.shape, jnp.float32)
    dn[PASSES : PASSES + rows, :] = d_ref[...]
    dn[0:PASSES, :] = north_d[0:PASSES] + north_d[PASSES : 2 * PASSES]
    dn[PASSES + rows : 2 * PASSES + rows, :] = south_d[0:PASSES] + south_d[PASSES : 2 * PASSES]


def pack_body(x_ref, d_ref, b_ref, a_ref, m_ref, dn):
    rows, snaps, width = x_ref.shape
    half = -(-rows // 2)
    count = half + 2 * PASSES
    edge = PASSES * snaps
    row = lax.broadcasted_iota(jnp.int32, (16, width), 0)
    lane = lane_iota((16, width))
    column = jnp.where(row % 8 < PASSES, row % 8, width - 8 + row % 8)
    pick = [((lane == column) & (row // 8 == k)).astype(jnp.bfloat16) for k in range(2)]
    picked = by_side(a_ref, b_ref)
    north, south = picked(0, edge)
    north_d, south_d = (v.astype(jnp.float32) for v in picked(edge, edge + 16))
    for k in range(0, count, 2):
        out = dot_t(pick[0], tile_rows(x_ref, north, south, k - PASSES))
        if k + 1 < count:
            out = out + dot_t(pick[1], tile_rows(x_ref, north, south, k + 1 - PASSES))
        m_ref[8 * k : 8 * k + 16, :] = out.astype(jnp.bfloat16)
    extend_rows(dn, d_ref, north_d, south_d)
    high, low = split2(dn[...])
    end = m_ref.shape[0]
    m_ref[end - 16 :, :] = (dot_t(pick[0], high) + dot_t(pick[1], low)).astype(jnp.bfloat16)


def halo_exchange(x, d):
    rows, snaps, width = x.shape
    count = -(-rows // 2) + 2 * PASSES
    shape = lambda n: jax.ShapeDtypeStruct((n, width), jnp.bfloat16)
    edge = PASSES * snaps + 16
    hbm = pl.BlockSpec(memory_space=pltpu.HBM)
    a, b = kernel_call(
        edge_body,
        (shape(edge), shape(edge)),
        [VMEM(d.shape, d.dtype), pltpu.SemaphoreType.DMA((2 * PASSES + 1,))],
        specs=[hbm, hbm],
        vmem=60 << 20,
    )(x, d)
    lons, lats = lax.axis_size("lon"), lax.axis_size("lat")

    def swapped(message, start):
        pairs = [(i, i + 1) for i in range(start, lats - 1, 2)]
        return lax.ppermute(message, "lat", pairs + [(j, i) for i, j in pairs])

    a, b = swapped(a, 0), swapped(b, 1)
    packed = kernel_call(
        pack_body, shape(16 * (-(-count // 2)) + 16), [VMEM((width, LANES), jnp.float32)]
    )(x, d, b, a)
    forward = [(i, (i + 1) % lons) for i in range(lons)]
    side = lax.ppermute(packed, "lon", forward)
    if lons > 2:
        from_east = lax.ppermute(packed, "lon", [(j, i) for i, j in forward])
        side = jnp.where(lax.broadcasted_iota(jnp.int32, side.shape, 0) % 8 < PASSES, from_east, side)
    return side, a, b


OWN = 16
EDGE = 16
EDGES = 8 + 2 * EDGE + 8


def spread_faces(here, beside, k0, count, ce, cs, rows_at, snaps, shift):
    n = here.shape[0]
    lane = lane_iota((1, LANES))
    faces = jnp.concatenate([here + beside, here + roll(here, -1)], axis=0) * 0.5
    high, low = (v.astype(jnp.float32) for v in split2(faces))
    terms = jnp.where(lane < LANES // 2, high, roll(low, LANES // 2)).astype(jnp.bfloat16)
    source = lax.broadcasted_iota(jnp.int32, (LANES, LANES), 0) % (LANES // 2)
    relative = source - jnp.where(lane_iota((LANES, LANES)) < snaps, 0, shift)
    for k in range(count):
        pick = (relative == k0 + k).astype(jnp.bfloat16)
        spread = jnp.dot(terms, pick, preferred_element_type=jnp.float32)
        ce[k, rows_at, :] = spread[:n]
        cs[k, rows_at, :] = spread[n:]


def smoothing_passes(u0, u1, ce, cs, low, high, own_low, own_high, half, left):
    count = u0.shape[0]
    lats, lat = lax.axis_size("lat"), lax.axis_index("lat")
    buffers = (u0, u1)
    first_row = lax.broadcasted_iota(jnp.int32, (8, LANES), 0) == 0
    for step in range(PASSES):
        src, dst = buffers[step % 2], buffers[(step + 1) % 2]
        final = step == PASSES - 1
        start, stop = step + 1, count - 1 - step
        blocks = range(own_low, own_high, 8) if final else range(low, high, 8)
        current = [src[start, r : r + 8, :] for r in blocks]
        above = [
            cs[start - 1, r : r + 8, :] * (c - src[start - 1, r : r + 8, :])
            for r, c in zip(blocks, current)
        ]

        def eastward(k, r, here):
            return ce[k, r : r + 8, :] * (src[k, r + 1 : r + 9, :] - here)

        for k in range(start, stop):
            before = None
            if blocks[0] > low:
                r = blocks[0] - 8
                before = pltpu.roll(eastward(k, r, src[k, r : r + 8, :]), 1, 0)
            for i, r in enumerate(blocks):
                here = current[i]
                east_flux = eastward(k, r, here)
                turned = pltpu.roll(east_flux, 1, 0)
                west_flux = turned if before is None else jnp.where(first_row, before, turned)
                below = src[k + 1, r : r + 8, :]
                south_flux = cs[k, r : r + 8, :] * (below - here)
                dst[k, r : r + 8, :] = here + ((south_flux - above[i]) + (east_flux - west_flux))
                current[i], above[i], before = below, south_flux, turned
        if not final:
            north, beyond, at = PASSES - 1, PASSES + half, slice(low, high)

            @pl.when(lat == 0)
            def _():
                dst[north, at, :] = jnp.where(left, 0.0, dst[north, at, :])

            @pl.when(lat == lats - 1)
            def _():
                dst[beyond, at, :] = jnp.where(left, dst[beyond, at, :], 0.0)

    return buffers[PASSES % 2]


def area_scale(rows, snaps):
    half = -(-rows // 2)
    shape = (-(-half // 8) * 8, LANES)
    lats, lat = lax.axis_size("lat"), lax.axis_index("lat")
    row = lax.broadcasted_iota(jnp.int32, shape, 0) + jnp.where(lane_iota(shape) < snaps, 0, rows - half)
    angle = ((row + lat * rows).astype(jnp.float32) + 0.5) * math.pi / (rows * lats) - math.pi / 2
    return jnp.sqrt(jnp.maximum(jnp.cos(angle), 0.0))


def interior_body(x_ref, d_ref, b_ref, a_ref, y_ref, ends_ref, dt_ref, u0, u1, ce, cs, dn):
    rows, snaps, width = x_ref.shape
    half = -(-rows // 2)
    shift = rows - half
    count = half + 2 * PASSES
    lane = lane_iota((1, LANES))
    east = OWN + width
    unit = eye(width)
    edge = PASSES * snaps
    picked = by_side(a_ref, b_ref)
    north, south = picked(0, edge)
    north_d, south_d = (v.astype(jnp.float32) for v in picked(edge, edge + 16))
    outside = jnp.zeros((8, LANES), jnp.float32)
    for k in range(count):
        tile = dot_t(unit, tile_rows(x_ref, north, south, k - PASSES))
        u0[k, OWN:east, :] = tile
        ends_ref[k, :EDGE, :] = tile[:EDGE]
        ends_ref[k, EDGE:, :] = tile[width - EDGE :]
        u0[k, east : east + 8, :] = outside
        u1[k, east : east + 8, :] = outside
    extend_rows(dn, d_ref, north_d, south_d)
    dt = dn[...].T
    dt_ref[:EDGE, :] = dt[:EDGE]
    dt_ref[EDGE:, :] = dt[width - EDGE :]
    beside = jnp.concatenate([dt[1:], jnp.zeros((1, LANES), jnp.float32)], axis=0)
    spread_faces(dt, beside, 0, count, ce, cs, slice(OWN, east), snaps, shift)
    done = smoothing_passes(u0, u1, ce, cs, OWN, east, OWN, east, half, lane < snaps)
    scale = area_scale(rows, snaps)
    for t in range(half):
        weighted = (done[t + PASSES, OWN:east, :] * scale[t : t + 1]).astype(jnp.bfloat16)
        both = dot_t(unit, weighted).astype(jnp.bfloat16)
        y_ref[t] = both[:snaps]
        y_ref[t + shift] = both[snaps:]


def ends_body(y_in, ends_ref, dt_ref, side_ref, y_ref, u0, u1, ce, cs):
    rows, snaps, width = y_in.shape
    half = -(-rows // 2)
    shift = rows - half
    count = half + 2 * PASSES
    lane = lane_iota((1, LANES))
    low, high = 8, 8 + EDGES
    inner = high - 8
    for k in range(count):
        pair = side_ref[16 * (k // 2) : 16 * (k // 2) + 16, :].astype(jnp.float32)
        halo = pair[8 * (k % 2) : 8 * (k % 2) + 8]
        u0[k, low : low + 8, :] = halo
        u0[k, low + 8 : inner, :] = ends_ref[k]
        u0[k, inner:high, :] = halo
    side_d = side_ref[side_ref.shape[0] - 16 :, :].astype(jnp.float32)
    halo = side_d[0:8] + side_d[8:16]
    here = jnp.concatenate([halo, dt_ref[...], halo], axis=0)
    beside = jnp.concatenate([here[1:], jnp.zeros((1, LANES), jnp.float32)], axis=0)
    spread_faces(here, beside, 0, count, ce, cs, slice(low, high), snaps, shift)
    outside = jnp.zeros((8, LANES), jnp.float32)
    for buffer in (u0, u1):
        for k in range(count):
            buffer[k, high : high + 8, :] = outside
    done = smoothing_passes(u0, u1, ce, cs, low, high, low + 8, inner, half, lane < snaps)
    scale = area_scale(rows, snaps)
    unit = eye(width)
    middle = jnp.zeros((width - 16, LANES), jnp.float32)
    ends = (lane < PASSES) | (lane >= width - PASSES)
    for t in range(half):
        west = done[t + PASSES, low + 8 : low + 16, :]
        east = done[t + PASSES, inner - 8 : inner, :]
        weighted = (jnp.concatenate([west, middle, east], axis=0) * scale[t : t + 1]).astype(jnp.bfloat16)
        both = dot_t(unit, weighted)
        for r, part in ((t, both[:snaps]), (t + shift, both[snaps:])):
            y_ref[r] = jnp.where(ends, part, y_in[r].astype(jnp.float32)).astype(jnp.bfloat16)


def smooth(x, d, side, a, b):
    rows, snaps, width = x.shape
    count = -(-rows // 2) + 2 * PASSES
    f32 = lambda *shape: jax.ShapeDtypeStruct(shape, jnp.float32)
    field = lambda n: VMEM((count, n, LANES), jnp.float32)
    out = jax.ShapeDtypeStruct(x.shape, jnp.bfloat16)
    y, ends, dt = kernel_call(
        interior_body,
        (out, f32(count, 2 * EDGE, LANES), f32(2 * EDGE, LANES)),
        [field(OWN + width + 16)] * 4 + [VMEM((width, LANES), jnp.float32)],
        flops=1 << 32,
    )(x, d, b, a)
    return kernel_call(ends_body, out, [field(EDGES + 16)] * 4)(y, ends, dt, side)


def mm(a, b):
    return jnp.dot(a, b, precision=exact, preferred_element_type=jnp.float32)


def mmt(a, b):
    return lax.dot_general(
        a, b, (((1,), (1,)), ((), ())), precision=exact, preferred_element_type=jnp.float32
    )


def inverse_factors(grams, block=16):
    n = RANK
    row = lax.broadcasted_iota(jnp.int32, (n, LANES), 0)
    lane = lane_iota((n, LANES))
    diagonal = row == lane % n
    unit = diagonal.astype(jnp.float32)
    first = lane // n * n
    s = jnp.concatenate(list(grams) + [unit[:, :n]] * (LANES // n - len(grams)), axis=1)

    def pivots(m):
        return jnp.sum(jnp.where(diagonal, m, 0.0), axis=0, keepdims=True)

    least = jnp.max(pivots(s), axis=1, keepdims=True) * 1e-12 + 1e-37
    inv = unit
    done = []
    for k0 in range(0, n, block):
        tall = n - k0
        cols = [jnp.take_along_axis(s, (first + (k0 + j))[:tall], axis=1) for j in range(block)]
        for p in range(min(block, tall - 1)):
            inverse = 1.0 / jnp.maximum(cols[p][p : p + 1], least)
            below = jnp.where(row[:tall] > p, cols[p], 0.0)
            for j in range(p + 1, block):
                cols[j] = cols[j] - below * (cols[j][p : p + 1] * inverse)
            s = s - below * (s[p : p + 1] * inverse)
            inv = inv - below * (inv[p : p + 1] * inverse)
        done.append((s[:block], inv[:block]))
        s, inv = s[block:], inv[block:]
    s, inv = (jnp.concatenate(v, axis=0) for v in zip(*done))
    scale = lax.rsqrt(jnp.maximum(pivots(s), least))
    out = []
    for g in range(len(grams)):
        seg = slice(n * g, n * g + n)
        rows_scale = jnp.sum(jnp.where(diagonal[:, seg], scale[:, seg], 0.0), axis=1, keepdims=True)
        out.append(inv[:, seg] * rows_scale)
    return out


def power_bases(hs, upper_first):
    squares, starts = [], []
    for h in hs:
        n = h.shape[0]
        on = lax.broadcasted_iota(jnp.int32, (n, n), 0) == lane_iota((n, n))
        top = jnp.max(jnp.max(jnp.where(on, h, 0.0), axis=1, keepdims=True), axis=0, keepdims=True)
        unit = 1.0 / jnp.maximum(top, 1e-30)
        h2 = mm(h, h) * (unit * unit)
        squares.append(h2)
        starts.append(h2[:RANK] if upper_first is None else jnp.where(upper_first, h2[RANK:], h2[:RANK]))
    factors = inverse_factors([mmt(z, z) for z in starts])
    return [mm(mm(f, z), h2) for f, z, h2 in zip(factors, starts, squares)]


def top_rows(hs, upper_first=None):
    zs = power_bases(hs, upper_first)
    return [mm(f, z) for f, z in zip(inverse_factors([mmt(z, z) for z in zs]), zs)]


def diagonal_blocks(a, b):
    top = jnp.concatenate([a, jnp.zeros((a.shape[0], b.shape[1]), a.dtype)], axis=1)
    low = jnp.concatenate([jnp.zeros((b.shape[0], a.shape[1]), b.dtype), b], axis=1)
    return jnp.concatenate([top, low], axis=0)


def projection(gram, coef, upper_first, w=None):
    zt = power_bases([gram], upper_first)[0]
    on, out = mmt(coef, zt), zt if w is None else mm(zt, w)
    f = inverse_factors([mmt(mm(zt, gram), zt)])[0]
    return mm(mmt(on, f), mm(f, out))


def stack_of(*refs):
    return lambda i: jnp.concatenate([ref[i] for ref in refs], axis=0)


def gram_sum(left, right, rows):
    acc = None
    for i in range(0, rows, 2):
        at = range(i, min(i + 2, rows))
        part = dot_t(
            jnp.concatenate([left(r) for r in at], axis=1),
            jnp.concatenate([right(r) for r in at], axis=1),
        )
        acc = part if acc is None else acc + part
    return acc


def pair_gram_body(own_ref, other_ref, o_ref):
    n = own_ref.shape[1]
    both = stack_of(own_ref, other_ref)
    acc = gram_sum(both, both, own_ref.shape[0])
    cross = jnp.where(odd(0), pltpu.roll(acc[n + n // 2 :], n, 1), acc[: n // 2])[:, n:]
    tall = o_ref.shape[1]
    packed = jnp.concatenate(
        [acc[:tall, :n], jnp.concatenate([acc[tall:n, :n], cross], axis=0)], axis=1
    )
    for j in range(o_ref.shape[0]):
        o_ref[j] = packed


def pair_gram(g, gp, n):
    tall = g.shape[0]
    rest = n - tall
    block = lambda v: jnp.concatenate([v[:, :n], v[:rest, n:]], axis=0)
    mine, theirs = g[rest:, n:], gp[rest:, n:]
    upper = odd(0)
    cross = jnp.concatenate([jnp.where(upper, theirs, mine), jnp.where(upper, mine, theirs)], axis=0)
    flipped = cross.T
    return block(g), block(gp), jnp.where(upper, flipped, cross), jnp.where(upper, cross, flipped)


def put_rows(w, stacked, o_ref):
    for i in range(o_ref.shape[0]):
        o_ref[i] = jnp.dot(w, stacked(i), preferred_element_type=jnp.float32).astype(jnp.bfloat16)


def put_result(w, stacked, o_hbm, buffer, sems):
    rows = buffer.shape[0]
    parts = sems.shape[0]
    size = -(-rows // parts)
    copies = []
    for p in range(parts):
        lo, hi = p * size, min(rows, p * size + size)
        for i in range(lo, hi):
            buffer[i] = jnp.dot(w, stacked(i), preferred_element_type=jnp.float32).astype(jnp.bfloat16)
        at = pl.ds(lo, hi - lo)
        copies.append(pltpu.make_async_copy(buffer.at[at], o_hbm.at[at], sems.at[p]))
        copies[-1].start()
    for copy in copies:
        copy.wait()


def result_call(body, rows, snaps, width):
    parts = 5
    return kernel_call(
        body,
        jax.ShapeDtypeStruct((rows, snaps, width), jnp.bfloat16),
        [VMEM((rows, snaps, width), jnp.bfloat16), pltpu.SemaphoreType.DMA((parts,))],
        out_spec=pl.BlockSpec(memory_space=pl.ANY),
    )


def put_modes(w, stacked, modes_ref, part_ref):
    rows, half = modes_ref.shape[0], part_ref.shape[0]
    put_rows(w, stacked, modes_ref)
    start = jnp.where(odd(0), rows - half, 0)
    for i in range(half):
        part_ref[i] = modes_ref[start + i]


def halves(rows, here_ref, there_ref):
    half = here_ref.shape[0]
    upper = odd(0)

    def row(i):
        if i < half:
            return jnp.where(upper, there_ref[i], here_ref[i])
        j = i - (rows - half)
        return jnp.where(upper, here_ref[j], there_ref[j])

    return row


def far_gram_body(own_ref, other_ref, far_ref, o_ref):
    n = own_ref.shape[1]
    acc = gram_sum(stack_of(own_ref, other_ref), lambda i: far_ref[i], own_ref.shape[0])
    packed = jnp.concatenate([acc[:n], acc[n:]], axis=1)
    for j in range(o_ref.shape[0]):
        o_ref[j] = packed


def square(a, b, c, d):
    return jnp.concatenate(
        [jnp.concatenate([a, b], axis=1), jnp.concatenate([c, d], axis=1)], axis=0
    )


def pair_levels_body(g_ref, gp_ref, wh_ref, c_ref):
    n = c_ref.shape[0]
    own, other, cross, flipped = pair_gram(g_ref[...], gp_ref[...], n)
    gram = square(own, cross, flipped, other)
    basis = diagonal_blocks(*top_rows([own, other]))
    merged = mmt(mm(basis, gram), basis)
    q = top_rows([merged], odd(0))[0]
    h = mmt(mm(q, merged), q)
    w = mm(q, basis)
    c_ref[...] = mmt(gram[:n], w)
    wh_ref[...] = jnp.concatenate(
        [w, jnp.concatenate([h, jnp.zeros((RANK, LANES - RANK), jnp.float32)], axis=1)], axis=0
    )


def quad_level(wh_ref, c_ref, far_wh_ref, cs_ref, twin_ref):
    n = c_ref.shape[0]
    cs, twin = cs_ref[...], twin_ref[...]
    between = square(cs[:, :n], twin[:, n:], cs[:, n:], twin[:, :n])
    wa, wb = wh_ref[:RANK, :], far_wh_ref[:RANK, :]
    on_b = mmt(between, wb)
    mixed = mm(wa, on_b)
    gram = square(wh_ref[RANK:, :RANK], mixed, mixed.T, far_wh_ref[RANK:, :RANK])
    return diagonal_blocks(wa, wb), gram, jnp.concatenate([c_ref[...], on_b[:n]], axis=1)


def quad_project_body(wh, c, far_wh, cs, twin, yo, yp, yy, yz, o_hbm, buffer, sems):
    w, gram, coef = quad_level(wh, c, far_wh, cs, twin)
    weights = projection(gram, coef, odd(1), w).astype(jnp.bfloat16)
    put_result(weights, stack_of(yo, yp, yy, yz), o_hbm, buffer, sems)


def quad_modes_body(wh, c, far_wh, cs, twin, yo, yp, yy, yz, modes_ref, part_ref, h_ref, c_ref):
    w, gram, coef = quad_level(wh, c, far_wh, cs, twin)
    q = top_rows([gram], odd(1))[0]
    h_ref[...] = mmt(mm(q, gram), q)
    c_ref[...] = mmt(coef, q)
    put_modes(mm(q, w).astype(jnp.bfloat16), stack_of(yo, yp, yy, yz), modes_ref, part_ref)


def cross_body(here_ref, there_ref, y_ref, own_ref, o_ref):
    rows = y_ref.shape[0]
    other = halves(rows, here_ref, there_ref)
    acc = gram_sum(other, lambda i: jnp.concatenate([y_ref[i], own_ref[i], other(i)], axis=0), rows)
    for j in range(o_ref.shape[0]):
        o_ref[j] = acc


def merged_gram(p_ref, h_ref, c_ref, n):
    total = p_ref[0]
    for j in range(1, p_ref.shape[0]):
        total = total + p_ref[j]
    mixed = total[:, n : n + RANK]
    gram = jnp.concatenate(
        [
            jnp.concatenate([h_ref[...], mixed.T], axis=1),
            jnp.concatenate([mixed, total[:, n + RANK :]], axis=1),
        ],
        axis=0,
    )
    coef = jnp.concatenate([c_ref[...], total[:, :n].T], axis=1)
    return gram, coef


def merge_body(level, p_ref, h_ref, c_ref, own_ref, here_ref, there_ref, modes_ref, part_ref, hn_ref, cn_ref):
    gram, coef = merged_gram(p_ref, h_ref, c_ref, c_ref.shape[0])
    w = top_rows([gram], odd(level))[0].astype(jnp.bfloat16)
    wf = w.astype(jnp.float32)
    cn_ref[...] = mmt(coef, wf)
    hn_ref[...] = mmt(mm(wf, gram), wf)
    other = halves(own_ref.shape[0], here_ref, there_ref)
    put_modes(w, lambda i: jnp.concatenate([own_ref[i], other(i)], axis=0), modes_ref, part_ref)


def project_body(level, p_ref, h_ref, c_ref, own_ref, here_ref, there_ref, o_hbm, buffer, sems):
    gram, coef = merged_gram(p_ref, h_ref, c_ref, c_ref.shape[0])
    weights = projection(gram, coef, odd(level)).astype(jnp.bfloat16)
    other = halves(own_ref.shape[0], here_ref, there_ref)
    stacked = lambda i: jnp.concatenate([own_ref[i], other(i)], axis=0)
    put_result(weights, stacked, o_hbm, buffer, sems)


def exchanged(block, level):
    count = lax.axis_size("tm")
    return lax.ppermute(block, "tm", [(i, i ^ 1 << level) for i in range(count)])


def gathered(parts):
    return lax.all_to_all(parts, ("lat", "lon"), 0, 0, tiled=True)


def shards(residuals, diffusivity):
    snaps, rows, width = residuals.shape
    tiles = lax.axis_size("lat") * lax.axis_size("lon")
    levels = lax.axis_size("tm").bit_length() - 1
    f32 = lambda *shape: jax.ShapeDtypeStruct(shape, jnp.float32)
    b16 = lambda *shape: jax.ShapeDtypeStruct(shape, jnp.bfloat16)
    x = jnp.transpose(residuals, (1, 0, 2))
    y = smooth(x, diffusivity, *halo_exchange(x, diffusivity))
    other, far = exchanged(y, 0), exchanged(y, 1)
    pair = kernel_call(pair_gram_body, f32(tiles, snaps * 3 // 4, 2 * snaps))(y, other)
    pair = jnp.sum(gathered(pair), axis=0)
    pair_twin = exchanged(pair, 0)
    far, pair_twin = lax.optimization_barrier((far, pair_twin))
    cross = kernel_call(far_gram_body, f32(tiles, snaps, 2 * snaps))(y, other, far)
    cross = jnp.sum(gathered(cross), axis=0)
    wh, c = kernel_call(
        pair_levels_body, (f32(2 * RANK, 2 * snaps), f32(snaps, RANK)), flops=1 << 32
    )(pair, pair_twin)
    operands = (wh, c, exchanged(wh, 1), cross, exchanged(cross, 0))
    operands += (y, other, far, exchanged(far, 0))
    if levels == 2:
        out = result_call(quad_project_body, rows, snaps, width)(*operands)
        return jnp.transpose(out, (1, 0, 2))
    block = (
        b16(rows, RANK, width),
        b16(-(-rows // 2), RANK, width),
        f32(RANK, RANK),
        f32(snaps, RANK),
    )
    modes, part, h, c = kernel_call(quad_modes_body, block)(*operands)
    for level in range(2, levels):
        here = exchanged(part, level)
        there = exchanged(here, 0)
        parts = gathered(kernel_call(cross_body, f32(tiles, RANK, snaps + 2 * RANK))(here, there, y, modes))
        if level < levels - 1:
            modes, part, h, c = kernel_call(functools.partial(merge_body, level), block)(
                parts, h, c, modes, here, there
            )
    out = result_call(functools.partial(project_body, levels - 1), rows, snaps, width)(
        parts, h, c, modes, here, there
    )
    return jnp.transpose(out, (1, 0, 2))


def solution(mesh):
    return jax.shard_map(
        shards,
        mesh=mesh,
        in_specs=(P("tm", "lat", "lon"), P("lat", "lon")),
        out_specs=P("tm", "lat", "lon"),
        check_vma=False,
    )
```

```python
import functools
import math

import jax
import jax.numpy as jnp
from jax import lax
from jax.experimental import pallas as pl
from jax.experimental.pallas import tpu as pltpu
from jax.sharding import PartitionSpec as P

RANK = 32
PASSES = 4
LANES = 128
exact = lax.Precision.HIGHEST
VMEM = pltpu.VMEM


def whole():
    return pl.BlockSpec(memory_space=VMEM)


def kernel_call(body, outs, scratch=(), flops=1 << 20, specs=None, vmem=48 << 20, out_spec=None):
    return pl.pallas_call(
        body,
        out_shape=outs,
        **({} if specs is None else {"in_specs": specs}),
        out_specs=jax.tree.map(lambda _: out_spec or whole(), outs),
        scratch_shapes=list(scratch),
        compiler_params=pltpu.CompilerParams(vmem_limit_bytes=vmem),
        cost_estimate=pl.CostEstimate(flops=flops, bytes_accessed=1 << 20, transcendentals=0),
    )


def lane_iota(shape):
    return lax.broadcasted_iota(jnp.int32, shape, len(shape) - 1)


def roll(x, shift):
    return pltpu.roll(x, shift % LANES, x.ndim - 1)


def eye(n, dtype=jnp.bfloat16):
    row = lax.broadcasted_iota(jnp.int32, (n, n), 0)
    return (row == lax.broadcasted_iota(jnp.int32, (n, n), 1)).astype(dtype)


def dot_t(a, b):
    return lax.dot_general(a, b, (((1,), (1,)), ((), ())), preferred_element_type=jnp.float32)


def split2(v):
    high = v.astype(jnp.bfloat16)
    return high, (v - high.astype(jnp.float32)).astype(jnp.bfloat16)


def odd(level):
    return (lax.axis_index("tm") >> level & 1) == 1


def even_lat():
    return lax.axis_index("lat") % 2 == 0


def edge_body(x_hbm, d_hbm, a_ref, b_ref, d_ref, sems):
    rows, snaps, width = x_hbm.shape
    even = even_lat()
    flags = ((a_ref, even), (b_ref, jnp.logical_not(even)))
    copies = [pltpu.make_async_copy(d_hbm, d_ref, sems.at[0])]
    for ref, south in flags:
        start = jnp.where(south, rows - PASSES, 0)
        for r in range(PASSES):
            copies.append(
                pltpu.make_async_copy(
                    x_hbm.at[start + r], ref.at[pl.ds(r * snaps, snaps)], sems.at[len(copies)]
                )
            )
    for copy in copies:
        copy.start()
    copies[0].wait()
    pad = jnp.zeros((8, width), jnp.float32)
    edge = lambda lo: [v.astype(jnp.float32) for v in split2(d_ref[lo : lo + PASSES, :])]
    first, final = edge(0), edge(rows - PASSES)
    for ref, south in flags:
        term = [jnp.where(south, f, g) for f, g in zip(final, first)]
        ref[PASSES * snaps :, :] = jnp.concatenate(term + [pad], axis=0).astype(jnp.bfloat16)
    for copy in copies[1:]:
        copy.wait()


def by_side(a_ref, b_ref):
    even = even_lat()

    def picked(lo, hi):
        a, b = a_ref[lo:hi, :], b_ref[lo:hi, :]
        return jnp.where(even, b, a), jnp.where(even, a, b)

    return picked


def tile_rows(x_ref, north, south, t):
    rows, snaps, _ = x_ref.shape
    first = north[(t + PASSES) * snaps : (t + PASSES + 1) * snaps] if t < 0 else x_ref[t]
    r = t + rows // 2
    second = x_ref[r] if r < rows else south[(r - rows) * snaps : (r - rows + 1) * snaps]
    return jnp.concatenate([first, second], axis=0)


def extend_rows(dn, d_ref, north_d, south_d):
    rows = d_ref.shape[0]
    dn[...] = jnp.zeros(dn.shape, jnp.float32)
    dn[PASSES : PASSES + rows, :] = d_ref[...]
    dn[0:PASSES, :] = north_d[0:PASSES] + north_d[PASSES : 2 * PASSES]
    dn[PASSES + rows : 2 * PASSES + rows, :] = south_d[0:PASSES] + south_d[PASSES : 2 * PASSES]


def edge_picks(width):
    row = lax.broadcasted_iota(jnp.int32, (16, width), 0)
    lane = lane_iota((16, width))
    column = jnp.where(row % 8 < PASSES, row % 8, width - 8 + row % 8)
    return [((lane == column) & (row // 8 == k)).astype(jnp.bfloat16) for k in range(2)]


def own_body(x_ref, m_ref, tiles_ref):
    rows, snaps, width = x_ref.shape
    half = tiles_ref.shape[0]
    pick, unit = edge_picks(width), eye(width)
    for t in range(half):
        tiles_ref[t] = dot_t(unit, tile_rows(x_ref, None, None, t))
    for t in range(0, half - 1, 2):
        first, second = (tile_rows(x_ref, None, None, t + j) for j in range(2))
        m_ref[8 * t : 8 * t + 16, :] = (dot_t(pick[0], first) + dot_t(pick[1], second)).astype(jnp.bfloat16)


def pack_body(x_ref, d_ref, b_ref, a_ref, own_ref, m_ref, dn):
    rows, snaps, width = x_ref.shape
    half = -(-rows // 2)
    count = half + 2 * PASSES
    edge = PASSES * snaps
    pick = edge_picks(width)
    picked = by_side(a_ref, b_ref)
    north, south = picked(0, edge)
    north_d, south_d = (v.astype(jnp.float32) for v in picked(edge, edge + 16))
    begin, end = 8 * PASSES, 8 * PASSES + own_ref.shape[0]
    m_ref[begin:end, :] = own_ref[...]
    for k in range(0, count, 2):
        if begin <= 8 * k < end:
            continue
        out = dot_t(pick[0], tile_rows(x_ref, north, south, k - PASSES))
        if k + 1 < count:
            out = out + dot_t(pick[1], tile_rows(x_ref, north, south, k + 1 - PASSES))
        m_ref[8 * k : 8 * k + 16, :] = out.astype(jnp.bfloat16)
    extend_rows(dn, d_ref, north_d, south_d)
    high, low = split2(dn[...])
    end = m_ref.shape[0]
    m_ref[end - 16 :, :] = (dot_t(pick[0], high) + dot_t(pick[1], low)).astype(jnp.bfloat16)


def halo_exchange(x, d):
    rows, snaps, width = x.shape
    count = -(-rows // 2) + 2 * PASSES
    shape = lambda n: jax.ShapeDtypeStruct((n, width), jnp.bfloat16)
    edge = PASSES * snaps + 16
    hbm = pl.BlockSpec(memory_space=pltpu.HBM)
    a, b = kernel_call(
        edge_body,
        (shape(edge), shape(edge)),
        [VMEM(d.shape, d.dtype), pltpu.SemaphoreType.DMA((2 * PASSES + 1,))],
        specs=[hbm, hbm],
        vmem=60 << 20,
    )(x, d)
    lons, lats = lax.axis_size("lon"), lax.axis_size("lat")

    def swapped(message, start):
        pairs = [(i, i + 1) for i in range(start, lats - 1, 2)]
        return lax.ppermute(message, "lat", pairs + [(j, i) for i, j in pairs])

    a, b = swapped(a, 0), swapped(b, 1)
    half = -(-rows // 2)
    own, tiles = kernel_call(
        own_body, (shape(16 * (half // 2)), jax.ShapeDtypeStruct((half, width, 2 * snaps), jnp.float32))
    )(x)
    packed = kernel_call(
        pack_body, shape(16 * (-(-count // 2)) + 16), [VMEM((width, LANES), jnp.float32)]
    )(x, d, b, a, own)
    forward = [(i, (i + 1) % lons) for i in range(lons)]
    side = lax.ppermute(packed, "lon", forward)
    if lons > 2:
        from_east = lax.ppermute(packed, "lon", [(j, i) for i, j in forward])
        side = jnp.where(lax.broadcasted_iota(jnp.int32, side.shape, 0) % 8 < PASSES, from_east, side)
    return side, a, b, tiles


OWN = 16
EDGE = 8
EDGES = 8 + 2 * EDGE + 8


def spread_faces(here, beside, k0, count, ce, cs, rows_at, snaps, shift):
    n = here.shape[0]
    lane = lane_iota((1, LANES))
    faces = jnp.concatenate([here + beside, here + roll(here, -1)], axis=0) * 0.5
    high, low = (v.astype(jnp.float32) for v in split2(faces))
    terms = jnp.where(lane < LANES // 2, high, roll(low, LANES // 2)).astype(jnp.bfloat16)
    source = lax.broadcasted_iota(jnp.int32, (LANES, LANES), 0) % (LANES // 2)
    relative = source - jnp.where(lane_iota((LANES, LANES)) < snaps, 0, shift)
    for k in range(count):
        pick = (relative == k0 + k).astype(jnp.bfloat16)
        spread = jnp.dot(terms, pick, preferred_element_type=jnp.float32)
        ce[k, rows_at, :] = spread[:n]
        cs[k, rows_at, :] = spread[n:]


def smoothing_passes(u0, u1, ce, cs, low, high, own_low, own_high, half, left):
    count = u0.shape[0]
    lats, lat = lax.axis_size("lat"), lax.axis_index("lat")
    buffers = (u0, u1)
    first_row = lax.broadcasted_iota(jnp.int32, (8, LANES), 0) == 0
    for step in range(PASSES):
        src, dst = buffers[step % 2], buffers[(step + 1) % 2]
        final = step == PASSES - 1
        start, stop = step + 1, count - 1 - step
        blocks = range(own_low, own_high, 8) if final else range(low, high, 8)
        current = [src[start, r : r + 8, :] for r in blocks]
        above = [
            cs[start - 1, r : r + 8, :] * (c - src[start - 1, r : r + 8, :])
            for r, c in zip(blocks, current)
        ]

        def eastward(k, r, here):
            return ce[k, r : r + 8, :] * (src[k, r + 1 : r + 9, :] - here)

        for k in range(start, stop):
            before = None
            if blocks[0] > low:
                r = blocks[0] - 8
                before = pltpu.roll(eastward(k, r, src[k, r : r + 8, :]), 1, 0)
            for i, r in enumerate(blocks):
                here = current[i]
                east_flux = eastward(k, r, here)
                turned = pltpu.roll(east_flux, 1, 0)
                west_flux = turned if before is None else jnp.where(first_row, before, turned)
                below = src[k + 1, r : r + 8, :]
                south_flux = cs[k, r : r + 8, :] * (below - here)
                dst[k, r : r + 8, :] = here + ((south_flux - above[i]) + (east_flux - west_flux))
                current[i], above[i], before = below, south_flux, turned
        if not final:
            north, beyond, at = PASSES - 1, PASSES + half, slice(low, high)

            @pl.when(lat == 0)
            def _():
                dst[north, at, :] = jnp.where(left, 0.0, dst[north, at, :])

            @pl.when(lat == lats - 1)
            def _():
                dst[beyond, at, :] = jnp.where(left, dst[beyond, at, :], 0.0)

    return buffers[PASSES % 2]


def area_scale(rows, snaps):
    half = -(-rows // 2)
    shape = (-(-half // 8) * 8, LANES)
    lats, lat = lax.axis_size("lat"), lax.axis_index("lat")
    row = lax.broadcasted_iota(jnp.int32, shape, 0) + jnp.where(lane_iota(shape) < snaps, 0, rows - half)
    angle = ((row + lat * rows).astype(jnp.float32) + 0.5) * math.pi / (rows * lats) - math.pi / 2
    return jnp.sqrt(jnp.maximum(jnp.cos(angle), 0.0))


def interior_body(x_ref, d_ref, b_ref, a_ref, tiles_ref, y_ref, ends_ref, dt_ref, u0, u1, ce, cs, dn):
    rows, snaps, width = x_ref.shape
    half = -(-rows // 2)
    shift = rows - half
    count = half + 2 * PASSES
    lane = lane_iota((1, LANES))
    east = OWN + width
    unit = eye(width)
    edge = PASSES * snaps
    picked = by_side(a_ref, b_ref)
    north, south = picked(0, edge)
    north_d, south_d = (v.astype(jnp.float32) for v in picked(edge, edge + 16))
    outside = jnp.zeros((8, LANES), jnp.float32)
    for k in range(count):
        t = k - PASSES
        if 0 <= t < half:
            tile = tiles_ref[t]
        else:
            tile = dot_t(unit, tile_rows(x_ref, north, south, t))
        u0[k, OWN:east, :] = tile
        ends_ref[k, :EDGE, :] = tile[:EDGE]
        ends_ref[k, EDGE:, :] = tile[width - EDGE :]
        u0[k, east : east + 8, :] = outside
        u1[k, east : east + 8, :] = outside
    extend_rows(dn, d_ref, north_d, south_d)
    dt = dn[...].T
    dt_ref[:EDGE, :] = dt[:EDGE]
    dt_ref[EDGE:, :] = dt[width - EDGE :]
    beside = jnp.concatenate([dt[1:], jnp.zeros((1, LANES), jnp.float32)], axis=0)
    spread_faces(dt, beside, 0, count, ce, cs, slice(OWN, east), snaps, shift)
    done = smoothing_passes(u0, u1, ce, cs, OWN, east, OWN, east, half, lane < snaps)
    scale = area_scale(rows, snaps)
    for t in range(half):
        weighted = (done[t + PASSES, OWN:east, :] * scale[t : t + 1]).astype(jnp.bfloat16)
        both = dot_t(unit, weighted).astype(jnp.bfloat16)
        y_ref[t] = both[:snaps]
        y_ref[t + shift] = both[snaps:]


def ends_body(y_in, ends_ref, dt_ref, side_ref, y_ref, u0, u1, ce, cs):
    rows, snaps, width = y_in.shape
    half = -(-rows // 2)
    shift = rows - half
    count = half + 2 * PASSES
    lane = lane_iota((1, LANES))
    low, high = 8, 8 + EDGES
    inner = high - 8
    for k in range(count):
        pair = side_ref[16 * (k // 2) : 16 * (k // 2) + 16, :].astype(jnp.float32)
        halo = pair[8 * (k % 2) : 8 * (k % 2) + 8]
        u0[k, low : low + 8, :] = halo
        u0[k, low + 8 : inner, :] = ends_ref[k]
        u0[k, inner:high, :] = halo
    side_d = side_ref[side_ref.shape[0] - 16 :, :].astype(jnp.float32)
    halo = side_d[0:8] + side_d[8:16]
    here = jnp.concatenate([halo, dt_ref[...], halo], axis=0)
    beside = jnp.concatenate([here[1:], jnp.zeros((1, LANES), jnp.float32)], axis=0)
    spread_faces(here, beside, 0, count, ce, cs, slice(low, high), snaps, shift)
    outside = jnp.zeros((8, LANES), jnp.float32)
    for buffer in (u0, u1):
        for k in range(count):
            buffer[k, high : high + 8, :] = outside
    done = smoothing_passes(u0, u1, ce, cs, low, high, low + 8, inner, half, lane < snaps)
    scale = area_scale(rows, snaps)
    unit = eye(width)
    middle = jnp.zeros((width - 16, LANES), jnp.float32)
    ends = (lane < PASSES) | (lane >= width - PASSES)
    for t in range(half):
        west = done[t + PASSES, low + 8 : low + 16, :]
        east = done[t + PASSES, inner - 8 : inner, :]
        weighted = (jnp.concatenate([west, middle, east], axis=0) * scale[t : t + 1]).astype(jnp.bfloat16)
        both = dot_t(unit, weighted)
        for r, part in ((t, both[:snaps]), (t + shift, both[snaps:])):
            y_ref[r] = jnp.where(ends, part, y_in[r].astype(jnp.float32)).astype(jnp.bfloat16)


def smooth(x, d, side, a, b, tiles):
    rows, snaps, width = x.shape
    count = -(-rows // 2) + 2 * PASSES
    f32 = lambda *shape: jax.ShapeDtypeStruct(shape, jnp.float32)
    field = lambda n: VMEM((count, n, LANES), jnp.float32)
    out = jax.ShapeDtypeStruct(x.shape, jnp.bfloat16)
    y, ends, dt = kernel_call(
        interior_body,
        (out, f32(count, 2 * EDGE, LANES), f32(2 * EDGE, LANES)),
        [field(OWN + width + 16)] * 4 + [VMEM((width, LANES), jnp.float32)],
        flops=1 << 32,
    )(x, d, b, a, tiles)
    return kernel_call(ends_body, out, [field(EDGES + 16)] * 4)(y, ends, dt, side)


def mm(a, b):
    return jnp.dot(a, b, precision=exact, preferred_element_type=jnp.float32)


def mmt(a, b):
    return lax.dot_general(
        a, b, (((1,), (1,)), ((), ())), precision=exact, preferred_element_type=jnp.float32
    )


def inverse_factors(grams, block=16):
    n = RANK
    row = lax.broadcasted_iota(jnp.int32, (n, LANES), 0)
    lane = lane_iota((n, LANES))
    diagonal = row == lane % n
    unit = diagonal.astype(jnp.float32)
    first = lane // n * n
    s = jnp.concatenate(list(grams) + [unit[:, :n]] * (LANES // n - len(grams)), axis=1)

    def pivots(m):
        return jnp.sum(jnp.where(diagonal, m, 0.0), axis=0, keepdims=True)

    least = jnp.max(pivots(s), axis=1, keepdims=True) * 1e-12 + 1e-37
    inv = unit
    done = []
    for k0 in range(0, n, block):
        tall = n - k0
        cols = [jnp.take_along_axis(s, (first + (k0 + j))[:tall], axis=1) for j in range(block)]
        for p in range(min(block, tall - 1)):
            inverse = 1.0 / jnp.maximum(cols[p][p : p + 1], least)
            below = jnp.where(row[:tall] > p, cols[p], 0.0)
            for j in range(p + 1, block):
                cols[j] = cols[j] - below * (cols[j][p : p + 1] * inverse)
            s = s - below * (s[p : p + 1] * inverse)
            inv = inv - below * (inv[p : p + 1] * inverse)
        done.append((s[:block], inv[:block]))
        s, inv = s[block:], inv[block:]
    s, inv = (jnp.concatenate(v, axis=0) for v in zip(*done))
    scale = lax.rsqrt(jnp.maximum(pivots(s), least))
    out = []
    for g in range(len(grams)):
        seg = slice(n * g, n * g + n)
        rows_scale = jnp.sum(jnp.where(diagonal[:, seg], scale[:, seg], 0.0), axis=1, keepdims=True)
        out.append(inv[:, seg] * rows_scale)
    return out


def power_bases(hs, upper_first):
    squares, starts = [], []
    for h in hs:
        n = h.shape[0]
        on = lax.broadcasted_iota(jnp.int32, (n, n), 0) == lane_iota((n, n))
        top = jnp.max(jnp.max(jnp.where(on, h, 0.0), axis=1, keepdims=True), axis=0, keepdims=True)
        unit = 1.0 / jnp.maximum(top, 1e-30)
        h2 = mm(h, h) * (unit * unit)
        squares.append(h2)
        starts.append(h2[:RANK] if upper_first is None else jnp.where(upper_first, h2[RANK:], h2[:RANK]))
    factors = inverse_factors([mmt(z, z) for z in starts])
    return [mm(mm(f, z), h2) for f, z, h2 in zip(factors, starts, squares)]


def top_rows(hs, upper_first=None):
    zs = power_bases(hs, upper_first)
    return [mm(f, z) for f, z in zip(inverse_factors([mmt(z, z) for z in zs]), zs)]


def diagonal_blocks(a, b):
    top = jnp.concatenate([a, jnp.zeros((a.shape[0], b.shape[1]), a.dtype)], axis=1)
    low = jnp.concatenate([jnp.zeros((b.shape[0], a.shape[1]), b.dtype), b], axis=1)
    return jnp.concatenate([top, low], axis=0)


def projection(gram, coef, upper_first, w=None):
    zt = power_bases([gram], upper_first)[0]
    on, out = mmt(coef, zt), zt if w is None else mm(zt, w)
    f = inverse_factors([mmt(mm(zt, gram), zt)])[0]
    return mm(mmt(on, f), mm(f, out))


def stack_of(*refs):
    return lambda i: jnp.concatenate([ref[i] for ref in refs], axis=0)


def gram_sum(left, right, rows):
    acc = None
    for i in range(0, rows, 2):
        at = range(i, min(i + 2, rows))
        part = dot_t(
            jnp.concatenate([left(r) for r in at], axis=1),
            jnp.concatenate([right(r) for r in at], axis=1),
        )
        acc = part if acc is None else acc + part
    return acc


def pair_gram_body(own_ref, other_ref, o_ref):
    n = own_ref.shape[1]
    both = stack_of(own_ref, other_ref)
    acc = gram_sum(both, both, own_ref.shape[0])
    cross = jnp.where(odd(0), pltpu.roll(acc[n + n // 2 :], n, 1), acc[: n // 2])[:, n:]
    tall = o_ref.shape[1]
    packed = jnp.concatenate(
        [acc[:tall, :n], jnp.concatenate([acc[tall:n, :n], cross], axis=0)], axis=1
    )
    for j in range(o_ref.shape[0]):
        o_ref[j] = packed


def pair_gram(g, gp, n):
    tall = g.shape[0]
    rest = n - tall
    block = lambda v: jnp.concatenate([v[:, :n], v[:rest, n:]], axis=0)
    mine, theirs = g[rest:, n:], gp[rest:, n:]
    upper = odd(0)
    cross = jnp.concatenate([jnp.where(upper, theirs, mine), jnp.where(upper, mine, theirs)], axis=0)
    flipped = cross.T
    return block(g), block(gp), jnp.where(upper, flipped, cross), jnp.where(upper, cross, flipped)


def put_rows(w, stacked, o_ref):
    for i in range(o_ref.shape[0]):
        o_ref[i] = jnp.dot(w, stacked(i), preferred_element_type=jnp.float32).astype(jnp.bfloat16)


def put_result(w, stacked, o_hbm, buffer, sems):
    rows = buffer.shape[0]
    parts = sems.shape[0]
    size = -(-rows // parts)
    copies = []
    for p in range(parts):
        lo, hi = p * size, min(rows, p * size + size)
        for i in range(lo, hi):
            buffer[i] = jnp.dot(w, stacked(i), preferred_element_type=jnp.float32).astype(jnp.bfloat16)
        at = pl.ds(lo, hi - lo)
        copies.append(pltpu.make_async_copy(buffer.at[at], o_hbm.at[at], sems.at[p]))
        copies[-1].start()
    for copy in copies:
        copy.wait()


def result_call(body, rows, snaps, width):
    parts = 5
    return kernel_call(
        body,
        jax.ShapeDtypeStruct((rows, snaps, width), jnp.bfloat16),
        [VMEM((rows, snaps, width), jnp.bfloat16), pltpu.SemaphoreType.DMA((parts,))],
        out_spec=pl.BlockSpec(memory_space=pl.ANY),
    )


def put_modes(w, stacked, modes_ref, part_ref):
    rows, half = modes_ref.shape[0], part_ref.shape[0]
    put_rows(w, stacked, modes_ref)
    start = jnp.where(odd(0), rows - half, 0)
    for i in range(half):
        part_ref[i] = modes_ref[start + i]


def halves(rows, here_ref, there_ref):
    half = here_ref.shape[0]
    upper = odd(0)

    def row(i):
        if i < half:
            return jnp.where(upper, there_ref[i], here_ref[i])
        j = i - (rows - half)
        return jnp.where(upper, here_ref[j], there_ref[j])

    return row


def far_gram_body(own_ref, other_ref, far_ref, o_ref):
    n = own_ref.shape[1]
    acc = gram_sum(stack_of(own_ref, other_ref), lambda i: far_ref[i], own_ref.shape[0])
    packed = jnp.concatenate([acc[:n], acc[n:]], axis=1)
    for j in range(o_ref.shape[0]):
        o_ref[j] = packed


def square(a, b, c, d):
    return jnp.concatenate(
        [jnp.concatenate([a, b], axis=1), jnp.concatenate([c, d], axis=1)], axis=0
    )


def pair_levels_body(g_ref, gp_ref, wh_ref, c_ref):
    n = c_ref.shape[0]
    own, other, cross, flipped = pair_gram(g_ref[...], gp_ref[...], n)
    gram = square(own, cross, flipped, other)
    basis = diagonal_blocks(*top_rows([own, other]))
    merged = mmt(mm(basis, gram), basis)
    q = top_rows([merged], odd(0))[0]
    h = mmt(mm(q, merged), q)
    w = mm(q, basis)
    c_ref[...] = mmt(gram[:n], w)
    wh_ref[...] = jnp.concatenate(
        [w, jnp.concatenate([h, jnp.zeros((RANK, LANES - RANK), jnp.float32)], axis=1)], axis=0
    )


def quad_level(wh_ref, c_ref, far_wh_ref, cs_ref, twin_ref):
    n = c_ref.shape[0]
    cs, twin = cs_ref[...], twin_ref[...]
    between = square(cs[:, :n], twin[:, n:], cs[:, n:], twin[:, :n])
    wa, wb = wh_ref[:RANK, :], far_wh_ref[:RANK, :]
    on_b = mmt(between, wb)
    mixed = mm(wa, on_b)
    gram = square(wh_ref[RANK:, :RANK], mixed, mixed.T, far_wh_ref[RANK:, :RANK])
    return diagonal_blocks(wa, wb), gram, jnp.concatenate([c_ref[...], on_b[:n]], axis=1)


def quad_project_body(wh, c, far_wh, cs, twin, yo, yp, yy, yz, o_hbm, buffer, sems):
    w, gram, coef = quad_level(wh, c, far_wh, cs, twin)
    weights = projection(gram, coef, odd(1), w).astype(jnp.bfloat16)
    put_result(weights, stack_of(yo, yp, yy, yz), o_hbm, buffer, sems)


def quad_modes_body(wh, c, far_wh, cs, twin, yo, yp, yy, yz, modes_ref, part_ref, h_ref, c_ref):
    w, gram, coef = quad_level(wh, c, far_wh, cs, twin)
    q = top_rows([gram], odd(1))[0]
    h_ref[...] = mmt(mm(q, gram), q)
    c_ref[...] = mmt(coef, q)
    put_modes(mm(q, w).astype(jnp.bfloat16), stack_of(yo, yp, yy, yz), modes_ref, part_ref)


def cross_body(here_ref, there_ref, y_ref, own_ref, o_ref):
    rows = y_ref.shape[0]
    other = halves(rows, here_ref, there_ref)
    acc = gram_sum(other, lambda i: jnp.concatenate([y_ref[i], own_ref[i], other(i)], axis=0), rows)
    for j in range(o_ref.shape[0]):
        o_ref[j] = acc


def merged_gram(p_ref, h_ref, c_ref, n):
    total = p_ref[0]
    for j in range(1, p_ref.shape[0]):
        total = total + p_ref[j]
    mixed = total[:, n : n + RANK]
    gram = jnp.concatenate(
        [
            jnp.concatenate([h_ref[...], mixed.T], axis=1),
            jnp.concatenate([mixed, total[:, n + RANK :]], axis=1),
        ],
        axis=0,
    )
    coef = jnp.concatenate([c_ref[...], total[:, :n].T], axis=1)
    return gram, coef


def merge_body(level, p_ref, h_ref, c_ref, own_ref, here_ref, there_ref, modes_ref, part_ref, hn_ref, cn_ref):
    gram, coef = merged_gram(p_ref, h_ref, c_ref, c_ref.shape[0])
    w = top_rows([gram], odd(level))[0].astype(jnp.bfloat16)
    wf = w.astype(jnp.float32)
    cn_ref[...] = mmt(coef, wf)
    hn_ref[...] = mmt(mm(wf, gram), wf)
    other = halves(own_ref.shape[0], here_ref, there_ref)
    put_modes(w, lambda i: jnp.concatenate([own_ref[i], other(i)], axis=0), modes_ref, part_ref)


def project_body(level, p_ref, h_ref, c_ref, own_ref, here_ref, there_ref, o_hbm, buffer, sems):
    gram, coef = merged_gram(p_ref, h_ref, c_ref, c_ref.shape[0])
    weights = projection(gram, coef, odd(level)).astype(jnp.bfloat16)
    other = halves(own_ref.shape[0], here_ref, there_ref)
    stacked = lambda i: jnp.concatenate([own_ref[i], other(i)], axis=0)
    put_result(weights, stacked, o_hbm, buffer, sems)


def exchanged(block, level):
    count = lax.axis_size("tm")
    return lax.ppermute(block, "tm", [(i, i ^ 1 << level) for i in range(count)])


def gathered(parts):
    return lax.all_to_all(parts, ("lat", "lon"), 0, 0, tiled=True)


def shards(residuals, diffusivity):
    snaps, rows, width = residuals.shape
    tiles = lax.axis_size("lat") * lax.axis_size("lon")
    levels = lax.axis_size("tm").bit_length() - 1
    f32 = lambda *shape: jax.ShapeDtypeStruct(shape, jnp.float32)
    b16 = lambda *shape: jax.ShapeDtypeStruct(shape, jnp.bfloat16)
    x = jnp.transpose(residuals, (1, 0, 2))
    y = smooth(x, diffusivity, *halo_exchange(x, diffusivity))
    other, far = exchanged(y, 0), exchanged(y, 1)
    pair = kernel_call(pair_gram_body, f32(tiles, snaps * 3 // 4, 2 * snaps))(y, other)
    pair = jnp.sum(gathered(pair), axis=0)
    pair_twin = exchanged(pair, 0)
    far, pair_twin = lax.optimization_barrier((far, pair_twin))
    cross = kernel_call(far_gram_body, f32(tiles, snaps, 2 * snaps))(y, other, far)
    cross = jnp.sum(gathered(cross), axis=0)
    wh, c = kernel_call(
        pair_levels_body, (f32(2 * RANK, 2 * snaps), f32(snaps, RANK)), flops=1 << 32
    )(pair, pair_twin)
    operands = (wh, c, exchanged(wh, 1), cross, exchanged(cross, 0))
    operands += (y, other, far, exchanged(far, 0))
    if levels == 2:
        out = result_call(quad_project_body, rows, snaps, width)(*operands)
        return jnp.transpose(out, (1, 0, 2))
    block = (
        b16(rows, RANK, width),
        b16(-(-rows // 2), RANK, width),
        f32(RANK, RANK),
        f32(snaps, RANK),
    )
    modes, part, h, c = kernel_call(quad_modes_body, block)(*operands)
    for level in range(2, levels):
        here = exchanged(part, level)
        there = exchanged(here, 0)
        parts = gathered(kernel_call(cross_body, f32(tiles, RANK, snaps + 2 * RANK))(here, there, y, modes))
        if level < levels - 1:
            modes, part, h, c = kernel_call(functools.partial(merge_body, level), block)(
                parts, h, c, modes, here, there
            )
    out = result_call(functools.partial(project_body, levels - 1), rows, snaps, width)(
        parts, h, c, modes, here, there
    )
    return jnp.transpose(out, (1, 0, 2))


def solution(mesh):
    return jax.shard_map(
        shards,
        mesh=mesh,
        in_specs=(P("tm", "lat", "lon"), P("lat", "lon")),
        out_specs=P("tm", "lat", "lon"),
        check_vma=False,
    )
```

```python
import functools
import math

import jax
import jax.numpy as jnp
import numpy as np
from jax import lax
from jax.experimental import pallas as pl
from jax.experimental.pallas import tpu as pltpu
from jax.sharding import PartitionSpec as P

RANK = 32
PASSES = 4
LANES = 128
exact = lax.Precision.HIGHEST
VMEM = pltpu.VMEM


def whole():
    return pl.BlockSpec(memory_space=VMEM)


def kernel_call(body, outs, scratch=(), flops=1 << 20, specs=None, vmem=48 << 20, out_spec=None):
    return pl.pallas_call(
        body,
        out_shape=outs,
        **({} if specs is None else {"in_specs": specs}),
        out_specs=jax.tree.map(lambda _: out_spec or whole(), outs),
        scratch_shapes=list(scratch),
        compiler_params=pltpu.CompilerParams(vmem_limit_bytes=vmem),
        cost_estimate=pl.CostEstimate(flops=flops, bytes_accessed=1 << 20, transcendentals=0),
    )


def lane_iota(shape):
    return lax.broadcasted_iota(jnp.int32, shape, len(shape) - 1)


def roll(x, shift):
    return pltpu.roll(x, shift % LANES, x.ndim - 1)


def eye(n, dtype=jnp.bfloat16):
    row = lax.broadcasted_iota(jnp.int32, (n, n), 0)
    return (row == lax.broadcasted_iota(jnp.int32, (n, n), 1)).astype(dtype)


def dot_t(a, b):
    return lax.dot_general(a, b, (((1,), (1,)), ((), ())), preferred_element_type=jnp.float32)


def split2(v):
    high = v.astype(jnp.bfloat16)
    return high, (v - high.astype(jnp.float32)).astype(jnp.bfloat16)


def odd(level):
    return (lax.axis_index("tm") >> level & 1) == 1


def even_lat():
    return lax.axis_index("lat") % 2 == 0


def edge_body(x_hbm, d_hbm, a_ref, b_ref, d_ref, sems):
    rows, snaps, width = x_hbm.shape
    even = even_lat()
    flags = ((a_ref, even), (b_ref, jnp.logical_not(even)))
    copies = [pltpu.make_async_copy(d_hbm, d_ref, sems.at[0])]
    for ref, south in flags:
        start = jnp.where(south, rows - PASSES, 0)
        for r in range(PASSES):
            copies.append(
                pltpu.make_async_copy(
                    x_hbm.at[start + r], ref.at[pl.ds(r * snaps, snaps)], sems.at[len(copies)]
                )
            )
    for copy in copies:
        copy.start()
    copies[0].wait()
    pad = jnp.zeros((8, width), jnp.float32)
    edge = lambda lo: [v.astype(jnp.float32) for v in split2(d_ref[lo : lo + PASSES, :])]
    first, final = edge(0), edge(rows - PASSES)
    for ref, south in flags:
        term = [jnp.where(south, f, g) for f, g in zip(final, first)]
        ref[PASSES * snaps :, :] = jnp.concatenate(term + [pad], axis=0).astype(jnp.bfloat16)
    for copy in copies[1:]:
        copy.wait()


def by_side(a_ref, b_ref):
    even = even_lat()

    def picked(lo, hi):
        a, b = a_ref[lo:hi, :], b_ref[lo:hi, :]
        return jnp.where(even, b, a), jnp.where(even, a, b)

    return picked


def tile_rows(x_ref, north, south, t):
    rows, snaps, _ = x_ref.shape
    first = north[(t + PASSES) * snaps : (t + PASSES + 1) * snaps] if t < 0 else x_ref[t]
    r = t + rows // 2
    second = x_ref[r] if r < rows else south[(r - rows) * snaps : (r - rows + 1) * snaps]
    return jnp.concatenate([first, second], axis=0)


def extend_rows(dn, d_ref, north_d, south_d):
    rows = d_ref.shape[0]
    dn[...] = jnp.zeros(dn.shape, jnp.float32)
    dn[PASSES : PASSES + rows, :] = d_ref[...]
    dn[0:PASSES, :] = north_d[0:PASSES] + north_d[PASSES : 2 * PASSES]
    dn[PASSES + rows : 2 * PASSES + rows, :] = south_d[0:PASSES] + south_d[PASSES : 2 * PASSES]


def edge_picks(width):
    row = lax.broadcasted_iota(jnp.int32, (16, width), 0)
    lane = lane_iota((16, width))
    column = jnp.where(row % 8 < PASSES, row % 8, width - 8 + row % 8)
    return [((lane == column) & (row // 8 == k)).astype(jnp.bfloat16) for k in range(2)]


def own_body(x_ref, m_ref, tiles_ref):
    rows, snaps, width = x_ref.shape
    half = tiles_ref.shape[0]
    pick, unit = edge_picks(width), eye(width)
    for t in range(half):
        tiles_ref[t] = dot_t(unit, tile_rows(x_ref, None, None, t))
    for t in range(0, half - 1, 2):
        first, second = (tile_rows(x_ref, None, None, t + j) for j in range(2))
        m_ref[8 * t : 8 * t + 16, :] = (dot_t(pick[0], first) + dot_t(pick[1], second)).astype(jnp.bfloat16)


def pack_body(x_ref, d_ref, b_ref, a_ref, own_ref, m_ref, dn):
    rows, snaps, width = x_ref.shape
    half = -(-rows // 2)
    count = half + 2 * PASSES
    edge = PASSES * snaps
    pick = edge_picks(width)
    picked = by_side(a_ref, b_ref)
    north, south = picked(0, edge)
    north_d, south_d = (v.astype(jnp.float32) for v in picked(edge, edge + 16))
    begin, end = 8 * PASSES, 8 * PASSES + own_ref.shape[0]
    m_ref[begin:end, :] = own_ref[...]
    for k in range(0, count, 2):
        if begin <= 8 * k < end:
            continue
        out = dot_t(pick[0], tile_rows(x_ref, north, south, k - PASSES))
        if k + 1 < count:
            out = out + dot_t(pick[1], tile_rows(x_ref, north, south, k + 1 - PASSES))
        m_ref[8 * k : 8 * k + 16, :] = out.astype(jnp.bfloat16)
    extend_rows(dn, d_ref, north_d, south_d)
    high, low = split2(dn[...])
    end = m_ref.shape[0]
    m_ref[end - 16 :, :] = (dot_t(pick[0], high) + dot_t(pick[1], low)).astype(jnp.bfloat16)


def halo_exchange(x, d):
    rows, snaps, width = x.shape
    count = -(-rows // 2) + 2 * PASSES
    shape = lambda n: jax.ShapeDtypeStruct((n, width), jnp.bfloat16)
    edge = PASSES * snaps + 16
    hbm = pl.BlockSpec(memory_space=pltpu.HBM)
    a, b = kernel_call(
        edge_body,
        (shape(edge), shape(edge)),
        [VMEM(d.shape, d.dtype), pltpu.SemaphoreType.DMA((2 * PASSES + 1,))],
        specs=[hbm, hbm],
        vmem=60 << 20,
    )(x, d)
    lons, lats = lax.axis_size("lon"), lax.axis_size("lat")

    def swapped(message, start):
        pairs = [(i, i + 1) for i in range(start, lats - 1, 2)]
        return lax.ppermute(message, "lat", pairs + [(j, i) for i, j in pairs])

    a, b = swapped(a, 0), swapped(b, 1)
    half = -(-rows // 2)
    own, tiles = kernel_call(
        own_body, (shape(16 * (half // 2)), jax.ShapeDtypeStruct((half, width, 2 * snaps), jnp.float32))
    )(x)
    packed = kernel_call(
        pack_body, shape(16 * (-(-count // 2)) + 16), [VMEM((width, LANES), jnp.float32)]
    )(x, d, b, a, own)
    forward = [(i, (i + 1) % lons) for i in range(lons)]
    side = lax.ppermute(packed, "lon", forward)
    if lons > 2:
        from_east = lax.ppermute(packed, "lon", [(j, i) for i, j in forward])
        side = jnp.where(lax.broadcasted_iota(jnp.int32, side.shape, 0) % 8 < PASSES, from_east, side)
    return side, a, b, tiles


OWN = 16
EDGE = 8
EDGES = 8 + 2 * EDGE + 8


def spread_faces(here, beside, select_ref, ce, cs, rows_at):
    n = here.shape[0]
    lane = lane_iota((1, LANES))
    faces = jnp.concatenate([here + beside, here + roll(here, -1)], axis=0) * 0.5
    high, low = (v.astype(jnp.float32) for v in split2(faces))
    terms = jnp.where(lane < LANES // 2, high, roll(low, LANES // 2)).astype(jnp.bfloat16)
    for k in range(select_ref.shape[0]):
        spread = jnp.dot(terms, select_ref[k], preferred_element_type=jnp.float32)
        ce[k, rows_at, :] = spread[:n]
        cs[k, rows_at, :] = spread[n:]


def smoothing_passes(u0, u1, ce, cs, low, high, own_low, own_high, half, left):
    count = u0.shape[0]
    lats, lat = lax.axis_size("lat"), lax.axis_index("lat")
    buffers = (u0, u1)
    first_row = lax.broadcasted_iota(jnp.int32, (8, LANES), 0) == 0
    for step in range(PASSES):
        src, dst = buffers[step % 2], buffers[(step + 1) % 2]
        final = step == PASSES - 1
        start, stop = step + 1, count - 1 - step
        blocks = range(own_low, own_high, 8) if final else range(low, high, 8)
        current = [src[start, r : r + 8, :] for r in blocks]
        above = [
            cs[start - 1, r : r + 8, :] * (c - src[start - 1, r : r + 8, :])
            for r, c in zip(blocks, current)
        ]

        def eastward(k, r, here):
            return ce[k, r : r + 8, :] * (src[k, r + 1 : r + 9, :] - here)

        for k in range(start, stop):
            before = None
            if blocks[0] > low:
                r = blocks[0] - 8
                before = pltpu.roll(eastward(k, r, src[k, r : r + 8, :]), 1, 0)
            for i, r in enumerate(blocks):
                here = current[i]
                east_flux = eastward(k, r, here)
                turned = pltpu.roll(east_flux, 1, 0)
                west_flux = turned if before is None else jnp.where(first_row, before, turned)
                below = src[k + 1, r : r + 8, :]
                south_flux = cs[k, r : r + 8, :] * (below - here)
                dst[k, r : r + 8, :] = here + ((south_flux - above[i]) + (east_flux - west_flux))
                current[i], above[i], before = below, south_flux, turned
        if not final:
            north, beyond, at = PASSES - 1, PASSES + half, slice(low, high)

            @pl.when(lat == 0)
            def _():
                dst[north, at, :] = jnp.where(left, 0.0, dst[north, at, :])

            @pl.when(lat == lats - 1)
            def _():
                dst[beyond, at, :] = jnp.where(left, dst[beyond, at, :], 0.0)

    return buffers[PASSES % 2]


def area_scale(rows, snaps):
    half = -(-rows // 2)
    shape = (-(-half // 8) * 8, LANES)
    lats, lat = lax.axis_size("lat"), lax.axis_index("lat")
    row = lax.broadcasted_iota(jnp.int32, shape, 0) + jnp.where(lane_iota(shape) < snaps, 0, rows - half)
    angle = ((row + lat * rows).astype(jnp.float32) + 0.5) * math.pi / (rows * lats) - math.pi / 2
    return jnp.sqrt(jnp.maximum(jnp.cos(angle), 0.0))


def interior_body(x_ref, d_ref, b_ref, a_ref, tiles_ref, select_ref, y_ref, ends_ref, dt_ref, scale_ref, u0, u1, ce, cs, dn):
    rows, snaps, width = x_ref.shape
    half = -(-rows // 2)
    shift = rows - half
    count = half + 2 * PASSES
    lane = lane_iota((1, LANES))
    east = OWN + width
    unit = eye(width)
    edge = PASSES * snaps
    picked = by_side(a_ref, b_ref)
    north, south = picked(0, edge)
    north_d, south_d = (v.astype(jnp.float32) for v in picked(edge, edge + 16))
    outside = jnp.zeros((8, LANES), jnp.float32)
    for k in range(count):
        t = k - PASSES
        if 0 <= t < half:
            tile = tiles_ref[t]
        else:
            tile = dot_t(unit, tile_rows(x_ref, north, south, t))
        u0[k, OWN:east, :] = tile
        ends_ref[k, :EDGE, :] = tile[:EDGE]
        ends_ref[k, EDGE:, :] = tile[width - EDGE :]
        u0[k, east : east + 8, :] = outside
        u1[k, east : east + 8, :] = outside
    extend_rows(dn, d_ref, north_d, south_d)
    dt = dn[...].T
    dt_ref[:EDGE, :] = dt[:EDGE]
    dt_ref[EDGE:, :] = dt[width - EDGE :]
    beside = jnp.concatenate([dt[1:], jnp.zeros((1, LANES), jnp.float32)], axis=0)
    spread_faces(dt, beside, select_ref, ce, cs, slice(OWN, east))
    done = smoothing_passes(u0, u1, ce, cs, OWN, east, OWN, east, half, lane < snaps)
    scale = area_scale(rows, snaps)
    scale_ref[...] = scale
    for t in range(half):
        weighted = (done[t + PASSES, OWN:east, :] * scale[t : t + 1]).astype(jnp.bfloat16)
        both = dot_t(unit, weighted).astype(jnp.bfloat16)
        y_ref[t] = both[:snaps]
        y_ref[t + shift] = both[snaps:]


def ends_body(y_in, ends_ref, dt_ref, scale_ref, select_ref, side_ref, y_ref, u0, u1, ce, cs):
    rows, snaps, width = y_in.shape
    half = -(-rows // 2)
    shift = rows - half
    count = half + 2 * PASSES
    lane = lane_iota((1, LANES))
    low, high = 8, 8 + EDGES
    inner = high - 8
    for k in range(count):
        pair = side_ref[16 * (k // 2) : 16 * (k // 2) + 16, :].astype(jnp.float32)
        halo = pair[8 * (k % 2) : 8 * (k % 2) + 8]
        u0[k, low : low + 8, :] = halo
        u0[k, low + 8 : inner, :] = ends_ref[k]
        u0[k, inner:high, :] = halo
    side_d = side_ref[side_ref.shape[0] - 16 :, :].astype(jnp.float32)
    halo = side_d[0:8] + side_d[8:16]
    here = jnp.concatenate([halo, dt_ref[...], halo], axis=0)
    beside = jnp.concatenate([here[1:], jnp.zeros((1, LANES), jnp.float32)], axis=0)
    spread_faces(here, beside, select_ref, ce, cs, slice(low, high))
    outside = jnp.zeros((8, LANES), jnp.float32)
    for buffer in (u0, u1):
        for k in range(count):
            buffer[k, high : high + 8, :] = outside
    done = smoothing_passes(u0, u1, ce, cs, low, high, low + 8, inner, half, lane < snaps)
    unit = eye(width)
    middle = jnp.zeros((width - 16, LANES), jnp.float32)
    ends = (lane < PASSES) | (lane >= width - PASSES)
    for t in range(half):
        west = done[t + PASSES, low + 8 : low + 16, :]
        east = done[t + PASSES, inner - 8 : inner, :]
        weighted = (jnp.concatenate([west, middle, east], axis=0) * scale_ref[t : t + 1, :]).astype(jnp.bfloat16)
        both = dot_t(unit, weighted)
        for r, part in ((t, both[:snaps]), (t + shift, both[snaps:])):
            y_ref[r] = jnp.where(ends, part.astype(jnp.bfloat16), y_in[r])


def smooth(x, d, side, a, b, tiles):
    rows, snaps, width = x.shape
    count = -(-rows // 2) + 2 * PASSES
    f32 = lambda *shape: jax.ShapeDtypeStruct(shape, jnp.float32)
    field = lambda n: VMEM((count, n, LANES), jnp.float32)
    source = np.arange(LANES) % (LANES // 2)
    wanted = np.arange(count)[:, None] + np.where(np.arange(LANES) < snaps, 0, rows // 2)
    select = jnp.asarray(source[None, :, None] == wanted[:, None, :], jnp.bfloat16)
    out = jax.ShapeDtypeStruct(x.shape, jnp.bfloat16)
    tall = -(-(-(-rows // 2)) // 8) * 8
    y, ends, dt, scale = kernel_call(
        interior_body,
        (out, f32(count, 2 * EDGE, LANES), f32(2 * EDGE, LANES), f32(tall, LANES)),
        [field(OWN + width + 16)] * 4 + [VMEM((width, LANES), jnp.float32)],
        flops=1 << 32,
    )(x, d, b, a, tiles, select)
    return kernel_call(ends_body, out, [field(EDGES + 16)] * 4)(y, ends, dt, scale, select, side)


def mm(a, b):
    return jnp.dot(a, b, precision=exact, preferred_element_type=jnp.float32)


def mmt(a, b):
    return lax.dot_general(
        a, b, (((1,), (1,)), ((), ())), precision=exact, preferred_element_type=jnp.float32
    )


def inverse_factors(grams, block=16):
    n = RANK
    row = lax.broadcasted_iota(jnp.int32, (n, LANES), 0)
    lane = lane_iota((n, LANES))
    diagonal = row == lane % n
    unit = diagonal.astype(jnp.float32)
    first = lane // n * n
    s = jnp.concatenate(list(grams) + [unit[:, :n]] * (LANES // n - len(grams)), axis=1)

    def pivots(m):
        return jnp.sum(jnp.where(diagonal, m, 0.0), axis=0, keepdims=True)

    least = jnp.max(pivots(s), axis=1, keepdims=True) * 1e-12 + 1e-37
    inv = unit
    done = []
    for k0 in range(0, n, block):
        tall = n - k0
        cols = [jnp.take_along_axis(s, (first + (k0 + j))[:tall], axis=1) for j in range(block)]
        for p in range(min(block, tall - 1)):
            inverse = 1.0 / jnp.maximum(cols[p][p : p + 1], least)
            below = jnp.where(row[:tall] > p, cols[p], 0.0)
            for j in range(p + 1, block):
                cols[j] = cols[j] - below * (cols[j][p : p + 1] * inverse)
            s = s - below * (s[p : p + 1] * inverse)
            inv = inv - below * (inv[p : p + 1] * inverse)
        done.append((s[:block], inv[:block]))
        s, inv = s[block:], inv[block:]
    s, inv = (jnp.concatenate(v, axis=0) for v in zip(*done))
    scale = lax.rsqrt(jnp.maximum(pivots(s), least))
    out = []
    for g in range(len(grams)):
        seg = slice(n * g, n * g + n)
        rows_scale = jnp.sum(jnp.where(diagonal[:, seg], scale[:, seg], 0.0), axis=1, keepdims=True)
        out.append(inv[:, seg] * rows_scale)
    return out


def power_bases(hs, upper_first):
    squares, starts = [], []
    for h in hs:
        n = h.shape[0]
        on = lax.broadcasted_iota(jnp.int32, (n, n), 0) == lane_iota((n, n))
        top = jnp.max(jnp.max(jnp.where(on, h, 0.0), axis=1, keepdims=True), axis=0, keepdims=True)
        unit = 1.0 / jnp.maximum(top, 1e-30)
        h2 = mm(h, h) * (unit * unit)
        squares.append(h2)
        starts.append(h2[:RANK] if upper_first is None else jnp.where(upper_first, h2[RANK:], h2[:RANK]))
    factors = inverse_factors([mmt(z, z) for z in starts])
    return [mm(mm(f, z), h2) for f, z, h2 in zip(factors, starts, squares)]


def top_rows(hs, upper_first=None):
    zs = power_bases(hs, upper_first)
    return [mm(f, z) for f, z in zip(inverse_factors([mmt(z, z) for z in zs]), zs)]


def diagonal_blocks(a, b):
    top = jnp.concatenate([a, jnp.zeros((a.shape[0], b.shape[1]), a.dtype)], axis=1)
    low = jnp.concatenate([jnp.zeros((b.shape[0], a.shape[1]), b.dtype), b], axis=1)
    return jnp.concatenate([top, low], axis=0)


def projection(gram, coef, upper_first, w=None):
    zt = power_bases([gram], upper_first)[0]
    on, out = mmt(coef, zt), zt if w is None else mm(zt, w)
    f = inverse_factors([mmt(mm(zt, gram), zt)])[0]
    return mm(mmt(on, f), mm(f, out))


def stack_of(*refs):
    return lambda i: jnp.concatenate([ref[i] for ref in refs], axis=0)


def gram_sum(left, right, rows):
    acc = None
    for i in range(0, rows, 2):
        at = range(i, min(i + 2, rows))
        part = dot_t(
            jnp.concatenate([left(r) for r in at], axis=1),
            jnp.concatenate([right(r) for r in at], axis=1),
        )
        acc = part if acc is None else acc + part
    return acc


def pair_gram_body(own_ref, other_ref, o_ref):
    n = own_ref.shape[1]
    both = stack_of(own_ref, other_ref)
    acc = gram_sum(both, both, own_ref.shape[0])
    cross = jnp.where(odd(0), pltpu.roll(acc[n + n // 2 :], n, 1), acc[: n // 2])[:, n:]
    tall = o_ref.shape[1]
    packed = jnp.concatenate(
        [acc[:tall, :n], jnp.concatenate([acc[tall:n, :n], cross], axis=0)], axis=1
    )
    for j in range(o_ref.shape[0]):
        o_ref[j] = packed


def pair_gram(g, gp, n):
    tall = g.shape[0]
    rest = n - tall
    block = lambda v: jnp.concatenate([v[:, :n], v[:rest, n:]], axis=0)
    mine, theirs = g[rest:, n:], gp[rest:, n:]
    upper = odd(0)
    cross = jnp.concatenate([jnp.where(upper, theirs, mine), jnp.where(upper, mine, theirs)], axis=0)
    flipped = cross.T
    return block(g), block(gp), jnp.where(upper, flipped, cross), jnp.where(upper, cross, flipped)


def put_rows(w, stacked, o_ref):
    for i in range(o_ref.shape[0]):
        o_ref[i] = jnp.dot(w, stacked(i), preferred_element_type=jnp.float32).astype(jnp.bfloat16)


def put_result(w, stacked, o_hbm, buffer, sems):
    rows = buffer.shape[0]
    parts = sems.shape[0]
    size = -(-rows // parts)
    copies = []
    for p in range(parts):
        lo, hi = p * size, min(rows, p * size + size)
        for i in range(lo, hi):
            buffer[i] = jnp.dot(w, stacked(i), preferred_element_type=jnp.float32).astype(jnp.bfloat16)
        at = pl.ds(lo, hi - lo)
        copies.append(pltpu.make_async_copy(buffer.at[at], o_hbm.at[at], sems.at[p]))
        copies[-1].start()
    for copy in copies:
        copy.wait()


def result_call(body, rows, snaps, width):
    parts = 5
    return kernel_call(
        body,
        jax.ShapeDtypeStruct((rows, snaps, width), jnp.bfloat16),
        [VMEM((rows, snaps, width), jnp.bfloat16), pltpu.SemaphoreType.DMA((parts,))],
        out_spec=pl.BlockSpec(memory_space=pl.ANY),
    )


def put_modes(w, stacked, modes_ref, part_ref):
    rows, half = modes_ref.shape[0], part_ref.shape[0]
    put_rows(w, stacked, modes_ref)
    start = jnp.where(odd(0), rows - half, 0)
    for i in range(half):
        part_ref[i] = modes_ref[start + i]


def halves(rows, here_ref, there_ref):
    half = here_ref.shape[0]
    upper = odd(0)

    def row(i):
        if i < half:
            return jnp.where(upper, there_ref[i], here_ref[i])
        j = i - (rows - half)
        return jnp.where(upper, here_ref[j], there_ref[j])

    return row


def far_gram_body(own_ref, other_ref, far_ref, o_ref):
    n = own_ref.shape[1]
    acc = gram_sum(stack_of(own_ref, other_ref), lambda i: far_ref[i], own_ref.shape[0])
    packed = jnp.concatenate([acc[:n], acc[n:]], axis=1)
    for j in range(o_ref.shape[0]):
        o_ref[j] = packed


def square(a, b, c, d):
    return jnp.concatenate(
        [jnp.concatenate([a, b], axis=1), jnp.concatenate([c, d], axis=1)], axis=0
    )


def pair_levels_body(g_ref, gp_ref, wh_ref, c_ref):
    n = c_ref.shape[0]
    own, other, cross, flipped = pair_gram(g_ref[...], gp_ref[...], n)
    gram = square(own, cross, flipped, other)
    basis = diagonal_blocks(*top_rows([own, other]))
    merged = mmt(mm(basis, gram), basis)
    q = top_rows([merged], odd(0))[0]
    h = mmt(mm(q, merged), q)
    w = mm(q, basis)
    c_ref[...] = mmt(gram[:n], w)
    wh_ref[...] = jnp.concatenate(
        [w, jnp.concatenate([h, jnp.zeros((RANK, LANES - RANK), jnp.float32)], axis=1)], axis=0
    )


def quad_level(wh_ref, c_ref, far_wh_ref, cs_ref, twin_ref):
    n = c_ref.shape[0]
    cs, twin = cs_ref[...], twin_ref[...]
    between = square(cs[:, :n], twin[:, n:], cs[:, n:], twin[:, :n])
    wa, wb = wh_ref[:RANK, :], far_wh_ref[:RANK, :]
    on_b = mmt(between, wb)
    mixed = mm(wa, on_b)
    gram = square(wh_ref[RANK:, :RANK], mixed, mixed.T, far_wh_ref[RANK:, :RANK])
    return diagonal_blocks(wa, wb), gram, jnp.concatenate([c_ref[...], on_b[:n]], axis=1)


def quad_project_body(wh, c, far_wh, cs, twin, yo, yp, yy, yz, o_hbm, buffer, sems):
    w, gram, coef = quad_level(wh, c, far_wh, cs, twin)
    weights = projection(gram, coef, odd(1), w).astype(jnp.bfloat16)
    put_result(weights, stack_of(yo, yp, yy, yz), o_hbm, buffer, sems)


def quad_modes_body(wh, c, far_wh, cs, twin, yo, yp, yy, yz, modes_ref, part_ref, h_ref, c_ref):
    w, gram, coef = quad_level(wh, c, far_wh, cs, twin)
    q = top_rows([gram], odd(1))[0]
    h_ref[...] = mmt(mm(q, gram), q)
    c_ref[...] = mmt(coef, q)
    put_modes(mm(q, w).astype(jnp.bfloat16), stack_of(yo, yp, yy, yz), modes_ref, part_ref)


def cross_body(here_ref, there_ref, y_ref, own_ref, o_ref):
    rows = y_ref.shape[0]
    other = halves(rows, here_ref, there_ref)
    acc = gram_sum(other, lambda i: jnp.concatenate([y_ref[i], own_ref[i], other(i)], axis=0), rows)
    for j in range(o_ref.shape[0]):
        o_ref[j] = acc


def merged_gram(p_ref, h_ref, c_ref, n):
    total = p_ref[0]
    for j in range(1, p_ref.shape[0]):
        total = total + p_ref[j]
    mixed = total[:, n : n + RANK]
    gram = jnp.concatenate(
        [
            jnp.concatenate([h_ref[...], mixed.T], axis=1),
            jnp.concatenate([mixed, total[:, n + RANK :]], axis=1),
        ],
        axis=0,
    )
    coef = jnp.concatenate([c_ref[...], total[:, :n].T], axis=1)
    return gram, coef


def merge_body(level, p_ref, h_ref, c_ref, own_ref, here_ref, there_ref, modes_ref, part_ref, hn_ref, cn_ref):
    gram, coef = merged_gram(p_ref, h_ref, c_ref, c_ref.shape[0])
    w = top_rows([gram], odd(level))[0].astype(jnp.bfloat16)
    wf = w.astype(jnp.float32)
    cn_ref[...] = mmt(coef, wf)
    hn_ref[...] = mmt(mm(wf, gram), wf)
    other = halves(own_ref.shape[0], here_ref, there_ref)
    put_modes(w, lambda i: jnp.concatenate([own_ref[i], other(i)], axis=0), modes_ref, part_ref)


def project_body(level, p_ref, h_ref, c_ref, own_ref, here_ref, there_ref, o_hbm, buffer, sems):
    gram, coef = merged_gram(p_ref, h_ref, c_ref, c_ref.shape[0])
    weights = projection(gram, coef, odd(level)).astype(jnp.bfloat16)
    other = halves(own_ref.shape[0], here_ref, there_ref)
    stacked = lambda i: jnp.concatenate([own_ref[i], other(i)], axis=0)
    put_result(weights, stacked, o_hbm, buffer, sems)


def exchanged(block, level):
    count = lax.axis_size("tm")
    return lax.ppermute(block, "tm", [(i, i ^ 1 << level) for i in range(count)])


def gathered(parts):
    return lax.all_to_all(parts, ("lat", "lon"), 0, 0, tiled=True)


def shards(residuals, diffusivity):
    snaps, rows, width = residuals.shape
    tiles = lax.axis_size("lat") * lax.axis_size("lon")
    levels = lax.axis_size("tm").bit_length() - 1
    f32 = lambda *shape: jax.ShapeDtypeStruct(shape, jnp.float32)
    b16 = lambda *shape: jax.ShapeDtypeStruct(shape, jnp.bfloat16)
    x = jnp.transpose(residuals, (1, 0, 2))
    y = smooth(x, diffusivity, *halo_exchange(x, diffusivity))
    other, far = exchanged(y, 0), exchanged(y, 1)
    pair = kernel_call(pair_gram_body, f32(tiles, snaps * 3 // 4, 2 * snaps))(y, other)
    pair = jnp.sum(gathered(pair), axis=0)
    pair_twin = exchanged(pair, 0)
    far, pair_twin = lax.optimization_barrier((far, pair_twin))
    cross = kernel_call(far_gram_body, f32(tiles, snaps, 2 * snaps))(y, other, far)
    cross = jnp.sum(gathered(cross), axis=0)
    wh, c = kernel_call(
        pair_levels_body, (f32(2 * RANK, 2 * snaps), f32(snaps, RANK)), flops=1 << 32
    )(pair, pair_twin)
    operands = (wh, c, exchanged(wh, 1), cross, exchanged(cross, 0))
    operands += (y, other, far, exchanged(far, 0))
    if levels == 2:
        out = result_call(quad_project_body, rows, snaps, width)(*operands)
        return jnp.transpose(out, (1, 0, 2))
    block = (
        b16(rows, RANK, width),
        b16(-(-rows // 2), RANK, width),
        f32(RANK, RANK),
        f32(snaps, RANK),
    )
    modes, part, h, c = kernel_call(quad_modes_body, block)(*operands)
    for level in range(2, levels):
        here = exchanged(part, level)
        there = exchanged(here, 0)
        parts = gathered(kernel_call(cross_body, f32(tiles, RANK, snaps + 2 * RANK))(here, there, y, modes))
        if level < levels - 1:
            modes, part, h, c = kernel_call(functools.partial(merge_body, level), block)(
                parts, h, c, modes, here, there
            )
    out = result_call(functools.partial(project_body, levels - 1), rows, snaps, width)(
        parts, h, c, modes, here, there
    )
    return jnp.transpose(out, (1, 0, 2))


def solution(mesh):
    return jax.shard_map(
        shards,
        mesh=mesh,
        in_specs=(P("tm", "lat", "lon"), P("lat", "lon")),
        out_specs=P("tm", "lat", "lon"),
        check_vma=False,
    )
```

```python
import functools
import math

import jax
import jax.numpy as jnp
import numpy as np
from jax import lax
from jax.experimental import pallas as pl
from jax.experimental.pallas import tpu as pltpu
from jax.sharding import PartitionSpec as P

RANK = 32
PASSES = 4
LANES = 128
exact = lax.Precision.HIGHEST
VMEM = pltpu.VMEM


def whole():
    return pl.BlockSpec(memory_space=VMEM)


def kernel_call(body, outs, scratch=(), flops=1 << 20, specs=None, vmem=48 << 20, out_spec=None):
    return pl.pallas_call(
        body,
        out_shape=outs,
        **({} if specs is None else {"in_specs": specs}),
        out_specs=jax.tree.map(lambda _: out_spec or whole(), outs),
        scratch_shapes=list(scratch),
        compiler_params=pltpu.CompilerParams(vmem_limit_bytes=vmem),
        cost_estimate=pl.CostEstimate(flops=flops, bytes_accessed=1 << 20, transcendentals=0),
    )


def lane_iota(shape):
    return lax.broadcasted_iota(jnp.int32, shape, len(shape) - 1)


def roll(x, shift):
    return pltpu.roll(x, shift % LANES, x.ndim - 1)


def eye(n, dtype=jnp.bfloat16):
    row = lax.broadcasted_iota(jnp.int32, (n, n), 0)
    return (row == lax.broadcasted_iota(jnp.int32, (n, n), 1)).astype(dtype)


def dot_t(a, b):
    return lax.dot_general(a, b, (((1,), (1,)), ((), ())), preferred_element_type=jnp.float32)


def split2(v):
    high = v.astype(jnp.bfloat16)
    return high, (v - high.astype(jnp.float32)).astype(jnp.bfloat16)


def odd(level):
    return (lax.axis_index("tm") >> level & 1) == 1


def even_lat():
    return lax.axis_index("lat") % 2 == 0


def edge_body(x_hbm, d_hbm, a_ref, b_ref, d_ref, sems):
    rows, snaps, width = x_hbm.shape
    even = even_lat()
    flags = ((a_ref, even), (b_ref, jnp.logical_not(even)))
    copies = [pltpu.make_async_copy(d_hbm, d_ref, sems.at[0])]
    for ref, south in flags:
        start = jnp.where(south, rows - PASSES, 0)
        for r in range(PASSES):
            copies.append(
                pltpu.make_async_copy(
                    x_hbm.at[start + r], ref.at[pl.ds(r * snaps, snaps)], sems.at[len(copies)]
                )
            )
    for copy in copies:
        copy.start()
    copies[0].wait()
    pad = jnp.zeros((8, width), jnp.float32)
    edge = lambda lo: [v.astype(jnp.float32) for v in split2(d_ref[lo : lo + PASSES, :])]
    first, final = edge(0), edge(rows - PASSES)
    for ref, south in flags:
        term = [jnp.where(south, f, g) for f, g in zip(final, first)]
        ref[PASSES * snaps :, :] = jnp.concatenate(term + [pad], axis=0).astype(jnp.bfloat16)
    for copy in copies[1:]:
        copy.wait()


def by_side(a_ref, b_ref):
    even = even_lat()

    def picked(lo, hi):
        a, b = a_ref[lo:hi, :], b_ref[lo:hi, :]
        return jnp.where(even, b, a), jnp.where(even, a, b)

    return picked


def tile_rows(x_ref, north, south, t):
    rows, snaps, _ = x_ref.shape
    first = north[(t + PASSES) * snaps : (t + PASSES + 1) * snaps] if t < 0 else x_ref[t]
    r = t + rows // 2
    second = x_ref[r] if r < rows else south[(r - rows) * snaps : (r - rows + 1) * snaps]
    return jnp.concatenate([first, second], axis=0)


def extend_rows(dn, d_ref, north_d, south_d):
    rows = d_ref.shape[0]
    dn[...] = jnp.zeros(dn.shape, jnp.float32)
    dn[PASSES : PASSES + rows, :] = d_ref[...]
    dn[0:PASSES, :] = north_d[0:PASSES] + north_d[PASSES : 2 * PASSES]
    dn[PASSES + rows : 2 * PASSES + rows, :] = south_d[0:PASSES] + south_d[PASSES : 2 * PASSES]


def edge_picks(width):
    row = lax.broadcasted_iota(jnp.int32, (16, width), 0)
    lane = lane_iota((16, width))
    column = jnp.where(row % 8 < PASSES, row % 8, width - 8 + row % 8)
    return [((lane == column) & (row // 8 == k)).astype(jnp.bfloat16) for k in range(2)]


def own_body(x_ref, m_ref, tiles_ref):
    rows, snaps, width = x_ref.shape
    half = tiles_ref.shape[0]
    pick, unit = edge_picks(width), eye(width)
    for t in range(half):
        tiles_ref[t] = dot_t(unit, tile_rows(x_ref, None, None, t))
    for t in range(0, half - 1, 2):
        first, second = (tile_rows(x_ref, None, None, t + j) for j in range(2))
        m_ref[8 * t : 8 * t + 16, :] = (dot_t(pick[0], first) + dot_t(pick[1], second)).astype(jnp.bfloat16)


def pack_body(x_ref, d_ref, b_ref, a_ref, own_ref, m_ref, dn):
    rows, snaps, width = x_ref.shape
    half = -(-rows // 2)
    count = half + 2 * PASSES
    edge = PASSES * snaps
    pick = edge_picks(width)
    picked = by_side(a_ref, b_ref)
    north, south = picked(0, edge)
    north_d, south_d = (v.astype(jnp.float32) for v in picked(edge, edge + 16))
    begin, end = 8 * PASSES, 8 * PASSES + own_ref.shape[0]
    m_ref[begin:end, :] = own_ref[...]
    for k in range(0, count, 2):
        if begin <= 8 * k < end:
            continue
        out = dot_t(pick[0], tile_rows(x_ref, north, south, k - PASSES))
        if k + 1 < count:
            out = out + dot_t(pick[1], tile_rows(x_ref, north, south, k + 1 - PASSES))
        m_ref[8 * k : 8 * k + 16, :] = out.astype(jnp.bfloat16)
    extend_rows(dn, d_ref, north_d, south_d)
    high, low = split2(dn[...])
    end = m_ref.shape[0]
    m_ref[end - 16 :, :] = (dot_t(pick[0], high) + dot_t(pick[1], low)).astype(jnp.bfloat16)


def halo_exchange(x, d):
    rows, snaps, width = x.shape
    count = -(-rows // 2) + 2 * PASSES
    shape = lambda n: jax.ShapeDtypeStruct((n, width), jnp.bfloat16)
    edge = PASSES * snaps + 16
    hbm = pl.BlockSpec(memory_space=pltpu.HBM)
    a, b = kernel_call(
        edge_body,
        (shape(edge), shape(edge)),
        [VMEM(d.shape, d.dtype), pltpu.SemaphoreType.DMA((2 * PASSES + 1,))],
        specs=[hbm, hbm],
        vmem=60 << 20,
    )(x, d)
    lons, lats = lax.axis_size("lon"), lax.axis_size("lat")

    def swapped(message, start):
        pairs = [(i, i + 1) for i in range(start, lats - 1, 2)]
        return lax.ppermute(message, "lat", pairs + [(j, i) for i, j in pairs])

    a, b = swapped(a, 0), swapped(b, 1)
    half = -(-rows // 2)
    own, tiles = kernel_call(
        own_body, (shape(16 * (half // 2)), jax.ShapeDtypeStruct((half, width, 2 * snaps), jnp.float32))
    )(x)
    packed = kernel_call(
        pack_body, shape(16 * (-(-count // 2)) + 16), [VMEM((width, LANES), jnp.float32)]
    )(x, d, b, a, own)
    forward = [(i, (i + 1) % lons) for i in range(lons)]
    side = lax.ppermute(packed, "lon", forward)
    if lons > 2:
        from_east = lax.ppermute(packed, "lon", [(j, i) for i, j in forward])
        side = jnp.where(lax.broadcasted_iota(jnp.int32, side.shape, 0) % 8 < PASSES, from_east, side)
    return side, a, b, tiles


OWN = 16
EDGE = 8
EDGES = 8 + 2 * EDGE + 8


def spread_faces(here, beside, select_ref, ce, cs, rows_at):
    n = here.shape[0]
    lane = lane_iota((1, LANES))
    faces = jnp.concatenate([here + beside, here + roll(here, -1)], axis=0) * 0.5
    high, low = (v.astype(jnp.float32) for v in split2(faces))
    terms = jnp.where(lane < LANES // 2, high, roll(low, LANES // 2)).astype(jnp.bfloat16)
    for k in range(select_ref.shape[0]):
        spread = jnp.dot(terms, select_ref[k], preferred_element_type=jnp.float32)
        ce[k, rows_at, :] = spread[:n]
        cs[k, rows_at, :] = spread[n:]


def smoothing_passes(u0, u1, ce, cs, low, high, own_low, own_high, half, left):
    count = u0.shape[0]
    lats, lat = lax.axis_size("lat"), lax.axis_index("lat")
    buffers = (u0, u1)
    first_row = lax.broadcasted_iota(jnp.int32, (8, LANES), 0) == 0
    for step in range(PASSES):
        src, dst = buffers[step % 2], buffers[(step + 1) % 2]
        final = step == PASSES - 1
        start, stop = step + 1, count - 1 - step
        blocks = range(own_low, own_high, 8) if final else range(low, high, 8)
        current = [src[start, r : r + 8, :] for r in blocks]
        above = [
            cs[start - 1, r : r + 8, :] * (c - src[start - 1, r : r + 8, :])
            for r, c in zip(blocks, current)
        ]

        def eastward(k, r, here):
            return ce[k, r : r + 8, :] * (src[k, r + 1 : r + 9, :] - here)

        for k in range(start, stop):
            before = None
            if blocks[0] > low:
                r = blocks[0] - 8
                before = pltpu.roll(eastward(k, r, src[k, r : r + 8, :]), 1, 0)
            for i, r in enumerate(blocks):
                here = current[i]
                east_flux = eastward(k, r, here)
                turned = pltpu.roll(east_flux, 1, 0)
                west_flux = turned if before is None else jnp.where(first_row, before, turned)
                below = src[k + 1, r : r + 8, :]
                south_flux = cs[k, r : r + 8, :] * (below - here)
                dst[k, r : r + 8, :] = here + ((south_flux - above[i]) + (east_flux - west_flux))
                current[i], above[i], before = below, south_flux, turned
        if not final:
            north, beyond, at = PASSES - 1, PASSES + half, slice(low, high)

            @pl.when(lat == 0)
            def _():
                dst[north, at, :] = jnp.where(left, 0.0, dst[north, at, :])

            @pl.when(lat == lats - 1)
            def _():
                dst[beyond, at, :] = jnp.where(left, dst[beyond, at, :], 0.0)

    return buffers[PASSES % 2]


def area_scale(rows, snaps):
    half = -(-rows // 2)
    shape = (-(-half // 8) * 8, LANES)
    lats, lat = lax.axis_size("lat"), lax.axis_index("lat")
    row = lax.broadcasted_iota(jnp.int32, shape, 0) + jnp.where(lane_iota(shape) < snaps, 0, rows - half)
    angle = ((row + lat * rows).astype(jnp.float32) + 0.5) * math.pi / (rows * lats) - math.pi / 2
    return jnp.sqrt(jnp.maximum(jnp.cos(angle), 0.0))


def interior_body(x_ref, d_ref, b_ref, a_ref, tiles_ref, select_ref, y_ref, ends_ref, dt_ref, scale_ref, u0, u1, ce, cs, dn):
    rows, snaps, width = x_ref.shape
    half = -(-rows // 2)
    shift = rows - half
    count = half + 2 * PASSES
    lane = lane_iota((1, LANES))
    east = OWN + width
    unit = eye(width)
    edge = PASSES * snaps
    picked = by_side(a_ref, b_ref)
    north, south = picked(0, edge)
    north_d, south_d = (v.astype(jnp.float32) for v in picked(edge, edge + 16))
    outside = jnp.zeros((8, LANES), jnp.float32)
    for k in range(count):
        t = k - PASSES
        if 0 <= t < half:
            tile = tiles_ref[t]
        else:
            tile = dot_t(unit, tile_rows(x_ref, north, south, t))
        u0[k, OWN:east, :] = tile
        ends_ref[k, :EDGE, :] = tile[:EDGE]
        ends_ref[k, EDGE:, :] = tile[width - EDGE :]
        u0[k, east : east + 8, :] = outside
        u1[k, east : east + 8, :] = outside
    extend_rows(dn, d_ref, north_d, south_d)
    dt = dn[...].T
    dt_ref[:EDGE, :] = dt[:EDGE]
    dt_ref[EDGE:, :] = dt[width - EDGE :]
    beside = jnp.concatenate([dt[1:], jnp.zeros((1, LANES), jnp.float32)], axis=0)
    spread_faces(dt, beside, select_ref, ce, cs, slice(OWN, east))
    done = smoothing_passes(u0, u1, ce, cs, OWN, east, OWN, east, half, lane < snaps)
    scale = area_scale(rows, snaps)
    scale_ref[...] = scale
    for t in range(half):
        weighted = (done[t + PASSES, OWN:east, :] * scale[t : t + 1]).astype(jnp.bfloat16)
        both = dot_t(unit, weighted).astype(jnp.bfloat16)
        y_ref[t] = both[:snaps]
        y_ref[t + shift] = both[snaps:]


def ends_body(y_in, ends_ref, dt_ref, scale_ref, select_ref, side_ref, y_ref, u0, u1, ce, cs):
    rows, snaps, width = y_in.shape
    half = -(-rows // 2)
    shift = rows - half
    count = half + 2 * PASSES
    lane = lane_iota((1, LANES))
    low, high = 8, 8 + EDGES
    inner = high - 8
    for k in range(count):
        pair = side_ref[16 * (k // 2) : 16 * (k // 2) + 16, :].astype(jnp.float32)
        halo = pair[8 * (k % 2) : 8 * (k % 2) + 8]
        u0[k, low : low + 8, :] = halo
        u0[k, low + 8 : inner, :] = ends_ref[k]
        u0[k, inner:high, :] = halo
    side_d = side_ref[side_ref.shape[0] - 16 :, :].astype(jnp.float32)
    halo = side_d[0:8] + side_d[8:16]
    here = jnp.concatenate([halo, dt_ref[...], halo], axis=0)
    beside = jnp.concatenate([here[1:], jnp.zeros((1, LANES), jnp.float32)], axis=0)
    spread_faces(here, beside, select_ref, ce, cs, slice(low, high))
    outside = jnp.zeros((8, LANES), jnp.float32)
    for buffer in (u0, u1):
        for k in range(count):
            buffer[k, high : high + 8, :] = outside
    done = smoothing_passes(u0, u1, ce, cs, low, high, low + 8, inner, half, lane < snaps)
    row, column = (lax.broadcasted_iota(jnp.int32, (16, width), axis) for axis in range(2))
    place = (column == jnp.where(row < 8, row, width - 16 + row)).astype(jnp.bfloat16)
    ends = (lane < PASSES) | (lane >= width - PASSES)
    for t in range(half):
        west = done[t + PASSES, low + 8 : low + 16, :]
        east = done[t + PASSES, inner - 8 : inner, :]
        weighted = (jnp.concatenate([west, east], axis=0) * scale_ref[t : t + 1, :]).astype(jnp.bfloat16)
        both = lax.dot_general(
            weighted, place, (((0,), (0,)), ((), ())), preferred_element_type=jnp.float32
        )
        for r, part in ((t, both[:snaps]), (t + shift, both[snaps:])):
            y_ref[r] = jnp.where(ends, part.astype(jnp.bfloat16), y_in[r])


def smooth(x, d, side, a, b, tiles):
    rows, snaps, width = x.shape
    count = -(-rows // 2) + 2 * PASSES
    f32 = lambda *shape: jax.ShapeDtypeStruct(shape, jnp.float32)
    field = lambda n: VMEM((count, n, LANES), jnp.float32)
    source = np.arange(LANES) % (LANES // 2)
    wanted = np.arange(count)[:, None] + np.where(np.arange(LANES) < snaps, 0, rows // 2)
    select = jnp.asarray(source[None, :, None] == wanted[:, None, :], jnp.bfloat16)
    out = jax.ShapeDtypeStruct(x.shape, jnp.bfloat16)
    tall = -(-(-(-rows // 2)) // 8) * 8
    y, ends, dt, scale = kernel_call(
        interior_body,
        (out, f32(count, 2 * EDGE, LANES), f32(2 * EDGE, LANES), f32(tall, LANES)),
        [field(OWN + width + 16)] * 4 + [VMEM((width, LANES), jnp.float32)],
        flops=1 << 32,
    )(x, d, b, a, tiles, select)
    return kernel_call(ends_body, out, [field(EDGES + 16)] * 4)(y, ends, dt, scale, select, side)


def mm(a, b):
    return jnp.dot(a, b, precision=exact, preferred_element_type=jnp.float32)


def mmt(a, b):
    return lax.dot_general(
        a, b, (((1,), (1,)), ((), ())), precision=exact, preferred_element_type=jnp.float32
    )


def inverse_factors(grams, block=16):
    n = RANK
    row = lax.broadcasted_iota(jnp.int32, (n, LANES), 0)
    lane = lane_iota((n, LANES))
    diagonal = row == lane % n
    unit = diagonal.astype(jnp.float32)
    first = lane // n * n
    s = jnp.concatenate(list(grams) + [unit[:, :n]] * (LANES // n - len(grams)), axis=1)

    def pivots(m):
        return jnp.sum(jnp.where(diagonal, m, 0.0), axis=0, keepdims=True)

    least = jnp.max(pivots(s), axis=1, keepdims=True) * 1e-12 + 1e-37
    inv = unit
    done = []
    for k0 in range(0, n, block):
        tall = n - k0
        cols = [jnp.take_along_axis(s, (first + (k0 + j))[:tall], axis=1) for j in range(block)]
        for p in range(min(block, tall - 1)):
            inverse = 1.0 / jnp.maximum(cols[p][p : p + 1], least)
            below = jnp.where(row[:tall] > p, cols[p], 0.0)
            for j in range(p + 1, block):
                cols[j] = cols[j] - below * (cols[j][p : p + 1] * inverse)
            s = s - below * (s[p : p + 1] * inverse)
            inv = inv - below * (inv[p : p + 1] * inverse)
        done.append((s[:block], inv[:block]))
        s, inv = s[block:], inv[block:]
    s, inv = (jnp.concatenate(v, axis=0) for v in zip(*done))
    scale = lax.rsqrt(jnp.maximum(pivots(s), least))
    out = []
    for g in range(len(grams)):
        seg = slice(n * g, n * g + n)
        rows_scale = jnp.sum(jnp.where(diagonal[:, seg], scale[:, seg], 0.0), axis=1, keepdims=True)
        out.append(inv[:, seg] * rows_scale)
    return out


def power_bases(hs, upper_first):
    squares, starts = [], []
    for h in hs:
        n = h.shape[0]
        on = lax.broadcasted_iota(jnp.int32, (n, n), 0) == lane_iota((n, n))
        top = jnp.max(jnp.max(jnp.where(on, h, 0.0), axis=1, keepdims=True), axis=0, keepdims=True)
        unit = 1.0 / jnp.maximum(top, 1e-30)
        h2 = mm(h, h) * (unit * unit)
        squares.append(h2)
        starts.append(h2[:RANK] if upper_first is None else jnp.where(upper_first, h2[RANK:], h2[:RANK]))
    factors = inverse_factors([mmt(z, z) for z in starts])
    return [mm(mm(f, z), h2) for f, z, h2 in zip(factors, starts, squares)]


def top_rows(hs, upper_first=None):
    zs = power_bases(hs, upper_first)
    return [mm(f, z) for f, z in zip(inverse_factors([mmt(z, z) for z in zs]), zs)]


def diagonal_blocks(a, b):
    top = jnp.concatenate([a, jnp.zeros((a.shape[0], b.shape[1]), a.dtype)], axis=1)
    low = jnp.concatenate([jnp.zeros((b.shape[0], a.shape[1]), b.dtype), b], axis=1)
    return jnp.concatenate([top, low], axis=0)


def projection(gram, coef, upper_first, w=None):
    zt = power_bases([gram], upper_first)[0]
    on, out = mmt(coef, zt), zt if w is None else mm(zt, w)
    f = inverse_factors([mmt(mm(zt, gram), zt)])[0]
    return mm(mmt(on, f), mm(f, out))


def stack_of(*refs):
    return lambda i: jnp.concatenate([ref[i] for ref in refs], axis=0)


def gram_sum(left, right, rows):
    acc = None
    for i in range(0, rows, 2):
        at = range(i, min(i + 2, rows))
        part = dot_t(
            jnp.concatenate([left(r) for r in at], axis=1),
            jnp.concatenate([right(r) for r in at], axis=1),
        )
        acc = part if acc is None else acc + part
    return acc


def pair_gram_body(own_ref, other_ref, o_ref):
    n = own_ref.shape[1]
    both = stack_of(own_ref, other_ref)
    acc = gram_sum(both, both, own_ref.shape[0])
    cross = jnp.where(odd(0), pltpu.roll(acc[n + n // 2 :], n, 1), acc[: n // 2])[:, n:]
    tall = o_ref.shape[1]
    packed = jnp.concatenate(
        [acc[:tall, :n], jnp.concatenate([acc[tall:n, :n], cross], axis=0)], axis=1
    )
    for j in range(o_ref.shape[0]):
        o_ref[j] = packed


def pair_gram(g, gp, n):
    tall = g.shape[0]
    rest = n - tall
    block = lambda v: jnp.concatenate([v[:, :n], v[:rest, n:]], axis=0)
    mine, theirs = g[rest:, n:], gp[rest:, n:]
    upper = odd(0)
    cross = jnp.concatenate([jnp.where(upper, theirs, mine), jnp.where(upper, mine, theirs)], axis=0)
    flipped = cross.T
    return block(g), block(gp), jnp.where(upper, flipped, cross), jnp.where(upper, cross, flipped)


def put_rows(w, stacked, o_ref):
    for i in range(o_ref.shape[0]):
        o_ref[i] = jnp.dot(w, stacked(i), preferred_element_type=jnp.float32).astype(jnp.bfloat16)


def put_result(w, stacked, o_hbm, buffer, sems):
    rows = buffer.shape[0]
    parts = sems.shape[0]
    size = -(-rows // parts)
    copies = []
    for p in range(parts):
        lo, hi = p * size, min(rows, p * size + size)
        for i in range(lo, hi):
            buffer[i] = jnp.dot(w, stacked(i), preferred_element_type=jnp.float32).astype(jnp.bfloat16)
        at = pl.ds(lo, hi - lo)
        copies.append(pltpu.make_async_copy(buffer.at[at], o_hbm.at[at], sems.at[p]))
        copies[-1].start()
    for copy in copies:
        copy.wait()


def result_call(body, rows, snaps, width):
    parts = 5
    return kernel_call(
        body,
        jax.ShapeDtypeStruct((rows, snaps, width), jnp.bfloat16),
        [VMEM((rows, snaps, width), jnp.bfloat16), pltpu.SemaphoreType.DMA((parts,))],
        out_spec=pl.BlockSpec(memory_space=pl.ANY),
    )


def put_modes(w, stacked, modes_ref, part_ref):
    rows, half = modes_ref.shape[0], part_ref.shape[0]
    put_rows(w, stacked, modes_ref)
    start = jnp.where(odd(0), rows - half, 0)
    for i in range(half):
        part_ref[i] = modes_ref[start + i]


def halves(rows, here_ref, there_ref):
    half = here_ref.shape[0]
    upper = odd(0)

    def row(i):
        if i < half:
            return jnp.where(upper, there_ref[i], here_ref[i])
        j = i - (rows - half)
        return jnp.where(upper, here_ref[j], there_ref[j])

    return row


def far_gram_body(own_ref, other_ref, far_ref, o_ref):
    n = own_ref.shape[1]
    acc = gram_sum(stack_of(own_ref, other_ref), lambda i: far_ref[i], own_ref.shape[0])
    packed = jnp.concatenate([acc[:n], acc[n:]], axis=1)
    for j in range(o_ref.shape[0]):
        o_ref[j] = packed


def square(a, b, c, d):
    return jnp.concatenate(
        [jnp.concatenate([a, b], axis=1), jnp.concatenate([c, d], axis=1)], axis=0
    )


def pair_levels_body(g_ref, gp_ref, wh_ref, c_ref):
    n = c_ref.shape[0]
    own, other, cross, flipped = pair_gram(g_ref[...], gp_ref[...], n)
    gram = square(own, cross, flipped, other)
    basis = diagonal_blocks(*top_rows([own, other]))
    merged = mmt(mm(basis, gram), basis)
    q = top_rows([merged], odd(0))[0]
    h = mmt(mm(q, merged), q)
    w = mm(q, basis)
    c_ref[...] = mmt(gram[:n], w)
    wh_ref[...] = jnp.concatenate(
        [w, jnp.concatenate([h, jnp.zeros((RANK, LANES - RANK), jnp.float32)], axis=1)], axis=0
    )


def quad_level(wh_ref, c_ref, far_wh_ref, cs_ref, twin_ref):
    n = c_ref.shape[0]
    cs, twin = cs_ref[...], twin_ref[...]
    between = square(cs[:, :n], twin[:, n:], cs[:, n:], twin[:, :n])
    wa, wb = wh_ref[:RANK, :], far_wh_ref[:RANK, :]
    on_b = mmt(between, wb)
    mixed = mm(wa, on_b)
    gram = square(wh_ref[RANK:, :RANK], mixed, mixed.T, far_wh_ref[RANK:, :RANK])
    return diagonal_blocks(wa, wb), gram, jnp.concatenate([c_ref[...], on_b[:n]], axis=1)


def quad_project_body(wh, c, far_wh, cs, twin, yo, yp, yy, yz, o_hbm, buffer, sems):
    w, gram, coef = quad_level(wh, c, far_wh, cs, twin)
    weights = projection(gram, coef, odd(1), w).astype(jnp.bfloat16)
    put_result(weights, stack_of(yo, yp, yy, yz), o_hbm, buffer, sems)


def quad_modes_body(wh, c, far_wh, cs, twin, yo, yp, yy, yz, modes_ref, part_ref, h_ref, c_ref):
    w, gram, coef = quad_level(wh, c, far_wh, cs, twin)
    q = top_rows([gram], odd(1))[0]
    h_ref[...] = mmt(mm(q, gram), q)
    c_ref[...] = mmt(coef, q)
    put_modes(mm(q, w).astype(jnp.bfloat16), stack_of(yo, yp, yy, yz), modes_ref, part_ref)


def cross_body(here_ref, there_ref, y_ref, own_ref, o_ref):
    rows = y_ref.shape[0]
    other = halves(rows, here_ref, there_ref)
    acc = gram_sum(other, lambda i: jnp.concatenate([y_ref[i], own_ref[i], other(i)], axis=0), rows)
    for j in range(o_ref.shape[0]):
        o_ref[j] = acc


def merged_gram(p_ref, h_ref, c_ref, n):
    total = p_ref[0]
    for j in range(1, p_ref.shape[0]):
        total = total + p_ref[j]
    mixed = total[:, n : n + RANK]
    gram = jnp.concatenate(
        [
            jnp.concatenate([h_ref[...], mixed.T], axis=1),
            jnp.concatenate([mixed, total[:, n + RANK :]], axis=1),
        ],
        axis=0,
    )
    coef = jnp.concatenate([c_ref[...], total[:, :n].T], axis=1)
    return gram, coef


def merge_body(level, p_ref, h_ref, c_ref, own_ref, here_ref, there_ref, modes_ref, part_ref, hn_ref, cn_ref):
    gram, coef = merged_gram(p_ref, h_ref, c_ref, c_ref.shape[0])
    w = top_rows([gram], odd(level))[0].astype(jnp.bfloat16)
    wf = w.astype(jnp.float32)
    cn_ref[...] = mmt(coef, wf)
    hn_ref[...] = mmt(mm(wf, gram), wf)
    other = halves(own_ref.shape[0], here_ref, there_ref)
    put_modes(w, lambda i: jnp.concatenate([own_ref[i], other(i)], axis=0), modes_ref, part_ref)


def project_body(level, p_ref, h_ref, c_ref, own_ref, here_ref, there_ref, o_hbm, buffer, sems):
    gram, coef = merged_gram(p_ref, h_ref, c_ref, c_ref.shape[0])
    weights = projection(gram, coef, odd(level)).astype(jnp.bfloat16)
    other = halves(own_ref.shape[0], here_ref, there_ref)
    stacked = lambda i: jnp.concatenate([own_ref[i], other(i)], axis=0)
    put_result(weights, stacked, o_hbm, buffer, sems)


def exchanged(block, level):
    count = lax.axis_size("tm")
    return lax.ppermute(block, "tm", [(i, i ^ 1 << level) for i in range(count)])


def gathered(parts):
    return lax.all_to_all(parts, ("lat", "lon"), 0, 0, tiled=True)


def shards(residuals, diffusivity):
    snaps, rows, width = residuals.shape
    tiles = lax.axis_size("lat") * lax.axis_size("lon")
    levels = lax.axis_size("tm").bit_length() - 1
    f32 = lambda *shape: jax.ShapeDtypeStruct(shape, jnp.float32)
    b16 = lambda *shape: jax.ShapeDtypeStruct(shape, jnp.bfloat16)
    x = jnp.transpose(residuals, (1, 0, 2))
    y = smooth(x, diffusivity, *halo_exchange(x, diffusivity))
    other, far = exchanged(y, 0), exchanged(y, 1)
    pair = kernel_call(pair_gram_body, f32(tiles, snaps * 3 // 4, 2 * snaps))(y, other)
    pair = jnp.sum(gathered(pair), axis=0)
    pair_twin = exchanged(pair, 0)
    far, pair_twin = lax.optimization_barrier((far, pair_twin))
    cross = kernel_call(far_gram_body, f32(tiles, snaps, 2 * snaps))(y, other, far)
    cross = jnp.sum(gathered(cross), axis=0)
    wh, c = kernel_call(
        pair_levels_body, (f32(2 * RANK, 2 * snaps), f32(snaps, RANK)), flops=1 << 32
    )(pair, pair_twin)
    operands = (wh, c, exchanged(wh, 1), cross, exchanged(cross, 0))
    operands += (y, other, far, exchanged(far, 0))
    if levels == 2:
        out = result_call(quad_project_body, rows, snaps, width)(*operands)
        return jnp.transpose(out, (1, 0, 2))
    block = (
        b16(rows, RANK, width),
        b16(-(-rows // 2), RANK, width),
        f32(RANK, RANK),
        f32(snaps, RANK),
    )
    modes, part, h, c = kernel_call(quad_modes_body, block)(*operands)
    for level in range(2, levels):
        here = exchanged(part, level)
        there = exchanged(here, 0)
        parts = gathered(kernel_call(cross_body, f32(tiles, RANK, snaps + 2 * RANK))(here, there, y, modes))
        if level < levels - 1:
            modes, part, h, c = kernel_call(functools.partial(merge_body, level), block)(
                parts, h, c, modes, here, there
            )
    out = result_call(functools.partial(project_body, levels - 1), rows, snaps, width)(
        parts, h, c, modes, here, there
    )
    return jnp.transpose(out, (1, 0, 2))


def solution(mesh):
    return jax.shard_map(
        shards,
        mesh=mesh,
        in_specs=(P("tm", "lat", "lon"), P("lat", "lon")),
        out_specs=P("tm", "lat", "lon"),
        check_vma=False,
    )
```
